32 devices in a mesh: gx: 4 (over z), gz: 4 (over y, x), gy: 2 (over core).
Axes of the slice: x: 2, y: 2, z: 4, core: 2. Of those that a mesh axis runs over, the one named last changes fastest.
Arguments:
- velocity: float32 [3, 128, 192, 512], P(None, ('gx', 'gy'), None, 'gz'), may hold values from -6 to 6
- metric_x: float32 [128], P(('gx', 'gy')), may hold values from 0.5 to 2
- metric_y: float32 [192], replicated, may hold values from 0.5 to 2
- metric_z: float32 [512], P('gz'), may hold values from 0.5 to 2
- x_inverse: float32 [128, 16], P(('gx', 'gy')), may hold values from -5 to 5, as said below
- y_inverse: float32 [192, 192], replicated, may hold values from -5 to 5, as said below
- z_inverse: float32 [512, 128], P('gz'), may hold values from -5 to 5, as said below
Outputs:
- gradient: float32 [3, 3, 128, 192, 512], P(None, None, ('gx', 'gy'), None, 'gz')
- convection: float32 [3, 128, 192, 512], P(None, ('gx', 'gy'), None, 'gz')
The draws below stay inside these ranges and needn't reach their ends.
Inputs may be any that keep to these rules, and one draw needn't show every extreme that they name: Rows b * 16 to b * 16 + 15 of x_inverse hold the inverse of a 16 x 16 tridiagonal matrix with unit diagonal whose row r has one value between 0.2 and 0.4 on both sides of the diagonal (where they exist), drawn afresh for each row and block. y_inverse holds the inverse of such a 192 x 192 matrix. Likewise for z_inverse with blocks of 128 rows.
All inputs are finite; a program needn't handle non-finite values.
Results may differ from the reference program's by a relative error of at most 0.0003.
Values sent between devices are 32-bit elements; how exact they have to be, the bound alone decides.
No kernel may reach another device: no remote copies, remote signals or barrier semaphores. Data moves between devices by JAX's collectives and lax.ppermute only.
A program may use at most 192 MiB of HBM per device.

```python
import math
import jax
import jax.numpy as jnp
from jax import lax

CX = 16
NY = 192
CZ = 128
NX = 128
NZ = 512


def block_inverse(key, blocks, length):
    alphas = jax.random.uniform(key, (blocks, length), jnp.float32, 0.2, 0.4)
    indices = jnp.arange(length)
    beside = (jnp.abs(indices[:, None] - indices[None, :]) == 1).astype(jnp.float32)
    matrix = jnp.eye(length, dtype=jnp.float32)[None] + alphas[:, :, None] * beside[None]
    return jnp.linalg.inv(matrix).reshape(blocks * length, length)


def draw_x_inverse(key, part):
    return block_inverse(jax.random.fold_in(key, 11), NX // CX, CX)


def draw_y_inverse(key, part):
    return block_inverse(jax.random.fold_in(key, 23), 1, NY)


def draw_z_inverse(key, part):
    return block_inverse(jax.random.fold_in(key, 37), NZ // CZ, CZ)


def block_levels(key, dims, pieces, low, high):
    factor_of, own = 1.0, jax.random.fold_in(key, 6)
    for dim, shards_of in pieces:
        steps = jnp.exp(jax.random.uniform(jax.random.fold_in(own, dim), (shards_of,), jnp.float32, low / len(pieces), high / len(pieces)))
        factor_of = factor_of * jnp.repeat(steps, dims[dim] // shards_of).reshape([-1 if axis == dim else 1 for axis in range(len(dims))])
    return factor_of


def scatter_about(rng, shape, width, limit, cuts=(), held_as=jnp.bfloat16):
    gain = block_levels(rng, shape, cuts, -0.22, 0.18) if cuts else 1.0
    values = jax.random.normal(rng, shape, jnp.float32) * width * gain
    return jnp.minimum(jnp.maximum(values, -limit), limit).astype(held_as)


def setup_inputs(seed: int = 0) -> dict:
    key_of = jax.random.split(jax.random.key(seed), 8)
    return {
        "velocity": scatter_about(key_of[0], (3, NX, NY, NZ), 1.0, 6.0, ((1, 8), (3, 4)), jnp.float32),
        "metric_x": jnp.clip(jnp.exp(math.log(2.0) - 1.3862944 * jax.random.uniform(key_of[1], (NX,), jnp.float32) ** block_levels(key_of[1], (NX,), ((0, 8),), -0.2, 0.2)), 0.5, 2.0),
        "metric_y": jnp.clip(jnp.exp(jax.random.uniform(key_of[2], (NY,), jnp.float32, math.log(0.5), math.log(2.0))), 0.5, 2.0),
        "metric_z": jnp.clip(jnp.exp(math.log(2.0) - 1.3862944 * jax.random.uniform(key_of[3], (NZ,), jnp.float32) ** block_levels(key_of[3], (NZ,), ((0, 4),), -0.2, 0.2)), 0.5, 2.0),
        "x_inverse": draw_x_inverse(jax.random.fold_in(key_of[7], 71), 0),
        "y_inverse": draw_y_inverse(jax.random.fold_in(key_of[7], 71), 0),
        "z_inverse": draw_z_inverse(jax.random.fold_in(key_of[7], 71), 0),
    }


COUPLING = 1.0 / 3.0
NEAR_WEIGHT = 7.0 / 9.0
FAR_WEIGHT = 1.0 / 36.0

def stencil(values, axis_of, periodic):
    length = values.shape[axis_of]
    if periodic:

        def shifted(offset):
            return jnp.roll(values, -offset, axis=axis_of)
    else:
        widths = [(0, 0)] * values.ndim
        widths[axis_of] = (2, 2)
        padded = jnp.pad(values, widths)

        def shifted(offset):
            return lax.slice_in_dim(padded, 2 + offset, 2 + offset + length, axis=axis_of)
    return NEAR_WEIGHT * (shifted(1) - shifted(-1)) + FAR_WEIGHT * (shifted(2) - shifted(-2))

def line_solve(source, inverse, axis_of, periodic):
    length = source.shape[axis_of]
    block_size = inverse.shape[1]
    blocks = length // block_size
    moved_source = jnp.moveaxis(source, axis_of, 0)
    rest_shape = moved_source.shape[1:]
    line_view = moved_source.reshape(blocks, block_size, -1)
    inverses = inverse.reshape(blocks, block_size, block_size)
    inside = jnp.einsum('pij,pjl->pil', inverses, line_view, precision=lax.Precision.HIGHEST)
    system = jnp.eye(2 * blocks, dtype=jnp.float32)
    for block_index in range(blocks):
        left_block = block_index - 1
        right_block = block_index + 1
        if periodic:
            left_block = left_block % blocks
            right_block = right_block % blocks
        if left_block >= 0:
            system = system.at[2 * block_index, 2 * left_block + 1].add(COUPLING * inverses[block_index, 0, 0])
            system = system.at[2 * block_index + 1, 2 * left_block + 1].add(COUPLING * inverses[block_index, block_size - 1, 0])
        if right_block < blocks:
            system = system.at[2 * block_index, 2 * right_block].add(COUPLING * inverses[block_index, 0, block_size - 1])
            system = system.at[2 * block_index + 1, 2 * right_block].add(COUPLING * inverses[block_index, block_size - 1, block_size - 1])
    end_values = jnp.stack([inside[:, 0], inside[:, block_size - 1]], axis=1).reshape(2 * blocks, -1)
    solved = jnp.linalg.solve(system, end_values).reshape(blocks, 2, -1)
    starts = solved[:, 0]
    finals = solved[:, 1]
    if periodic:
        left_final = jnp.roll(finals, 1, axis=0)
        right_start = jnp.roll(starts, -1, axis=0)
    else:
        zero_row = jnp.zeros_like(finals[:1])
        left_final = jnp.concatenate([zero_row, finals[:-1]], axis=0)
        right_start = jnp.concatenate([starts[1:], zero_row], axis=0)
    result = inside - COUPLING * inverses[:, :, 0:1] * left_final[:, None, :] - COUPLING * inverses[:, :, block_size - 1:] * right_start[:, None, :]
    return jnp.moveaxis(result.reshape((length,) + rest_shape), 0, axis_of)

def derivative(values, inverse, metric, axis_of, periodic):
    slope = line_solve(stencil(values, axis_of, periodic), inverse, axis_of, periodic)
    layout = [1] * values.ndim
    layout[axis_of] = metric.shape[0]
    return slope * metric.reshape(layout)

def reference(velocity, metric_x, metric_y, metric_z, x_inverse, y_inverse, z_inverse):
    settings = ((metric_x, x_inverse, True), (metric_y, y_inverse, False), (metric_z, z_inverse, True))
    convection = [jnp.zeros_like(velocity[0]) for component in range(3)]
    gradient_rows = []
    for direction in range(3):
        metric, inverse, periodic = settings[direction]
        per_component = []
        for component in range(3):
            per_component.append(derivative(velocity[component], inverse, metric, direction, periodic))
            product = velocity[component] * velocity[direction]
            convection[component] = convection[component] + derivative(product, inverse, metric, direction, periodic)
        gradient_rows.append(jnp.stack(per_component))
    gradient = jnp.stack(gradient_rows, axis=1)
    return (gradient, jnp.stack(convection))
```

```python
import functools

import jax
import jax.numpy as jnp
from jax import lax
from jax.experimental import pallas as pl
from jax.experimental.pallas import tpu as pltpu
from jax.sharding import PartitionSpec as P

COUPLING = 1.0 / 3.0
NEAR = 7.0 / 9.0
FAR = 1.0 / 36.0
F32 = jnp.float32
BF16 = jnp.bfloat16
SMEM = pltpu.SMEM
VMEM_LIMIT = 48 * 1024 * 1024


def split(values):
    high = values.astype(BF16)
    low = (values - high.astype(F32)).astype(BF16)
    return high, low


def dot(a, b):
    return lax.dot_general(a, b, (((1,), (0,)), ((), ())), preferred_element_type=F32)


def dot_nt(a, b):
    return lax.dot_general(a, b, (((1,), (1,)), ((), ())), preferred_element_type=F32)


def params():
    return pltpu.CompilerParams(vmem_limit_bytes=VMEM_LIMIT)


def six(velocity, direction):
    return list(velocity) + [velocity[i] * velocity[direction] for i in range(3)]


def times_stencil(inverse):
    rows, length = inverse.shape
    zeros = jnp.zeros((rows, 2), F32)
    wide = jnp.concatenate([zeros, inverse, zeros], axis=1)

    def column(offset):
        return wide[:, 2 + offset : 2 + offset + length]

    return NEAR * (column(-1) - column(1)) + FAR * (column(-2) - column(2))


class Ends:
    def __init__(self, n):
        self.first = lax.axis_index("gy") == 0
        self.n = n
        self.o = jnp.where(self.first, 0, n - 1)
        self.o1 = jnp.where(self.first, 1, n - 2)
        self.q = jnp.where(self.first, n - 1, 0)
        self.q1 = jnp.where(self.first, n - 2, 1)
        self.sign_o = jnp.where(self.first, -1.0, 1.0).astype(F32)
        self.sign_q = -self.sign_o


def row_times_stencil(x_ref, row, n):
    entries = [x_ref[row, k] for k in range(n)]

    def at(k):
        return entries[k] if 0 <= k < n else 0.0

    return [NEAR * (at(k - 1) - at(k + 1)) + FAR * (at(k - 2) - at(k + 2)) for k in range(n)]


def x_ends_kernel(n, x_ref, v_ref, halo_ref, w_ref, l_ref):
    ends = Ends(n)
    send = [-COUPLING * value for value in row_times_stencil(x_ref, ends.o, n)]
    send[0] = send[0] + jnp.where(ends.first, NEAR, 0.0)
    send[1] = send[1] + jnp.where(ends.first, FAR, 0.0)
    send[n - 1] = send[n - 1] - jnp.where(ends.first, 0.0, NEAR)
    send[n - 2] = send[n - 2] - jnp.where(ends.first, 0.0, FAR)
    last = row_times_stencil(x_ref, ends.q, n)

    def halo_pair(row):
        near = ends.sign_q * (NEAR * x_ref[row, ends.q] + FAR * x_ref[row, ends.q1])
        far = ends.sign_q * FAR * x_ref[row, ends.q]
        return jnp.where(ends.first, near, far), jnp.where(ends.first, far, near)

    send_halo = [-COUPLING * value for value in halo_pair(ends.o)]
    last_halo = halo_pair(ends.q)

    def tile(index, carry):
        rows = pl.ds(pl.multiple_of(index * 8, 8), 8)
        w = [None] * 6
        l = [None] * 6
        for k in range(n + 2):
            if k < n:
                fields = six([v_ref[i, k, rows, :] for i in range(3)], 0)
                a, b = send[k], last[k]
            else:
                fields = six([halo_ref[i, k - n, rows, :] for i in range(3)], 0)
                a, b = send_halo[k - n], last_halo[k - n]
            for f in range(6):
                w[f] = a * fields[f] if k == 0 else w[f] + a * fields[f]
                l[f] = b * fields[f] if k == 0 else l[f] + b * fields[f]
        for f in range(6):
            w_ref[f, rows, :] = w[f]
            l_ref[f, rows, :] = l[f]
        return carry

    lax.fori_loop(0, v_ref.shape[2] // 8, tile, 0)


def x_ends(x_inverse, velocity, halo, tile=64):
    _, n, ny, nz = velocity.shape
    layer = jax.ShapeDtypeStruct((6, ny, nz), F32)
    return pl.pallas_call(
        functools.partial(x_ends_kernel, n),
        grid=(ny // tile,),
        in_specs=[
            pl.BlockSpec(memory_space=SMEM),
            pl.BlockSpec((3, n, tile, nz), lambda i: (0, 0, i, 0)),
            pl.BlockSpec((3, 2, tile, nz), lambda i: (0, 0, i, 0)),
        ],
        out_specs=[pl.BlockSpec((6, tile, nz), lambda i: (0, i, 0))] * 2,
        out_shape=[layer, layer],
        compiler_params=params(),
        name="x_ends",
    )(x_inverse, velocity, halo)


def x_face_kernel(n, x_ref, p_ref, wr_ref, ws_ref, l_ref, own_ref, near_ref, w_ref, e_ref):
    ends = Ends(n)
    p_o = jnp.where(ends.first, n - 1, 0)
    p_o1 = jnp.where(ends.first, n - 2, 1)
    p_oo = p_ref[p_o, p_o]
    p_oo1 = p_ref[p_o, p_o1]
    x_oo = x_ref[ends.o, ends.o]
    x_oo1 = x_ref[ends.o, ends.o1]
    x_qo = x_ref[ends.q, ends.o]
    x_qo1 = x_ref[ends.q, ends.o1]
    inverse_den = 1.0 / jnp.full((8, wr_ref.shape[2]), 1.0 - COUPLING * COUPLING * p_oo * x_oo, F32)
    own_weight = COUPLING * FAR * ends.sign_o * p_oo1
    near_weight = COUPLING * FAR * ends.sign_o * COUPLING * p_oo * x_oo1
    end_weight = x_qo1 * ends.sign_o * FAR

    def tile(index, carry):
        rows = pl.ds(pl.multiple_of(index * 8, 8), 8)
        own = six([own_ref[i, rows, :] for i in range(3)], 0)
        near = six([near_ref[i, rows, :] for i in range(3)], 0)
        for f in range(6):
            w = wr_ref[f, rows, :] - (COUPLING * p_oo) * ws_ref[f, rows, :]
            w = (w + own_weight * own[f] + near_weight * near[f]) * inverse_den
            w_ref[f, rows, :] = w
            e_ref[f, rows, :] = l_ref[f, rows, :] + x_qo * w + end_weight * near[f]
        return carry

    lax.fori_loop(0, wr_ref.shape[1] // 8, tile, 0)


def x_face(x_inverse, x_outer, received, sent, partial, own, near):
    n = x_inverse.shape[0]
    layer = jax.ShapeDtypeStruct(received.shape, F32)
    return pl.pallas_call(
        functools.partial(x_face_kernel, n),
        in_specs=[pl.BlockSpec(memory_space=SMEM)] * 2 + [pl.BlockSpec(memory_space=pltpu.VMEM)] * 5,
        out_specs=[pl.BlockSpec(memory_space=pltpu.VMEM)] * 2,
        out_shape=[layer, layer],
        compiler_params=params(),
        name="x_face",
    )(x_inverse, x_outer, received, sent, partial, own, near)


def x_solve_kernel(
    n, x_ref, p_ref, m_ref, v_ref, near_ref, halo_ref, w_ref, e_ref, r_ref, part_ref, held_ref, g_ref, c_ref, coef_ref
):
    ends = Ends(n)

    @pl.when(pl.program_id(0) == 0)
    def _():
        ratios = [-x_ref[i, i + 1] / x_ref[i + 1, i + 1] for i in range(n - 1)]
        ratios.append(-x_ref[n - 1, n - 2] / x_ref[n - 2, n - 2] * x_ref[n - 1, n - 1])
        for i in range(n):
            if i == 0:
                pivot = 1.0
            elif i == n - 1:
                pivot = x_ref[n - 1, n - 1]
            else:
                pivot = 1.0 + ratios[i] * ratios[i - 1]
            coef_ref[0, i] = pivot * m_ref[i]
            coef_ref[1, i] = pivot * m_ref[i] * FAR
            if i > 0:
                coef_ref[2, i] = ratios[i] * m_ref[i] / m_ref[i - 1]
            if i < n - 1:
                coef_ref[3, i] = ratios[i] * m_ref[i] / m_ref[i + 1]
        p_q = jnp.where(ends.first, 0, n - 1)
        coef_ref[4, 0] = p_ref[p_q, p_q] * COUPLING
        coef_ref[4, 1] = -COUPLING / (1.0 - COUPLING * COUPLING * p_ref[p_q, p_q] * x_ref[ends.q, ends.q])

    near_first = jnp.where(ends.first, NEAR * ends.sign_q, FAR * ends.sign_q)
    near_second = jnp.where(ends.first, FAR * ends.sign_q, NEAR * ends.sign_q)
    far_first = jnp.where(ends.first, FAR * ends.sign_q, 0.0)
    far_second = jnp.where(ends.first, 0.0, FAR * ends.sign_q)

    def tile(index, carry):
        rows = pl.ds(pl.multiple_of(index * 8, 8), 8)
        near = six([near_ref[i, rows, :] for i in range(3)], 0)
        halo_a = six([halo_ref[i, 0, rows, :] for i in range(3)], 0)
        halo_b = six([halo_ref[i, 1, rows, :] for i in range(3)], 0)
        for f in range(6):
            if f < 3:
                line = [v_ref[f, k, rows, :] for k in range(n)]
            else:
                line = [v_ref[f - 3, k, rows, :] * v_ref[0, k, rows, :] for k in range(n)]
            outer_0 = w_ref[f, rows, :]
            outer_1 = (FAR * ends.sign_o) * near[f]
            inner_0 = r_ref[f, rows, :] - coef_ref[4, 0] * e_ref[f, rows, :]
            inner_0 = near_first * halo_a[f] + near_second * halo_b[f] + coef_ref[4, 1] * inner_0
            inner_1 = far_first * halo_a[f] + far_second * halo_b[f]
            added = {
                0: jnp.where(ends.first, outer_0, inner_0),
                1: jnp.where(ends.first, outer_1, inner_1),
                n - 1: jnp.where(ends.first, inner_0, outer_0),
                n - 2: jnp.where(ends.first, inner_1, outer_1),
            }
            zero = jnp.zeros_like(outer_0)

            def at(k):
                return line[k] if 0 <= k < n else zero

            steps = [at(k + 1) - at(k - 1) if 0 < k < n - 1 else None for k in range(n)]
            forward = []
            for k in range(n):
                if k == 0:
                    source = 28.0 * line[1] + line[2]
                elif k == 1:
                    source = 28.0 * (line[2] - line[0]) + line[3]
                elif k == n - 1:
                    source = -28.0 * line[n - 2] - line[n - 3]
                elif k == n - 2:
                    source = 28.0 * (line[n - 1] - line[n - 3]) - line[n - 4]
                else:
                    source = 28.0 * (line[k + 1] - line[k - 1]) + (line[k + 2] - line[k - 2])
                value = coef_ref[1, k] * source
                if k in added:
                    value = value + coef_ref[0, k] * added[k]
                if k > 0:
                    value = value - coef_ref[2, k] * forward[k - 1]
                forward.append(value)
            solved = None
            for k in reversed(range(n)):
                solved = forward[k] if k == n - 1 else forward[k] - coef_ref[3, k] * solved
                if f < 3:
                    g_ref[f, 0, k, rows, :] = solved
                else:
                    c_ref[f - 3, k, rows, :] = solved + part_ref[f - 3, k, rows, :]
        return carry

    lax.fori_loop(0, v_ref.shape[2] // 8, tile, 0)


def x_solve(x_inverse, x_inner, metric, velocity, near, halo, outer, ends, received, partial, gradient, tile=32):
    _, n, ny, nz = velocity.shape
    field = pl.BlockSpec((3, n, tile, nz), lambda i: (0, 0, i, 0))
    layer = pl.BlockSpec((6, tile, nz), lambda i: (0, i, 0))
    return pl.pallas_call(
        functools.partial(x_solve_kernel, n),
        grid=(ny // tile,),
        in_specs=[
            pl.BlockSpec(memory_space=SMEM),
            pl.BlockSpec(memory_space=SMEM),
            pl.BlockSpec(memory_space=SMEM),
            field,
            pl.BlockSpec((3, tile, nz), lambda i: (0, i, 0)),
            pl.BlockSpec((3, 2, tile, nz), lambda i: (0, 0, i, 0)),
            layer,
            layer,
            layer,
            field,
            pl.BlockSpec(memory_space=pl.ANY),
        ],
        out_specs=[pl.BlockSpec((3, 1, n, tile, nz), lambda i: (0, 0, 0, i, 0)), field],
        out_shape=[
            jax.ShapeDtypeStruct(gradient.shape, F32),
            jax.ShapeDtypeStruct(partial.shape, F32),
        ],
        scratch_shapes=[pltpu.SMEM((5, n), F32)],
        input_output_aliases={10: 0, 9: 1},
        compiler_params=params(),
        name="x_solve",
    )(x_inverse, x_inner, metric, velocity, near, halo, outer, ends, received, partial, gradient)


def y_kernel(planes, inv_ref, m_ref, v_ref, g_ref, c_ref, high_ref, low_ref):
    ny = inv_ref.shape[0]

    @pl.when(pl.program_id(0) == 0)
    def _():
        row = lax.broadcasted_iota(jnp.int32, (ny, ny), 0)
        column = lax.broadcasted_iota(jnp.int32, (ny, ny), 1)
        metric = jnp.sum(jnp.where(row == column, m_ref[...], 0.0), axis=1, keepdims=True)
        high, low = split(times_stencil(inv_ref[...]) * metric)
        high_ref[...] = high
        low_ref[...] = low

    for p in range(planes):
        fields = jnp.concatenate(six([v_ref[i, p] for i in range(3)], 1), axis=1)
        high, low = split(fields)
        result = dot(high_ref[...], high) + dot(low_ref[...], high) + dot(high_ref[...], low)
        nz = v_ref.shape[3]
        for i in range(3):
            g_ref[i, 0, p] = result[:, i * nz : (i + 1) * nz]
            c_ref[i, p] = result[:, (3 + i) * nz : (4 + i) * nz]


def y_solve(y_inverse, metric, velocity, planes=2):
    _, n, ny, nz = velocity.shape
    return pl.pallas_call(
        functools.partial(y_kernel, planes),
        grid=(n // planes,),
        in_specs=[
            pl.BlockSpec((ny, ny), lambda i: (0, 0)),
            pl.BlockSpec((1, ny), lambda i: (0, 0)),
            pl.BlockSpec((3, planes, ny, nz), lambda i: (0, i, 0, 0)),
        ],
        out_specs=[
            pl.BlockSpec((3, 1, planes, ny, nz), lambda i: (0, 1, i, 0, 0)),
            pl.BlockSpec((3, planes, ny, nz), lambda i: (0, i, 0, 0)),
        ],
        out_shape=[
            jax.ShapeDtypeStruct((3, 3, n, ny, nz), F32),
            jax.ShapeDtypeStruct((3, n, ny, nz), F32),
        ],
        scratch_shapes=[pltpu.VMEM((ny, ny), BF16), pltpu.VMEM((ny, ny), BF16)],
        compiler_params=params(),
        name="y_solve",
    )(y_inverse, metric.reshape(1, ny), velocity)


def z_ends_kernel(planes, inv_ref, v_ref, left_ref, right_ref, e_ref, weight_ref):
    nz = inv_ref.shape[0]

    @pl.when(pl.program_id(0) == 0)
    def _():
        index = lax.broadcasted_iota(jnp.int32, (8, nz), 0)
        column = lax.broadcasted_iota(jnp.int32, (8, nz), 1)
        wanted = jnp.where(index < 2, index, nz - 4 + index)
        pick = jnp.where((wanted == column) & (index < 4), 1.0, 0.0)
        ends = times_stencil(jnp.concatenate([inv_ref[0:8], inv_ref[nz - 8 : nz]], axis=0))
        first = jnp.broadcast_to(ends[0:1], (8, nz))
        last = jnp.broadcast_to(ends[15:16], (8, nz))
        rows = jnp.where(index == 4, first, jnp.where(index == 5, last, pick))
        high, low = split(rows)
        weight_ref[...] = jnp.concatenate([high, low], axis=0)

    for p in range(planes):
        for f, field in enumerate(six([v_ref[i, p] for i in range(3)], 2)):
            high, low = split(field)
            a = dot_nt(weight_ref[...], high)
            b = dot_nt(weight_ref[...], low)
            values = a[0:8] + a[8:16] + b[0:8]
            if f < 3:
                left_ref[p, 2 * f : 2 * f + 2] = values[0:2]
                right_ref[p, 2 * f : 2 * f + 2] = values[2:4]
            e_ref[p, f : f + 1] = values[4:5]
            e_ref[p, 8 + f : 9 + f] = values[5:6]


def z_ends(z_inverse, velocity, planes=4):
    _, n, ny, nz = velocity.shape
    return pl.pallas_call(
        functools.partial(z_ends_kernel, planes),
        grid=(n // planes,),
        in_specs=[
            pl.BlockSpec((nz, nz), lambda i: (0, 0)),
            pl.BlockSpec((3, planes, ny, nz), lambda i: (0, i, 0, 0)),
        ],
        out_specs=[
            pl.BlockSpec((planes, 6, ny), lambda i: (i, 0, 0)),
            pl.BlockSpec((planes, 6, ny), lambda i: (i, 0, 0)),
            pl.BlockSpec((planes, 16, ny), lambda i: (i, 0, 0)),
        ],
        out_shape=[
            jax.ShapeDtypeStruct((n, 6, ny), F32),
            jax.ShapeDtypeStruct((n, 6, ny), F32),
            jax.ShapeDtypeStruct((n, 16, ny), F32),
        ],
        scratch_shapes=[pltpu.VMEM((16, nz), BF16)],
        compiler_params=params(),
        name="z_ends",
    )(z_inverse, velocity)


def z_added(left, right):
    left_far = six([left[2 * i : 2 * i + 1] for i in range(3)], 2)
    left_near = six([left[2 * i + 1 : 2 * i + 2] for i in range(3)], 2)
    right_near = six([right[2 * i : 2 * i + 1] for i in range(3)], 2)
    right_far = six([right[2 * i + 1 : 2 * i + 2] for i in range(3)], 2)
    pad = [jnp.zeros_like(left[0:2])]
    left_far, left_near, right_near, right_far = (
        jnp.concatenate(rows + pad, axis=0) for rows in (left_far, left_near, right_near, right_far)
    )
    return (
        -NEAR * left_near - FAR * left_far,
        -FAR * left_near,
        NEAR * right_near + FAR * right_far,
        FAR * right_near,
    )


def z_face_kernel(inv_ref, left_ref, right_ref, e_ref, first_ref, last_ref):
    nz = inv_ref.shape[0]
    ny = left_ref.shape[2]

    def entry(i, j):
        return inv_ref[i : i + 1, j : j + 1]

    row = lax.broadcasted_iota(jnp.int32, (8, ny), 0)
    for p in range(left_ref.shape[0]):
        a_left, b_left, a_right, b_right = z_added(left_ref[p], right_ref[p])
        for end, ref in ((0, first_ref), (nz - 1, last_ref)):
            own = e_ref[p, 0:8] if end == 0 else e_ref[p, 8:16]
            value = (
                own
                + entry(end, 0) * a_left
                + entry(end, 1) * b_left
                + entry(end, nz - 1) * a_right
                + entry(end, nz - 2) * b_right
            )
            ref[p] = jnp.where(row < 6, value, entry(end, end))


def z_face(z_inverse, left, right, ends):
    n, _, ny = left.shape
    block = jax.ShapeDtypeStruct((n, 8, ny), F32)
    return pl.pallas_call(
        z_face_kernel,
        in_specs=[pl.BlockSpec(memory_space=pltpu.VMEM)] * 4,
        out_specs=[pl.BlockSpec(memory_space=pltpu.VMEM)] * 2,
        out_shape=[block, block],
        compiler_params=params(),
        name="z_face",
    )(z_inverse, left, right, ends)


def z_kernel(
    planes, inv_ref, m_ref, v_ref, left_ref, right_ref, first_ref, last_ref, left_end_ref, right_end_ref,
    part_ref, held_ref, g_ref, c_ref, main_ref, side_ref,
):
    nz = inv_ref.shape[0]

    @pl.when(pl.program_id(0) == 0)
    def _():
        turned = times_stencil(inv_ref[...]).T * m_ref[...]
        high, low = split(turned)
        both = jnp.concatenate([high, low], axis=1)
        main_ref[...] = jnp.concatenate([both, both], axis=0)
        columns = inv_ref[...].T * m_ref[...]
        index = lax.broadcasted_iota(jnp.int32, (32, nz), 0)
        kind = index // 8
        picked = jnp.where(
            kind == 0,
            columns[0:1],
            jnp.where(kind == 1, columns[1:2], jnp.where(kind == 2, columns[nz - 1 : nz], columns[nz - 2 : nz - 1])),
        )
        wide = jnp.concatenate([jnp.where(index % 8 == f, picked, 0.0) for f in range(6)], axis=1)
        high, low = split(wide)
        side_ref[...] = jnp.concatenate([high, high, low], axis=0)

    ny = v_ref.shape[2]
    for p in range(planes):
        a_left, b_left, a_right, b_right = z_added(left_ref[p], right_ref[p])
        own_first = first_ref[p]
        own_last = last_ref[p]
        left_end = left_end_ref[p]
        right_end = right_end_ref[p]
        left_tail = left_end[6:7]
        right_head = right_end[6:7]
        left_final = (left_end - COUPLING * left_tail * own_first) / (
            1.0 - COUPLING * COUPLING * left_tail * own_first[6:7]
        )
        right_start = (right_end - COUPLING * right_head * own_last) / (
            1.0 - COUPLING * COUPLING * right_head * own_last[6:7]
        )
        side = jnp.concatenate(
            [a_left - COUPLING * left_final, b_left, a_right - COUPLING * right_start, b_right], axis=0
        )
        side_high, side_low = split(side.T)
        added = dot(jnp.concatenate([side_high, side_low, side_high], axis=1), side_ref[...])
        for f, field in enumerate(six([v_ref[i, p] for i in range(3)], 2)):
            high, low = split(field)
            both = dot(jnp.concatenate([high, low], axis=1), main_ref[...])
            value = both[:, :nz] + both[:, nz:] + added[:, f * nz : (f + 1) * nz]
            if f < 3:
                g_ref[f, 0, p] = value
            else:
                c_ref[f - 3, p] = value + part_ref[f - 3, p]


def z_solve(z_inverse, metric, velocity, left, right, first, last, left_end, right_end, partial, gradient, planes=2):
    _, n, ny, nz = velocity.shape
    field = pl.BlockSpec((3, planes, ny, nz), lambda i: (0, i, 0, 0))
    halo = pl.BlockSpec((planes, 6, ny), lambda i: (i, 0, 0))
    end = pl.BlockSpec((planes, 8, ny), lambda i: (i, 0, 0))
    return pl.pallas_call(
        functools.partial(z_kernel, planes),
        grid=(n // planes,),
        in_specs=[
            pl.BlockSpec((nz, nz), lambda i: (0, 0)),
            pl.BlockSpec((1, nz), lambda i: (0, 0)),
            field,
            halo,
            halo,
            end,
            end,
            end,
            end,
            field,
            pl.BlockSpec(memory_space=pl.ANY),
        ],
        out_specs=[pl.BlockSpec((3, 1, planes, ny, nz), lambda i: (0, 2, i, 0, 0)), field],
        out_shape=[
            jax.ShapeDtypeStruct(gradient.shape, F32),
            jax.ShapeDtypeStruct(partial.shape, F32),
        ],
        scratch_shapes=[pltpu.VMEM((2 * nz, 2 * nz), BF16), pltpu.VMEM((96, 6 * nz), BF16)],
        input_output_aliases={10: 0, 9: 1},
        compiler_params=params(),
        name="z_solve",
    )(z_inverse, metric.reshape(1, nz), velocity, left, right, first, last, left_end, right_end, partial, gradient)


def on_device(mesh, velocity, metric_x, metric_y, metric_z, x_inverse, y_inverse, z_inverse):
    n = velocity.shape[1]
    blocks = mesh.shape["gx"] * 2
    across = [(i, (i + 1) % blocks) for i in range(1, blocks, 2)]
    across = across + [(j, i) for i, j in across]
    beside = [(0, 1), (1, 0)]
    count = mesh.shape["gz"]
    rightward = [(i, (i + 1) % count) for i in range(count)]
    leftward = [((i + 1) % count, i) for i in range(count)]
    core = lax.axis_index("gy")

    own = lax.dynamic_slice_in_dim(velocity, core * (n - 1), 1, axis=1)[:, 0]
    near = lax.ppermute(own, ("gx", "gy"), across)
    x_outer = lax.ppermute(x_inverse, ("gx", "gy"), across)
    halo = lax.ppermute(lax.dynamic_slice_in_dim(velocity, (1 - core) * (n - 2), 2, axis=1), "gy", beside)
    x_inner = lax.ppermute(x_inverse, "gy", beside)

    left_send, right_send, z_own = z_ends(z_inverse, velocity)
    z_left = lax.ppermute(right_send, "gz", rightward)
    z_right = lax.ppermute(left_send, "gz", leftward)

    x_sent, x_partial = x_ends(x_inverse, velocity, halo)
    x_received = lax.ppermute(x_sent, ("gx", "gy"), across)

    gradient, convection = y_solve(y_inverse, metric_y, velocity)

    z_first, z_last = z_face(z_inverse, z_left, z_right, z_own)
    z_left_end = lax.ppermute(z_last, "gz", rightward)
    z_right_end = lax.ppermute(z_first, "gz", leftward)
    gradient, convection = z_solve(
        z_inverse, metric_z, velocity, z_left, z_right, z_first, z_last, z_left_end, z_right_end, convection, gradient
    )

    outer, x_own_end = x_face(x_inverse, x_outer, x_received, x_sent, x_partial, own, near)
    x_end = lax.ppermute(x_own_end, "gy", beside)
    gradient, convection = x_solve(
        x_inverse, x_inner, metric_x, velocity, near, halo, outer, x_own_end, x_end, convection, gradient
    )
    return (gradient, convection)


def solution(mesh):
    return jax.shard_map(
        functools.partial(on_device, mesh),
        mesh=mesh,
        in_specs=(
            P(None, ("gx", "gy"), None, "gz"),
            P(("gx", "gy")),
            P(),
            P("gz"),
            P(("gx", "gy"), None),
            P(),
            P("gz", None),
        ),
        out_specs=(P(None, None, ("gx", "gy"), None, "gz"), P(None, ("gx", "gy"), None, "gz")),
        check_vma=False,
    )
```

```python
import functools

import jax
import jax.numpy as jnp
from jax import lax
from jax.experimental import pallas as pl
from jax.experimental.pallas import tpu as pltpu
from jax.sharding import PartitionSpec as P

COUPLING = 1.0 / 3.0
NEAR = 7.0 / 9.0
FAR = 1.0 / 36.0
F32 = jnp.float32
BF16 = jnp.bfloat16
SMEM = pltpu.SMEM
VMEM_LIMIT = 20 * 1024 * 1024
GROUP = 4


def split(values):
    high = values.astype(BF16)
    low = (values - high.astype(F32)).astype(BF16)
    return high, low


def dot(a, b):
    return lax.dot_general(a, b, (((1,), (0,)), ((), ())), preferred_element_type=F32)


def dot_nt(a, b):
    return lax.dot_general(a, b, (((1,), (1,)), ((), ())), preferred_element_type=F32)


def params():
    return pltpu.CompilerParams(vmem_limit_bytes=VMEM_LIMIT)


def six(velocity, direction):
    return list(velocity) + [velocity[i] * velocity[direction] for i in range(3)]


def times_stencil(inverse):
    rows, length = inverse.shape
    zeros = jnp.zeros((rows, 2), F32)
    wide = jnp.concatenate([zeros, inverse, zeros], axis=1)

    def column(offset):
        return wide[:, 2 + offset : 2 + offset + length]

    return NEAR * (column(-1) - column(1)) + FAR * (column(-2) - column(2))


def in_vmem(*shape):
    return pltpu.VMEM(shape, F32)


ANY = pl.BlockSpec(memory_space=pl.ANY)
WHOLE = pl.BlockSpec(memory_space=pltpu.VMEM)
SCALARS = pl.BlockSpec(memory_space=SMEM)


def cost(array, passes):
    return pl.CostEstimate(flops=passes, bytes_accessed=passes, transcendentals=0)


def layer_shape(*shape):
    return jax.ShapeDtypeStruct(shape, F32)


class Ends:
    def __init__(self, n):
        self.first = lax.axis_index("gy") == 0
        self.n = n
        self.o = jnp.where(self.first, 0, n - 1)
        self.o1 = jnp.where(self.first, 1, n - 2)
        self.q = jnp.where(self.first, n - 1, 0)
        self.q1 = jnp.where(self.first, n - 2, 1)
        self.sign_o = jnp.where(self.first, -1.0, 1.0).astype(F32)
        self.sign_q = -self.sign_o


class Table:
    def __init__(self, n):
        self.source, self.forward, self.backward = 0, n, 2 * n
        self.send, self.last = 3 * n, 4 * n + 2
        self.oo, self.oo1, self.qo, self.qo1, self.qq = range(5 * n + 4, 5 * n + 9)
        self.size = 5 * n + 9


def prepare_kernel(
    n, ny, xi_ref, mx_ref, yi_ref, my_ref, zi_ref, mz_ref, v_ref,
    own_ref, halo_ref, table_ref, y_ref, y_metric_ref, z_ref, z_metric_ref, x_ref, m_ref, sem,
):
    ends = Ends(n)
    nz = v_ref.shape[3]
    small = [pltpu.make_async_copy(xi_ref, x_ref, sem.at[9]), pltpu.make_async_copy(mx_ref, m_ref, sem.at[10])]
    copies = []
    for i in range(3):
        copies.append(pltpu.make_async_copy(v_ref.at[i, ends.o], own_ref.at[pl.ds(i * ny, ny)], sem.at[3 * i]))
        for j in range(2):
            plane = jnp.where(ends.first, n - 2 + j, j)
            copies.append(
                pltpu.make_async_copy(
                    v_ref.at[i, plane], halo_ref.at[pl.ds((2 * i + j) * ny, ny)], sem.at[3 * i + 1 + j]
                )
            )
    copies.append(pltpu.make_async_copy(zi_ref, z_ref, sem.at[11]))
    copies.append(pltpu.make_async_copy(mz_ref, z_metric_ref, sem.at[12]))
    copies.append(pltpu.make_async_copy(yi_ref, y_ref, sem.at[13]))
    copies.append(pltpu.make_async_copy(my_ref, y_metric_ref, sem.at[14]))
    for copy in small + copies:
        copy.start()
    for copy in small:
        copy.wait()

    wide = jnp.concatenate([x_ref[...], jnp.zeros((n, nz - n), F32)], axis=1)
    own_ref[3 * ny : 3 * ny + n, :] = wide
    halo_ref[6 * ny : 6 * ny + n, :] = wide

    table = Table(n)
    first = ends.first

    def spread(value):
        return jnp.broadcast_to(value, (8, nz))

    def entry(i, j):
        return spread(x_ref[i : i + 1, j : j + 1])

    metric = [spread(m_ref[0:1, k : k + 1]) for k in range(n)]
    above = [entry(i, i + 1) for i in range(n - 1)]
    diagonal = [entry(i, i) for i in range(n)]
    ratio = [-above[i] / diagonal[i + 1] for i in range(n - 1)]
    ratio.append(-entry(n - 1, n - 2) / diagonal[n - 2] * diagonal[n - 1])
    for k in range(n):
        if k == 0:
            source = metric[k]
        elif k == n - 1:
            source = diagonal[k] * metric[k]
        else:
            source = (1.0 + ratio[k] * ratio[k - 1]) * metric[k]
        table_ref[table.source + k] = FAR * source
        table_ref[table.forward + k] = ratio[k] * metric[k] / metric[k - 1] if k > 0 else metric[k]
        table_ref[table.backward + k] = ratio[k] * metric[k] / metric[k + 1] if k < n - 1 else metric[k]

    top = [entry(0, k) for k in range(n)]
    bottom = [entry(n - 1, k) for k in range(n)]
    outer = [jnp.where(first, top[k], bottom[k]) for k in range(n)]
    inner = [jnp.where(first, bottom[k], top[k]) for k in range(n)]
    sign_o, sign_q = ends.sign_o, ends.sign_q
    for base, row, factor in ((table.send, outer, -COUPLING), (table.last, inner, 1.0)):

        def at(k):
            return row[k] if 0 <= k < n else jnp.zeros_like(row[0])

        for k in range(n):
            value = factor * (NEAR * (at(k - 1) - at(k + 1)) + FAR * (at(k - 2) - at(k + 2)))
            if base == table.send:
                if k == 0:
                    value = value + jnp.where(first, NEAR, 0.0)
                elif k == 1:
                    value = value + jnp.where(first, FAR, 0.0)
                elif k == n - 2:
                    value = value - jnp.where(first, 0.0, FAR)
                elif k == n - 1:
                    value = value - jnp.where(first, 0.0, NEAR)
            table_ref[base + k] = value
        at_q = jnp.where(first, row[n - 1], row[0])
        at_q1 = jnp.where(first, row[n - 2], row[1])
        near = factor * sign_q * (NEAR * at_q + FAR * at_q1)
        far = factor * sign_q * FAR * at_q
        table_ref[base + n] = jnp.where(first, near, far)
        table_ref[base + n + 1] = jnp.where(first, far, near)
    table_ref[table.oo] = jnp.where(first, outer[0], outer[n - 1])
    table_ref[table.oo1] = jnp.where(first, outer[1], outer[n - 2])
    table_ref[table.qo] = jnp.where(first, inner[0], inner[n - 1])
    table_ref[table.qo1] = jnp.where(first, inner[1], inner[n - 2])
    table_ref[table.qq] = jnp.where(first, inner[n - 1], inner[0])
    for copy in copies:
        copy.wait()


def prepare(x_inverse, metric_x, y_inverse, metric_y, z_inverse, metric_z, velocity):
    _, n, ny, nz = velocity.shape
    inputs = (x_inverse, metric_x, y_inverse, metric_y, z_inverse, metric_z, velocity)
    return pl.pallas_call(
        functools.partial(prepare_kernel, n, ny),
        in_specs=[ANY] * 7,
        out_specs=[WHOLE] * 7,
        out_shape=[
            layer_shape(3 * ny + n, nz),
            layer_shape(6 * ny + n, nz),
            in_vmem(Table(n).size, 8, nz),
            in_vmem(ny, ny),
            in_vmem(1, ny),
            in_vmem(nz, nz),
            in_vmem(1, nz),
        ],
        scratch_shapes=[pltpu.VMEM((n, n), F32), pltpu.VMEM((1, n), F32), pltpu.SemaphoreType.DMA((15,))],
        compiler_params=params(),
        name="prepare",
    )(*(pltpu.with_memory_space_constraint(value, pltpu.HBM) for value in inputs))


def x_ends_kernel(n, ny, table_ref, v_ref, halo_ref, w_ref, l_ref):
    table = Table(n)

    def tile(index, carry):
        start = pl.multiple_of(index * 8, 8)
        rows = pl.ds(start, 8)
        w = [None] * 6
        l = [None] * 6
        for k in range(n + 2):
            if k < n:
                fields = six([v_ref[i, k, rows, :] for i in range(3)], 0)
            else:
                fields = six([halo_ref[pl.ds((2 * i + k - n) * ny + start, 8), :] for i in range(3)], 0)
            a, b = table_ref[table.send + k], table_ref[table.last + k]
            for f in range(6):
                w[f] = a * fields[f] if k == 0 else w[f] + a * fields[f]
                l[f] = b * fields[f] if k == 0 else l[f] + b * fields[f]
        for f in range(6):
            w_ref[f, rows, :] = w[f]
            l_ref[f, rows, :] = l[f]
        return carry

    lax.fori_loop(0, ny // 8, tile, 0)


def x_ends(table, velocity, halo):
    _, n, ny, nz = velocity.shape
    return pl.pallas_call(
        functools.partial(x_ends_kernel, n, ny),
        in_specs=[WHOLE] * 3,
        out_specs=[WHOLE, WHOLE],
        out_shape=[layer_shape(6, ny, nz), layer_shape(6, ny, nz)],
        compiler_params=params(),
        cost_estimate=cost(velocity, 3),
        name="x_ends",
    )(table, velocity, halo)


def x_face_kernel(n, ny, table_ref, wr_ref, ws_ref, l_ref, own_ref, near_ref, after_ref, w_ref, e_ref):
    ends = Ends(n)
    table = Table(n)
    shape = (8, wr_ref.shape[2])

    def corner(i, j):
        row = 3 * ny + i
        return jnp.broadcast_to(near_ref[row : row + 1, j : j + 1], shape)

    p_oo = jnp.where(ends.first, corner(n - 1, n - 1), corner(0, 0))
    p_oo1 = jnp.where(ends.first, corner(n - 1, n - 2), corner(0, 1))
    x_qo = table_ref[table.qo]
    inverse_den = 1.0 / (1.0 - COUPLING * COUPLING * table_ref[table.oo] * p_oo)
    sent_weight = COUPLING * p_oo
    own_weight = COUPLING * FAR * ends.sign_o * p_oo1
    near_weight = COUPLING * FAR * ends.sign_o * COUPLING * table_ref[table.oo1] * p_oo
    end_weight = ends.sign_o * FAR * table_ref[table.qo1]

    def tile(index, carry):
        start = pl.multiple_of(index * 8, 8)
        rows = pl.ds(start, 8)
        own = six([own_ref[pl.ds(i * ny + start, 8), :] for i in range(3)], 0)
        near = six([near_ref[pl.ds(i * ny + start, 8), :] for i in range(3)], 0)
        for f in range(6):
            w = wr_ref[f, rows, :] - sent_weight * ws_ref[f, rows, :]
            w = (w + own_weight * own[f] + near_weight * near[f]) * inverse_den
            w_ref[f, rows, :] = 36.0 * w
            e_ref[f, rows, :] = l_ref[f, rows, :] + x_qo * w + end_weight * near[f]
        return carry

    lax.fori_loop(0, ny // 8, tile, 0)


def x_face(table, received, sent, partial, own, near, after, n):
    _, ny, _ = received.shape
    layer = layer_shape(*received.shape)
    return pl.pallas_call(
        functools.partial(x_face_kernel, n, ny),
        in_specs=[WHOLE] * 6 + [ANY],
        out_specs=[WHOLE, WHOLE],
        out_shape=[layer, layer],
        compiler_params=params(),
        cost_estimate=cost(received, 1),
        name="x_face",
    )(table, received, sent, partial, own, near, after)


def x_solve_kernel(
    n, ny, table_ref, v_ref, near_ref, halo_ref, w_ref, e_ref, r_ref, part_ref, held_ref, gradient_ref, convection_ref,
    g_ref, c_ref, sem,
):
    ends = Ends(n)
    table = Table(n)
    nz = v_ref.shape[3]
    parts = sem.shape[1]
    share = ny // parts

    def corner(i):
        row = 6 * ny + i
        return jnp.broadcast_to(halo_ref[row : row + 1, i : i + 1], (8, nz))

    p_qq = jnp.where(ends.first, corner(0), corner(n - 1))
    weight = COUPLING * p_qq
    scale = -36.0 * COUPLING / (1.0 - COUPLING * COUPLING * table_ref[table.qq] * p_qq)
    near_first = jnp.where(ends.first, 28.0 * ends.sign_q, ends.sign_q)
    near_second = jnp.where(ends.first, ends.sign_q, 28.0 * ends.sign_q)
    far_first = jnp.where(ends.first, ends.sign_q, 0.0)
    far_second = jnp.where(ends.first, 0.0, ends.sign_q)

    def tile(index, carry):
        start = pl.multiple_of(index * 8, 8)
        rows = pl.ds(start, 8)
        near = six([near_ref[pl.ds(i * ny + start, 8), :] for i in range(3)], 0)
        halo_a = six([halo_ref[pl.ds(2 * i * ny + start, 8), :] for i in range(3)], 0)
        halo_b = six([halo_ref[pl.ds((2 * i + 1) * ny + start, 8), :] for i in range(3)], 0)
        for f in range(6):
            if f < 3:
                line = [v_ref[f, k, rows, :] for k in range(n)]
            else:
                line = [v_ref[f - 3, k, rows, :] * v_ref[0, k, rows, :] for k in range(n)]
            outer_0 = w_ref[f, rows, :]
            outer_1 = ends.sign_o * near[f]
            inner_0 = near_first * halo_a[f] + near_second * halo_b[f]
            inner_0 = inner_0 + scale * (r_ref[f, rows, :] - weight * e_ref[f, rows, :])
            inner_1 = far_first * halo_a[f] + far_second * halo_b[f]
            added = {
                0: jnp.where(ends.first, outer_0, inner_0),
                1: jnp.where(ends.first, outer_1, inner_1),
                n - 1: jnp.where(ends.first, inner_0, outer_0),
                n - 2: jnp.where(ends.first, inner_1, outer_1),
            }
            forward = []
            for k in range(n):
                if k == 0:
                    source = 28.0 * line[1] + line[2]
                elif k == 1:
                    source = 28.0 * (line[2] - line[0]) + line[3]
                elif k == n - 1:
                    source = -28.0 * line[n - 2] - line[n - 3]
                elif k == n - 2:
                    source = 28.0 * (line[n - 1] - line[n - 3]) - line[n - 4]
                else:
                    source = 28.0 * (line[k + 1] - line[k - 1]) + (line[k + 2] - line[k - 2])
                if k in added:
                    source = source + added[k]
                value = table_ref[table.source + k] * source
                if k > 0:
                    value = value - table_ref[table.forward + k] * forward[k - 1]
                forward.append(value)
            solved = None
            for k in reversed(range(n)):
                solved = forward[k] if k == n - 1 else forward[k] - table_ref[table.backward + k] * solved
                if f < 3:
                    g_ref[f, k, rows, :] = solved
                else:
                    c_ref[f - 3, k, rows, :] = solved + part_ref[f - 3, k, rows, :]
        return carry

    def copies(part):
        rows = pl.ds(pl.multiple_of(part * share, 8), share)
        return (
            pltpu.make_async_copy(g_ref.at[:, :, rows], gradient_ref.at[:, 0, :, rows], sem.at[0, part]),
            pltpu.make_async_copy(c_ref.at[:, :, rows], convection_ref.at[:, :, rows], sem.at[1, part]),
        )

    def step(part, carry):
        lax.fori_loop(part * (share // 8), (part + 1) * (share // 8), tile, 0)
        for copy in copies(part):
            copy.start()
        return carry

    lax.fori_loop(0, parts, step, 0)

    def drain(part, carry):
        for copy in copies(part):
            copy.wait()
        return carry

    lax.fori_loop(0, parts, drain, 0)


def x_solve(table, velocity, near, halo, outer, ends, received, partial, gradient, parts=6):
    _, n, ny, nz = velocity.shape
    return pl.pallas_call(
        functools.partial(x_solve_kernel, n, ny),
        in_specs=[WHOLE] * 8 + [ANY],
        out_specs=[ANY, ANY],
        out_shape=[layer_shape(*gradient.shape), layer_shape(3, n, ny, nz)],
        scratch_shapes=[
            pltpu.VMEM((3, n, ny, nz), F32),
            pltpu.VMEM((3, n, ny, nz), F32),
            pltpu.SemaphoreType.DMA((2, parts)),
        ],
        input_output_aliases={8: 0},
        compiler_params=params(),
        cost_estimate=cost(velocity, 5),
        name="x_solve",
    )(table, velocity, near, halo, outer, ends, received, partial, gradient)


def y_kernel(n, inv_ref, m_ref, v_ref, part_ref, after_ref, gradient_ref, c_ref, high_ref, low_ref, out_ref, sem):
    ny = inv_ref.shape[0]
    nz = v_ref.shape[3]
    row = lax.broadcasted_iota(jnp.int32, (ny, ny), 0)
    column = lax.broadcasted_iota(jnp.int32, (ny, ny), 1)
    metric = jnp.sum(jnp.where(row == column, m_ref[...], 0.0), axis=1, keepdims=True)
    high, low = split(times_stencil(inv_ref[...]) * metric)
    high_ref[...] = high
    low_ref[...] = low

    def copy(group):
        planes = pl.ds(group * GROUP, GROUP)
        return pltpu.make_async_copy(out_ref.at[:, planes], gradient_ref.at[:, 1, planes], sem.at[group])

    def step(group, carry):
        for u in range(GROUP):
            p = group * GROUP + u
            fields = six([v_ref[i, p] for i in range(3)], 1)
            for a in (0, 2, 4):
                high, low = split(jnp.concatenate(fields[a : a + 2], axis=1))
                result = dot(high_ref[...], high) + dot(low_ref[...], high) + dot(high_ref[...], low)
                for j in range(2):
                    f = a + j
                    value = result[:, j * nz : (j + 1) * nz]
                    if f < 3:
                        out_ref[f, p] = value
                    else:
                        c_ref[f - 3, p] = value + part_ref[f - 3, p]
        copy(group).start()
        return carry

    lax.fori_loop(0, n // GROUP, step, 0)

    def drain(group, carry):
        copy(group).wait()
        return carry

    lax.fori_loop(0, n // GROUP, drain, 0)


def y_solve(y_inverse, metric, velocity, partial, after):
    _, n, ny, nz = velocity.shape
    return pl.pallas_call(
        functools.partial(y_kernel, n),
        in_specs=[WHOLE] * 4 + [ANY],
        out_specs=[ANY, WHOLE],
        out_shape=[layer_shape(3, 3, n, ny, nz), in_vmem(3, n, ny, nz)],
        scratch_shapes=[
            pltpu.VMEM((ny, ny), BF16),
            pltpu.VMEM((ny, ny), BF16),
            pltpu.VMEM((3, n, ny, nz), F32),
            pltpu.SemaphoreType.DMA((n // GROUP,)),
        ],
        input_output_aliases={3: 1},
        compiler_params=params(),
        cost_estimate=cost(velocity, 4),
        name="y_solve",
    )(y_inverse, metric, velocity, partial, after)


LINES = 128


def z_own_kernel(
    n, inv_ref, m_ref, v_ref, after_ref, g_ref, c_ref, right_ref, left_ref, right_2_ref, left_2_ref, main_ref
):
    nz = inv_ref.shape[0]
    ny = v_ref.shape[2]
    high, low = split(times_stencil(inv_ref[...]).T * m_ref[...])
    both = jnp.concatenate([high, low], axis=1)
    main_ref[...] = jnp.concatenate([both, both], axis=0)
    first_scale = 1.0 / m_ref[0:1, 0:1]
    last_scale = 1.0 / m_ref[0:1, nz - 1 : nz]
    lane = lax.broadcasted_iota(jnp.int32, (ny, nz), 1)

    def corner(i, j):
        return jnp.broadcast_to(inv_ref[i : i + 1, j : j + 1], (1, LINES))

    m = nz - 1
    corners_right = [corner(m, m), corner(m, m - 1), corner(m, 0), corner(m, 1)]
    corners_left = [corner(0, 0), corner(0, 1), corner(0, m), corner(0, m - 1)]

    def step(group, carry):
        gathered = []
        for u in range(GROUP):
            p = group * GROUP + u
            velocities = [v_ref[i, p] for i in range(3)]
            columns = jnp.zeros((ny, nz), F32)
            for f, field in enumerate(six(velocities, 2)):
                high, low = split(field)
                both = dot(jnp.concatenate([high, low], axis=1), main_ref[...])
                value = both[:, :nz] + both[:, nz:]
                if f < 3:
                    g_ref[f, p] = value
                else:
                    c_ref[f - 3, p] = value
                columns = jnp.where(lane // 2 == f, pltpu.roll(value, 1 + 2 * f, axis=1), columns)
            for i in range(3):
                columns = jnp.where(lane // 4 == 3 + i, pltpu.roll(velocities[i], 14 + 4 * i, axis=1), columns)
            gathered.append(columns)
        lines = jnp.concatenate(gathered, axis=0)
        for j in range(GROUP * ny // LINES):
            turned = lines[j * LINES : (j + 1) * LINES].T

            def row(index):
                return turned[index : index + 1]

            def block(ends, scale, column, corners):
                rows = [row(ends + 2 * f) * scale for f in range(6)] + corners[0:2]
                rows = rows + [row(12 + 4 * i + column) for i in range(3)] + corners[2:3]
                rows = rows + [row(13 + 4 * i + column) for i in range(3)] + corners[3:4]
                return jnp.concatenate(rows, axis=0)

            index = group * (GROUP * ny // LINES) + j
            to_right = block(0, last_scale, 0, corners_right)
            to_left = block(1, first_scale, 2, corners_left)
            right_ref[index] = to_right
            left_ref[index] = to_left
            right_2_ref[index] = to_right[8:16]
            left_2_ref[index] = to_left[8:16]
        return carry

    lax.fori_loop(0, n // GROUP, step, 0)


def z_own(z_inverse, metric, velocity, after):
    _, n, ny, nz = velocity.shape
    return pl.pallas_call(
        functools.partial(z_own_kernel, n),
        in_specs=[WHOLE, WHOLE, WHOLE, ANY],
        out_specs=[WHOLE] * 6,
        out_shape=[in_vmem(3, n, ny, nz)] * 2
        + [layer_shape(n * ny // LINES, 16, LINES)] * 2
        + [layer_shape(n * ny // LINES, 8, LINES)] * 2,
        scratch_shapes=[pltpu.VMEM((2 * nz, 2 * nz), BF16)],
        compiler_params=params(),
        cost_estimate=cost(velocity, 3),
        name="z_own",
    )(z_inverse, metric, velocity, after)


def z_side(own_right, own_left, left, right, left_2, right_2):
    index = lax.broadcasted_iota(jnp.int32, (8, LINES), 0)

    def row(values, i):
        return jnp.broadcast_to(values[i : i + 1], (8, LINES))

    def fields(velocities):
        products = velocities * row(velocities, 2)
        return jnp.where(index < 3, velocities, pltpu.roll(products, 3, axis=0))

    def pair(velocities):
        return fields(velocities), fields(pltpu.roll(velocities, 4, axis=0))

    def from_left(velocities):
        far, near = pair(velocities)
        return -NEAR * near - FAR * far, -FAR * near

    def from_right(velocities):
        near, far = pair(velocities)
        return NEAR * near + FAR * far, FAR * near

    def first_value(values, at_left, at_right):
        return (
            values[0:8]
            + row(values, 6) * at_left[0]
            + row(values, 7) * at_left[1]
            + row(values, 11) * at_right[0]
            + row(values, 15) * at_right[1]
        )

    def last_value(values, at_left, at_right):
        return (
            values[0:8]
            + row(values, 11) * at_left[0]
            + row(values, 15) * at_left[1]
            + row(values, 6) * at_right[0]
            + row(values, 7) * at_right[1]
        )

    at_left, at_right = from_left(left[8:16]), from_right(right[8:16])
    own_first = first_value(own_left, at_left, at_right)
    own_last = last_value(own_right, at_left, at_right)
    left_value = last_value(left, from_left(left_2), from_right(own_left[8:16]))
    right_value = first_value(right, from_left(own_right[8:16]), from_right(right_2))
    left_tail, right_head = row(left, 6), row(right, 6)
    left_final = (left_value - COUPLING * left_tail * own_first) / (
        1.0 - COUPLING * COUPLING * left_tail * row(own_left, 6)
    )
    right_start = (right_value - COUPLING * right_head * own_last) / (
        1.0 - COUPLING * COUPLING * right_head * row(own_right, 6)
    )
    return jnp.concatenate(
        [at_left[0] - COUPLING * left_final, at_left[1], at_right[0] - COUPLING * right_start, at_right[1]], axis=0
    )


def z_join_kernel(
    n, inv_ref, m_ref, g_ref, part_ref, own_right_ref, own_left_ref, left_ref, right_ref, left_2_ref, right_2_ref, held_ref,
    gradient_ref, c_ref, side_ref, out_ref, sem,
):
    nz = inv_ref.shape[0]
    ny = g_ref.shape[2]
    columns = inv_ref[...].T * m_ref[...]
    index = lax.broadcasted_iota(jnp.int32, (32, nz), 0)
    kind = index // 8
    picked = jnp.where(
        kind == 0,
        columns[0:1],
        jnp.where(kind == 1, columns[1:2], jnp.where(kind == 2, columns[nz - 1 : nz], columns[nz - 2 : nz - 1])),
    )
    wide = jnp.concatenate([jnp.where(index % 8 == f, picked, 0.0) for f in range(6)], axis=1)
    high, low = split(wide)
    side_ref[...] = jnp.concatenate([high, high, low], axis=0)
    blocks = GROUP * ny // LINES

    def copy(group):
        planes = pl.ds(group * GROUP, GROUP)
        return pltpu.make_async_copy(out_ref.at[:, planes], gradient_ref.at[:, 2, planes], sem.at[group])

    def step(group, carry):
        sides = []
        for j in range(blocks):
            lines = (own_right_ref, own_left_ref, left_ref, right_ref, left_2_ref, right_2_ref)
            high, low = split(z_side(*(ref[group * blocks + j] for ref in lines)).T)
            sides.append(jnp.concatenate([high, low, high], axis=1))
        for pair in range(GROUP // 2):
            half = blocks // (GROUP // 2)
            lines = jnp.concatenate(sides[pair * half : (pair + 1) * half], axis=0)
            for f in range(0, 6, 2):
                added = dot(lines, side_ref[:, f * nz : (f + 2) * nz])
                for u in range(2):
                    p = group * GROUP + 2 * pair + u
                    for j in range(2):
                        value = added[u * ny : (u + 1) * ny, j * nz : (j + 1) * nz]
                        if f + j < 3:
                            out_ref[f + j, p] = value + g_ref[f + j, p]
                        else:
                            c_ref[f + j - 3, p] = value + part_ref[f + j - 3, p]
        copy(group).start()
        return carry

    lax.fori_loop(0, n // GROUP, step, 0)

    def drain(group, carry):
        copy(group).wait()
        return carry

    lax.fori_loop(0, n // GROUP, drain, 0)


def z_join(z_inverse, metric, own, partial, lines, gradient):
    _, n, ny, nz = own.shape
    return pl.pallas_call(
        functools.partial(z_join_kernel, n),
        in_specs=[WHOLE] * 10 + [ANY],
        out_specs=[ANY, WHOLE],
        out_shape=[layer_shape(*gradient.shape), in_vmem(3, n, ny, nz)],
        scratch_shapes=[
            pltpu.VMEM((96, 6 * nz), BF16),
            pltpu.VMEM((3, n, ny, nz), F32),
            pltpu.SemaphoreType.DMA((n // GROUP,)),
        ],
        input_output_aliases={10: 0, 3: 1},
        compiler_params=params(),
        cost_estimate=cost(own, 3),
        name="z_join",
    )(z_inverse, metric, own, partial, *lines, gradient)


def on_device(mesh, velocity, metric_x, metric_y, metric_z, x_inverse, y_inverse, z_inverse):
    n = velocity.shape[1]
    blocks = mesh.shape["gx"] * 2
    across = [(i, (i + 1) % blocks) for i in range(1, blocks, 2)]
    across = across + [(j, i) for i, j in across]
    beside = [(0, 1), (1, 0)]
    count = mesh.shape["gz"]

    def shift(by):
        return [(i, (i + by) % count) for i in range(count)]

    own, inner, table, y_inverse, metric_y, z_inverse, metric_z = prepare(
        x_inverse, metric_x[None], y_inverse, metric_y[None], z_inverse, metric_z[None], velocity
    )
    near = lax.ppermute(own, ("gx", "gy"), across)
    halo = lax.ppermute(inner, "gy", beside)
    held = pltpu.with_memory_space_constraint(velocity, pltpu.VMEM)

    x_sent, x_partial = x_ends(table, held, halo)
    x_received = lax.ppermute(x_sent, ("gx", "gy"), across)

    z_gradient, convection, to_right, to_left, to_right_2, to_left_2 = z_own(z_inverse, metric_z, held, x_sent)
    z_lines = (
        to_right,
        to_left,
        lax.ppermute(to_right, "gz", shift(1)),
        lax.ppermute(to_left, "gz", shift(-1)),
        lax.ppermute(to_right_2, "gz", shift(2)),
        lax.ppermute(to_left_2, "gz", shift(-2)),
    )

    gradient, convection = y_solve(y_inverse, metric_y, held, convection, to_right)
    gradient, convection = z_join(z_inverse, metric_z, z_gradient, convection, z_lines, gradient)

    outer, x_end = x_face(table, x_received, x_sent, x_partial, own, near, convection, n)
    x_other = lax.ppermute(x_end, "gy", beside)
    return tuple(x_solve(table, held, near, halo, outer, x_end, x_other, convection, gradient))


def solution(mesh):
    return jax.shard_map(
        functools.partial(on_device, mesh),
        mesh=mesh,
        in_specs=(
            P(None, ("gx", "gy"), None, "gz"),
            P(("gx", "gy")),
            P(),
            P("gz"),
            P(("gx", "gy"), None),
            P(),
            P("gz", None),
        ),
        out_specs=(P(None, None, ("gx", "gy"), None, "gz"), P(None, ("gx", "gy"), None, "gz")),
        check_vma=False,
    )
```

```python
import functools

import jax
import jax.numpy as jnp
from jax import lax
from jax.experimental import pallas as pl
from jax.experimental.pallas import tpu as pltpu
from jax.sharding import PartitionSpec as P

COUPLING = 1.0 / 3.0
NEAR = 7.0 / 9.0
FAR = 1.0 / 36.0
F32 = jnp.float32
BF16 = jnp.bfloat16
SMEM = pltpu.SMEM
VMEM_LIMIT = 20 * 1024 * 1024
GROUP = 4
Y_COST = 20_000_000_000
Z_COST = 20_000_000_000


def split(values):
    high = values.astype(BF16)
    low = (values - high.astype(F32)).astype(BF16)
    return high, low


def dot(a, b):
    return lax.dot_general(a, b, (((1,), (0,)), ((), ())), preferred_element_type=F32)


def dot_nt(a, b):
    return lax.dot_general(a, b, (((1,), (1,)), ((), ())), preferred_element_type=F32)


def params():
    return pltpu.CompilerParams(vmem_limit_bytes=VMEM_LIMIT)


def six(velocity, direction):
    return list(velocity) + [velocity[i] * velocity[direction] for i in range(3)]


def times_stencil(inverse):
    rows, length = inverse.shape
    zeros = jnp.zeros((rows, 2), F32)
    wide = jnp.concatenate([zeros, inverse, zeros], axis=1)

    def column(offset):
        return wide[:, 2 + offset : 2 + offset + length]

    return NEAR * (column(-1) - column(1)) + FAR * (column(-2) - column(2))


def in_vmem(*shape):
    return pltpu.VMEM(shape, F32)


ANY = pl.BlockSpec(memory_space=pl.ANY)
WHOLE = pl.BlockSpec(memory_space=pltpu.VMEM)
SCALARS = pl.BlockSpec(memory_space=SMEM)


def cost(array, passes):
    return pl.CostEstimate(flops=passes, bytes_accessed=passes, transcendentals=0)


def layer_shape(*shape):
    return jax.ShapeDtypeStruct(shape, F32)


class Ends:
    def __init__(self, n):
        self.first = lax.axis_index("gy") == 0
        self.n = n
        self.o = jnp.where(self.first, 0, n - 1)
        self.o1 = jnp.where(self.first, 1, n - 2)
        self.q = jnp.where(self.first, n - 1, 0)
        self.q1 = jnp.where(self.first, n - 2, 1)
        self.sign_o = jnp.where(self.first, -1.0, 1.0).astype(F32)
        self.sign_q = -self.sign_o


class Table:
    def __init__(self, n):
        self.source, self.forward, self.backward = 0, n, 2 * n
        self.send, self.last = 3 * n, 4 * n + 2
        self.oo, self.oo1, self.qo, self.qo1, self.qq = range(5 * n + 4, 5 * n + 9)
        self.size = 5 * n + 9


def prepare_kernel(
    n, ny, xi_ref, mx_ref, yi_ref, my_ref, zi_ref, mz_ref, v_ref,
    own_ref, halo_ref, table_ref, y_ref, y_metric_ref, z_ref, z_metric_ref, x_ref, m_ref, sem,
):
    ends = Ends(n)
    nz = v_ref.shape[3]
    small = [pltpu.make_async_copy(xi_ref, x_ref, sem.at[9]), pltpu.make_async_copy(mx_ref, m_ref, sem.at[10])]
    copies = []
    for i in range(3):
        copies.append(pltpu.make_async_copy(v_ref.at[i, ends.o], own_ref.at[pl.ds(i * ny, ny)], sem.at[3 * i]))
        for j in range(2):
            plane = jnp.where(ends.first, n - 2 + j, j)
            copies.append(
                pltpu.make_async_copy(
                    v_ref.at[i, plane], halo_ref.at[pl.ds((2 * i + j) * ny, ny)], sem.at[3 * i + 1 + j]
                )
            )
    copies.append(pltpu.make_async_copy(zi_ref, z_ref, sem.at[11]))
    copies.append(pltpu.make_async_copy(mz_ref, z_metric_ref, sem.at[12]))
    copies.append(pltpu.make_async_copy(yi_ref, y_ref, sem.at[13]))
    copies.append(pltpu.make_async_copy(my_ref, y_metric_ref, sem.at[14]))
    for copy in small + copies:
        copy.start()
    for copy in small:
        copy.wait()

    wide = jnp.concatenate([x_ref[...], jnp.zeros((n, nz - n), F32)], axis=1)
    own_ref[3 * ny : 3 * ny + n, :] = wide
    halo_ref[6 * ny : 6 * ny + n, :] = wide

    table = Table(n)
    first = ends.first

    def spread(value):
        return jnp.broadcast_to(value, (8, nz))

    def entry(i, j):
        return spread(x_ref[i : i + 1, j : j + 1])

    metric = [spread(m_ref[0:1, k : k + 1]) for k in range(n)]
    above = [entry(i, i + 1) for i in range(n - 1)]
    diagonal = [entry(i, i) for i in range(n)]
    ratio = [-above[i] / diagonal[i + 1] for i in range(n - 1)]
    ratio.append(-entry(n - 1, n - 2) / diagonal[n - 2] * diagonal[n - 1])
    for k in range(n):
        if k == 0:
            source = metric[k]
        elif k == n - 1:
            source = diagonal[k] * metric[k]
        else:
            source = (1.0 + ratio[k] * ratio[k - 1]) * metric[k]
        table_ref[table.source + k] = FAR * source
        table_ref[table.forward + k] = ratio[k] * metric[k] / metric[k - 1] if k > 0 else metric[k]
        table_ref[table.backward + k] = ratio[k] * metric[k] / metric[k + 1] if k < n - 1 else metric[k]

    top = [entry(0, k) for k in range(n)]
    bottom = [entry(n - 1, k) for k in range(n)]
    outer = [jnp.where(first, top[k], bottom[k]) for k in range(n)]
    inner = [jnp.where(first, bottom[k], top[k]) for k in range(n)]
    sign_o, sign_q = ends.sign_o, ends.sign_q
    for base, row, factor in ((table.send, outer, -COUPLING), (table.last, inner, 1.0)):

        def at(k):
            return row[k] if 0 <= k < n else jnp.zeros_like(row[0])

        for k in range(n):
            value = factor * (NEAR * (at(k - 1) - at(k + 1)) + FAR * (at(k - 2) - at(k + 2)))
            if base == table.send:
                if k == 0:
                    value = value + jnp.where(first, NEAR, 0.0)
                elif k == 1:
                    value = value + jnp.where(first, FAR, 0.0)
                elif k == n - 2:
                    value = value - jnp.where(first, 0.0, FAR)
                elif k == n - 1:
                    value = value - jnp.where(first, 0.0, NEAR)
            table_ref[base + k] = value
        at_q = jnp.where(first, row[n - 1], row[0])
        at_q1 = jnp.where(first, row[n - 2], row[1])
        near = factor * sign_q * (NEAR * at_q + FAR * at_q1)
        far = factor * sign_q * FAR * at_q
        table_ref[base + n] = jnp.where(first, near, far)
        table_ref[base + n + 1] = jnp.where(first, far, near)
    table_ref[table.oo] = jnp.where(first, outer[0], outer[n - 1])
    table_ref[table.oo1] = jnp.where(first, outer[1], outer[n - 2])
    table_ref[table.qo] = jnp.where(first, inner[0], inner[n - 1])
    table_ref[table.qo1] = jnp.where(first, inner[1], inner[n - 2])
    table_ref[table.qq] = jnp.where(first, inner[n - 1], inner[0])
    for copy in copies:
        copy.wait()


def prepare(x_inverse, metric_x, y_inverse, metric_y, z_inverse, metric_z, velocity):
    _, n, ny, nz = velocity.shape
    inputs = (x_inverse, metric_x, y_inverse, metric_y, z_inverse, metric_z, velocity)
    return pl.pallas_call(
        functools.partial(prepare_kernel, n, ny),
        in_specs=[ANY] * 7,
        out_specs=[WHOLE] * 7,
        out_shape=[
            layer_shape(3 * ny + n, nz),
            layer_shape(6 * ny + n, nz),
            in_vmem(Table(n).size, 8, nz),
            in_vmem(ny, ny),
            in_vmem(1, ny),
            in_vmem(nz, nz),
            in_vmem(1, nz),
        ],
        scratch_shapes=[pltpu.VMEM((n, n), F32), pltpu.VMEM((1, n), F32), pltpu.SemaphoreType.DMA((15,))],
        compiler_params=params(),
        name="prepare",
    )(*(pltpu.with_memory_space_constraint(value, pltpu.HBM) for value in inputs))


def x_ends_kernel(n, ny, table_ref, v_ref, halo_ref, w_ref, l_ref):
    table = Table(n)

    def tile(index, carry):
        start = pl.multiple_of(index * 8, 8)
        rows = pl.ds(start, 8)
        w = [None] * 6
        l = [None] * 6
        for k in range(n + 2):
            if k < n:
                fields = six([v_ref[i, k, rows, :] for i in range(3)], 0)
            else:
                fields = six([halo_ref[pl.ds((2 * i + k - n) * ny + start, 8), :] for i in range(3)], 0)
            a, b = table_ref[table.send + k], table_ref[table.last + k]
            for f in range(6):
                w[f] = a * fields[f] if k == 0 else w[f] + a * fields[f]
                l[f] = b * fields[f] if k == 0 else l[f] + b * fields[f]
        for f in range(6):
            w_ref[f, rows, :] = w[f]
            l_ref[f, rows, :] = l[f]
        return carry

    lax.fori_loop(0, ny // 8, tile, 0)


def x_ends(table, velocity, halo):
    _, n, ny, nz = velocity.shape
    return pl.pallas_call(
        functools.partial(x_ends_kernel, n, ny),
        in_specs=[WHOLE] * 3,
        out_specs=[WHOLE, WHOLE],
        out_shape=[layer_shape(6, ny, nz), layer_shape(6, ny, nz)],
        compiler_params=params(),
        cost_estimate=cost(velocity, 3),
        name="x_ends",
    )(table, velocity, halo)


def x_face_kernel(n, ny, table_ref, wr_ref, ws_ref, l_ref, own_ref, near_ref, after_ref, w_ref, e_ref):
    ends = Ends(n)
    table = Table(n)
    shape = (8, wr_ref.shape[2])

    def corner(i, j):
        row = 3 * ny + i
        return jnp.broadcast_to(near_ref[row : row + 1, j : j + 1], shape)

    p_oo = jnp.where(ends.first, corner(n - 1, n - 1), corner(0, 0))
    p_oo1 = jnp.where(ends.first, corner(n - 1, n - 2), corner(0, 1))
    x_qo = table_ref[table.qo]
    inverse_den = 1.0 / (1.0 - COUPLING * COUPLING * table_ref[table.oo] * p_oo)
    sent_weight = COUPLING * p_oo
    own_weight = COUPLING * FAR * ends.sign_o * p_oo1
    near_weight = COUPLING * FAR * ends.sign_o * COUPLING * table_ref[table.oo1] * p_oo
    end_weight = ends.sign_o * FAR * table_ref[table.qo1]

    def tile(index, carry):
        start = pl.multiple_of(index * 8, 8)
        rows = pl.ds(start, 8)
        own = six([own_ref[pl.ds(i * ny + start, 8), :] for i in range(3)], 0)
        near = six([near_ref[pl.ds(i * ny + start, 8), :] for i in range(3)], 0)
        for f in range(6):
            w = wr_ref[f, rows, :] - sent_weight * ws_ref[f, rows, :]
            w = (w + own_weight * own[f] + near_weight * near[f]) * inverse_den
            w_ref[f, rows, :] = 36.0 * w
            e_ref[f, rows, :] = l_ref[f, rows, :] + x_qo * w + end_weight * near[f]
        return carry

    lax.fori_loop(0, ny // 8, tile, 0)


def x_face(table, received, sent, partial, own, near, after, n):
    _, ny, _ = received.shape
    layer = layer_shape(*received.shape)
    return pl.pallas_call(
        functools.partial(x_face_kernel, n, ny),
        in_specs=[WHOLE] * 6 + [ANY],
        out_specs=[WHOLE, WHOLE],
        out_shape=[layer, layer],
        compiler_params=params(),
        cost_estimate=cost(received, 1),
        name="x_face",
    )(table, received, sent, partial, own, near, after)


def x_solve_kernel(
    n, ny, table_ref, v_ref, near_ref, halo_ref, w_ref, e_ref, r_ref, part_ref, held_ref, gradient_ref, convection_ref,
    g_ref, c_ref, sem,
):
    ends = Ends(n)
    table = Table(n)
    nz = v_ref.shape[3]
    parts = sem.shape[1]
    share = ny // parts

    def corner(i):
        row = 6 * ny + i
        return jnp.broadcast_to(halo_ref[row : row + 1, i : i + 1], (8, nz))

    p_qq = jnp.where(ends.first, corner(0), corner(n - 1))
    weight = COUPLING * p_qq
    scale = -36.0 * COUPLING / (1.0 - COUPLING * COUPLING * table_ref[table.qq] * p_qq)
    near_first = jnp.where(ends.first, 28.0 * ends.sign_q, ends.sign_q)
    near_second = jnp.where(ends.first, ends.sign_q, 28.0 * ends.sign_q)
    far_first = jnp.where(ends.first, ends.sign_q, 0.0)
    far_second = jnp.where(ends.first, 0.0, ends.sign_q)

    def tile(index, carry):
        start = pl.multiple_of(index * 8, 8)
        rows = pl.ds(start, 8)
        near = six([near_ref[pl.ds(i * ny + start, 8), :] for i in range(3)], 0)
        halo_a = six([halo_ref[pl.ds(2 * i * ny + start, 8), :] for i in range(3)], 0)
        halo_b = six([halo_ref[pl.ds((2 * i + 1) * ny + start, 8), :] for i in range(3)], 0)
        for f in range(6):
            if f < 3:
                line = [v_ref[f, k, rows, :] for k in range(n)]
            else:
                line = [v_ref[f - 3, k, rows, :] * v_ref[0, k, rows, :] for k in range(n)]
            outer_0 = w_ref[f, rows, :]
            outer_1 = ends.sign_o * near[f]
            inner_0 = near_first * halo_a[f] + near_second * halo_b[f]
            inner_0 = inner_0 + scale * (r_ref[f, rows, :] - weight * e_ref[f, rows, :])
            inner_1 = far_first * halo_a[f] + far_second * halo_b[f]
            added = {
                0: jnp.where(ends.first, outer_0, inner_0),
                1: jnp.where(ends.first, outer_1, inner_1),
                n - 1: jnp.where(ends.first, inner_0, outer_0),
                n - 2: jnp.where(ends.first, inner_1, outer_1),
            }
            forward = []
            for k in range(n):
                if k == 0:
                    source = 28.0 * line[1] + line[2]
                elif k == 1:
                    source = 28.0 * (line[2] - line[0]) + line[3]
                elif k == n - 1:
                    source = -28.0 * line[n - 2] - line[n - 3]
                elif k == n - 2:
                    source = 28.0 * (line[n - 1] - line[n - 3]) - line[n - 4]
                else:
                    source = 28.0 * (line[k + 1] - line[k - 1]) + (line[k + 2] - line[k - 2])
                if k in added:
                    source = source + added[k]
                value = table_ref[table.source + k] * source
                if k > 0:
                    value = value - table_ref[table.forward + k] * forward[k - 1]
                forward.append(value)
            solved = None
            for k in reversed(range(n)):
                solved = forward[k] if k == n - 1 else forward[k] - table_ref[table.backward + k] * solved
                if f < 3:
                    g_ref[f, k, rows, :] = solved
                else:
                    c_ref[f - 3, k, rows, :] = solved + part_ref[f - 3, k, rows, :]
        return carry

    def copies(part):
        rows = pl.ds(pl.multiple_of(part * share, 8), share)
        return (
            pltpu.make_async_copy(g_ref.at[:, :, rows], gradient_ref.at[:, 0, :, rows], sem.at[0, part]),
            pltpu.make_async_copy(c_ref.at[:, :, rows], convection_ref.at[:, :, rows], sem.at[1, part]),
        )

    def step(part, carry):
        lax.fori_loop(part * (share // 8), (part + 1) * (share // 8), tile, 0)
        for copy in copies(part):
            copy.start()
        return carry

    lax.fori_loop(0, parts, step, 0)

    def drain(part, carry):
        for copy in copies(part):
            copy.wait()
        return carry

    lax.fori_loop(0, parts, drain, 0)


def x_solve(table, velocity, near, halo, outer, ends, received, partial, gradient, parts=6):
    _, n, ny, nz = velocity.shape
    return pl.pallas_call(
        functools.partial(x_solve_kernel, n, ny),
        in_specs=[WHOLE] * 8 + [ANY],
        out_specs=[ANY, ANY],
        out_shape=[layer_shape(*gradient.shape), layer_shape(3, n, ny, nz)],
        scratch_shapes=[
            pltpu.VMEM((3, n, ny, nz), F32),
            pltpu.VMEM((3, n, ny, nz), F32),
            pltpu.SemaphoreType.DMA((2, parts)),
        ],
        input_output_aliases={8: 0},
        compiler_params=params(),
        cost_estimate=cost(velocity, 5),
        name="x_solve",
    )(table, velocity, near, halo, outer, ends, received, partial, gradient)


def y_kernel(n, inv_ref, m_ref, v_ref, part_ref, after_ref, g_ref, c_ref, high_ref, low_ref):
    ny = inv_ref.shape[0]
    nz = v_ref.shape[3]
    row = lax.broadcasted_iota(jnp.int32, (ny, ny), 0)
    column = lax.broadcasted_iota(jnp.int32, (ny, ny), 1)
    metric = jnp.sum(jnp.where(row == column, m_ref[...], 0.0), axis=1, keepdims=True)
    high, low = split(times_stencil(inv_ref[...]) * metric)
    high_ref[...] = high
    low_ref[...] = low

    def step(group, carry):
        for u in range(GROUP):
            p = group * GROUP + u
            fields = six([v_ref[i, p] for i in range(3)], 1)
            for a in (0, 2, 4):
                high, low = split(jnp.concatenate(fields[a : a + 2], axis=1))
                result = dot(high_ref[...], high) + dot(low_ref[...], high) + dot(high_ref[...], low)
                for j in range(2):
                    f = a + j
                    value = result[:, j * nz : (j + 1) * nz]
                    if f < 3:
                        g_ref[f, p] = value
                    else:
                        c_ref[f - 3, p] = value + part_ref[f - 3, p]
        return carry

    lax.fori_loop(0, n // GROUP, step, 0)


def y_solve(y_inverse, metric, velocity, partial, after):
    _, n, ny, nz = velocity.shape
    return pl.pallas_call(
        functools.partial(y_kernel, n),
        in_specs=[WHOLE] * 4 + [ANY],
        out_specs=[WHOLE, WHOLE],
        out_shape=[in_vmem(3, n, ny, nz), in_vmem(3, n, ny, nz)],
        scratch_shapes=[pltpu.VMEM((ny, ny), BF16), pltpu.VMEM((ny, ny), BF16)],
        input_output_aliases={3: 1},
        compiler_params=params(),
        cost_estimate=cost(velocity, Y_COST),
        name="y_solve",
    )(y_inverse, metric, velocity, partial, after)


LINES = 128


def z_own_kernel(
    n, inv_ref, m_ref, v_ref, after_ref, g_ref, c_ref, right_ref, left_ref, far_ref, main_ref
):
    nz = inv_ref.shape[0]
    ny = v_ref.shape[2]
    high, low = split(times_stencil(inv_ref[...]).T * m_ref[...])
    both = jnp.concatenate([high, low], axis=1)
    main_ref[...] = jnp.concatenate([both, both], axis=0)
    first_scale = 1.0 / m_ref[0:1, 0:1]
    last_scale = 1.0 / m_ref[0:1, nz - 1 : nz]
    lane = lax.broadcasted_iota(jnp.int32, (ny, nz), 1)

    def corner(i, j):
        return jnp.broadcast_to(inv_ref[i : i + 1, j : j + 1], (1, LINES))

    m = nz - 1
    corners_right = [corner(m, m), corner(m, m - 1), corner(m, 0), corner(m, 1)]
    corners_left = [corner(0, 0), corner(0, 1), corner(0, m), corner(0, m - 1)]

    def step(group, carry):
        gathered = []
        for u in range(GROUP):
            p = group * GROUP + u
            velocities = [v_ref[i, p] for i in range(3)]
            columns = jnp.zeros((ny, nz), F32)
            for f, field in enumerate(six(velocities, 2)):
                high, low = split(field)
                both = dot(jnp.concatenate([high, low], axis=1), main_ref[...])
                value = both[:, :nz] + both[:, nz:]
                if f < 3:
                    g_ref[f, p] = value
                else:
                    c_ref[f - 3, p] = value
                columns = jnp.where(lane // 2 == f, pltpu.roll(value, 1 + 2 * f, axis=1), columns)
            for i in range(3):
                columns = jnp.where(lane // 4 == 3 + i, pltpu.roll(velocities[i], 14 + 4 * i, axis=1), columns)
            gathered.append(columns)
        lines = jnp.concatenate(gathered, axis=0)
        for j in range(GROUP * ny // LINES):
            turned = lines[j * LINES : (j + 1) * LINES].T

            def row(index):
                return turned[index : index + 1]

            def block(ends, scale, column, corners):
                rows = [row(ends + 2 * f) * scale for f in range(6)] + corners[0:2]
                rows = rows + [row(12 + 4 * i + column) for i in range(3)] + corners[2:3]
                rows = rows + [row(13 + 4 * i + column) for i in range(3)] + corners[3:4]
                return jnp.concatenate(rows, axis=0)

            index = group * (GROUP * ny // LINES) + j
            to_right = block(0, last_scale, 0, corners_right)
            to_left = block(1, first_scale, 2, corners_left)
            right_ref[index] = to_right
            left_ref[index] = to_left
            far_ref[index] = jnp.concatenate([to_right[8:16], to_left[8:16]], axis=0)
        return carry

    lax.fori_loop(0, n // GROUP, step, 0)


def z_own(z_inverse, metric, velocity, after):
    _, n, ny, nz = velocity.shape
    return pl.pallas_call(
        functools.partial(z_own_kernel, n),
        in_specs=[WHOLE, WHOLE, WHOLE, ANY],
        out_specs=[WHOLE] * 5,
        out_shape=[in_vmem(3, n, ny, nz)] * 2 + [layer_shape(n * ny // LINES, 16, LINES)] * 3,
        scratch_shapes=[pltpu.VMEM((2 * nz, 2 * nz), BF16)],
        compiler_params=params(),
        cost_estimate=cost(velocity, 3),
        name="z_own",
    )(z_inverse, metric, velocity, after)


def z_side(own_right, own_left, left, right, left_2, right_2):
    index = lax.broadcasted_iota(jnp.int32, (8, LINES), 0)

    def row(values, i):
        return jnp.broadcast_to(values[i : i + 1], (8, LINES))

    def fields(velocities):
        products = velocities * row(velocities, 2)
        return jnp.where(index < 3, velocities, pltpu.roll(products, 3, axis=0))

    def pair(velocities):
        return fields(velocities), fields(pltpu.roll(velocities, 4, axis=0))

    def from_left(velocities):
        far, near = pair(velocities)
        return -NEAR * near - FAR * far, -FAR * near

    def from_right(velocities):
        near, far = pair(velocities)
        return NEAR * near + FAR * far, FAR * near

    def first_value(values, at_left, at_right):
        return (
            values[0:8]
            + row(values, 6) * at_left[0]
            + row(values, 7) * at_left[1]
            + row(values, 11) * at_right[0]
            + row(values, 15) * at_right[1]
        )

    def last_value(values, at_left, at_right):
        return (
            values[0:8]
            + row(values, 11) * at_left[0]
            + row(values, 15) * at_left[1]
            + row(values, 6) * at_right[0]
            + row(values, 7) * at_right[1]
        )

    at_left, at_right = from_left(left[8:16]), from_right(right[8:16])
    own_first = first_value(own_left, at_left, at_right)
    own_last = last_value(own_right, at_left, at_right)
    left_value = last_value(left, from_left(left_2[0:8]), from_right(own_left[8:16]))
    right_value = first_value(right, from_left(own_right[8:16]), from_right(right_2[8:16]))
    left_tail, right_head = row(left, 6), row(right, 6)
    left_final = (left_value - COUPLING * left_tail * own_first) / (
        1.0 - COUPLING * COUPLING * left_tail * row(own_left, 6)
    )
    right_start = (right_value - COUPLING * right_head * own_last) / (
        1.0 - COUPLING * COUPLING * right_head * row(own_right, 6)
    )
    return jnp.concatenate(
        [at_left[0] - COUPLING * left_final, at_left[1], at_right[0] - COUPLING * right_start, at_right[1]], axis=0
    )


def z_join_kernel(
    n, inv_ref, m_ref, g_ref, part_ref, own_right_ref, own_left_ref, left_ref, right_ref, left_2_ref, right_2_ref, y_ref,
    after_ref, gradient_ref, c_ref, side_ref, out_ref, sem,
):
    nz = inv_ref.shape[0]
    ny = g_ref.shape[2]
    columns = inv_ref[...].T * m_ref[...]
    index = lax.broadcasted_iota(jnp.int32, (32, nz), 0)
    kind = index // 8
    picked = jnp.where(
        kind == 0,
        columns[0:1],
        jnp.where(kind == 1, columns[1:2], jnp.where(kind == 2, columns[nz - 1 : nz], columns[nz - 2 : nz - 1])),
    )
    wide = jnp.concatenate([jnp.where(index % 8 == f, picked, 0.0) for f in range(6)], axis=1)
    high, low = split(wide)
    side_ref[...] = jnp.concatenate([high, high, low], axis=0)
    blocks = GROUP * ny // LINES
    y_copy = pltpu.make_async_copy(y_ref, gradient_ref.at[:, 1], sem.at[n // GROUP])
    y_copy.start()

    def copy(group):
        planes = pl.ds(group * GROUP, GROUP)
        return pltpu.make_async_copy(out_ref.at[:, planes], gradient_ref.at[:, 2, planes], sem.at[group])

    def step(group, carry):
        sides = []
        for j in range(blocks):
            lines = (own_right_ref, own_left_ref, left_ref, right_ref, left_2_ref, right_2_ref)
            high, low = split(z_side(*(ref[group * blocks + j] for ref in lines)).T)
            sides.append(jnp.concatenate([high, low, high], axis=1))
        for pair in range(GROUP // 2):
            half = blocks // (GROUP // 2)
            lines = jnp.concatenate(sides[pair * half : (pair + 1) * half], axis=0)
            for f in range(0, 6, 2):
                added = dot(lines, side_ref[:, f * nz : (f + 2) * nz])
                for u in range(2):
                    p = group * GROUP + 2 * pair + u
                    for j in range(2):
                        value = added[u * ny : (u + 1) * ny, j * nz : (j + 1) * nz]
                        if f + j < 3:
                            out_ref[f + j, p] = value + g_ref[f + j, p]
                        else:
                            c_ref[f + j - 3, p] = value + part_ref[f + j - 3, p]
        copy(group).start()
        return carry

    lax.fori_loop(0, n // GROUP, step, 0)

    def drain(group, carry):
        copy(group).wait()
        return carry

    lax.fori_loop(0, n // GROUP, drain, 0)
    y_copy.wait()


def z_join(z_inverse, metric, own, partial, lines, y_gradient, after):
    _, n, ny, nz = own.shape
    return pl.pallas_call(
        functools.partial(z_join_kernel, n),
        in_specs=[WHOLE] * 11 + [ANY],
        out_specs=[ANY, WHOLE],
        out_shape=[layer_shape(3, 3, n, ny, nz), in_vmem(3, n, ny, nz)],
        scratch_shapes=[
            pltpu.VMEM((96, 6 * nz), BF16),
            pltpu.VMEM((3, n, ny, nz), F32),
            pltpu.SemaphoreType.DMA((n // GROUP + 1,)),
        ],
        input_output_aliases={3: 1},
        compiler_params=params(),
        cost_estimate=cost(own, Z_COST),
        name="z_join",
    )(z_inverse, metric, own, partial, *lines, y_gradient, after)


def on_device(mesh, velocity, metric_x, metric_y, metric_z, x_inverse, y_inverse, z_inverse):
    n = velocity.shape[1]
    blocks = mesh.shape["gx"] * 2
    across = [(i, (i + 1) % blocks) for i in range(1, blocks, 2)]
    across = across + [(j, i) for i, j in across]
    beside = [(0, 1), (1, 0)]
    count = mesh.shape["gz"]

    def shift(by):
        return [(i, (i + by) % count) for i in range(count)]

    own, inner, table, y_inverse, metric_y, z_inverse, metric_z = prepare(
        x_inverse, metric_x[None], y_inverse, metric_y[None], z_inverse, metric_z[None], velocity
    )
    near = lax.ppermute(own, ("gx", "gy"), across)
    halo = lax.ppermute(inner, "gy", beside)
    held = pltpu.with_memory_space_constraint(velocity, pltpu.VMEM)

    x_sent, x_partial = x_ends(table, held, halo)
    x_received = lax.ppermute(x_sent, ("gx", "gy"), across)

    z_gradient, convection, to_right, to_left, to_far = z_own(z_inverse, metric_z, held, x_sent)
    left_far = lax.ppermute(to_far, "gz", shift(2))
    right_far = left_far if shift(2) == shift(-2) else lax.ppermute(to_far, "gz", shift(-2))
    z_lines = (
        to_right,
        to_left,
        lax.ppermute(to_right, "gz", shift(1)),
        lax.ppermute(to_left, "gz", shift(-1)),
        left_far,
        right_far,
    )

    y_gradient, convection = y_solve(y_inverse, metric_y, held, convection, near)
    outer, x_end = x_face(table, x_received, x_sent, x_partial, own, near, convection, n)
    x_other = lax.ppermute(x_end, "gy", beside)

    gradient, convection = z_join(z_inverse, metric_z, z_gradient, convection, z_lines, y_gradient, x_end)
    return tuple(x_solve(table, held, near, halo, outer, x_end, x_other, convection, gradient))


def solution(mesh):
    return jax.shard_map(
        functools.partial(on_device, mesh),
        mesh=mesh,
        in_specs=(
            P(None, ("gx", "gy"), None, "gz"),
            P(("gx", "gy")),
            P(),
            P("gz"),
            P(("gx", "gy"), None),
            P(),
            P("gz", None),
        ),
        out_specs=(P(None, None, ("gx", "gy"), None, "gz"), P(None, ("gx", "gy"), None, "gz")),
        check_vma=False,
    )
```

```python
import functools

import jax
import jax.numpy as jnp
from jax import lax
from jax.experimental import pallas as pl
from jax.experimental.pallas import tpu as pltpu
from jax.sharding import PartitionSpec as P

COUPLING = 1.0 / 3.0
NEAR = 7.0 / 9.0
FAR = 1.0 / 36.0
F32 = jnp.float32
BF16 = jnp.bfloat16
SMEM = pltpu.SMEM
VMEM_LIMIT = 20 * 1024 * 1024
GROUP = 8
Y_COST = 20_000_000_000
Z_COST = 20_000_000_000


def split(values):
    high = values.astype(BF16)
    low = (values - high.astype(F32)).astype(BF16)
    return high, low


def dot(a, b):
    return lax.dot_general(a, b, (((1,), (0,)), ((), ())), preferred_element_type=F32)


def dot_nt(a, b):
    return lax.dot_general(a, b, (((1,), (1,)), ((), ())), preferred_element_type=F32)


def params():
    return pltpu.CompilerParams(vmem_limit_bytes=VMEM_LIMIT)


def six(velocity, direction):
    return list(velocity) + [velocity[i] * velocity[direction] for i in range(3)]


def times_stencil(inverse):
    rows, length = inverse.shape
    zeros = jnp.zeros((rows, 2), F32)
    wide = jnp.concatenate([zeros, inverse, zeros], axis=1)

    def column(offset):
        return wide[:, 2 + offset : 2 + offset + length]

    return NEAR * (column(-1) - column(1)) + FAR * (column(-2) - column(2))


def in_vmem(*shape):
    return pltpu.VMEM(shape, F32)


ANY = pl.BlockSpec(memory_space=pl.ANY)
WHOLE = pl.BlockSpec(memory_space=pltpu.VMEM)
SCALARS = pl.BlockSpec(memory_space=SMEM)


def cost(array, passes):
    return pl.CostEstimate(flops=passes, bytes_accessed=passes, transcendentals=0)


def layer_shape(*shape):
    return jax.ShapeDtypeStruct(shape, F32)


class Ends:
    def __init__(self, n):
        self.first = lax.axis_index("gy") == 0
        self.n = n
        self.o = jnp.where(self.first, 0, n - 1)
        self.o1 = jnp.where(self.first, 1, n - 2)
        self.q = jnp.where(self.first, n - 1, 0)
        self.q1 = jnp.where(self.first, n - 2, 1)
        self.sign_o = jnp.where(self.first, -1.0, 1.0).astype(F32)
        self.sign_q = -self.sign_o


class Table:
    def __init__(self, n):
        self.source, self.forward, self.backward = 0, n, 2 * n
        self.send, self.last = 3 * n, 4 * n + 2
        self.oo, self.oo1, self.qo, self.qo1, self.qq = range(5 * n + 4, 5 * n + 9)
        self.size = 5 * n + 9


def prepare_kernel(n, v_ref, own_ref, halo_ref, sem):
    ends = Ends(n)
    copies = []
    for i in range(3):
        copies.append(pltpu.make_async_copy(v_ref.at[i, ends.o], own_ref.at[i], sem.at[3 * i]))
        for j in range(2):
            plane = jnp.where(ends.first, n - 2 + j, j)
            copies.append(pltpu.make_async_copy(v_ref.at[i, plane], halo_ref.at[i, j], sem.at[3 * i + 1 + j]))
    for copy in copies:
        copy.start()
    for copy in copies:
        copy.wait()


def prepare(velocity):
    _, n, ny, nz = velocity.shape
    return pl.pallas_call(
        functools.partial(prepare_kernel, n),
        in_specs=[ANY],
        out_specs=[WHOLE] * 2,
        out_shape=[layer_shape(3, ny, nz), layer_shape(3, 2, ny, nz)],
        scratch_shapes=[pltpu.SemaphoreType.DMA((9,))],
        compiler_params=params(),
        name="prepare",
    )(pltpu.with_memory_space_constraint(velocity, pltpu.HBM))


def tables_kernel(
    n, xi_ref, mx_ref, yi_ref, my_ref, zi_ref, mz_ref, after_ref,
    table_ref, y_ref, y_metric_ref, z_ref, z_metric_ref, x_ref, m_ref, sem,
):
    ends = Ends(n)
    nz = table_ref.shape[2]
    small = [pltpu.make_async_copy(xi_ref, x_ref, sem.at[0]), pltpu.make_async_copy(mx_ref, m_ref, sem.at[1])]
    copies = [
        pltpu.make_async_copy(zi_ref, z_ref, sem.at[2]),
        pltpu.make_async_copy(mz_ref, z_metric_ref, sem.at[3]),
        pltpu.make_async_copy(yi_ref, y_ref, sem.at[4]),
        pltpu.make_async_copy(my_ref, y_metric_ref, sem.at[5]),
    ]
    for copy in small + copies:
        copy.start()
    for copy in small:
        copy.wait()

    table = Table(n)
    first = ends.first

    def spread(value):
        return jnp.broadcast_to(value, (8, nz))

    def entry(i, j):
        return spread(x_ref[i : i + 1, j : j + 1])

    metric = [spread(m_ref[0:1, k : k + 1]) for k in range(n)]
    above = [entry(i, i + 1) for i in range(n - 1)]
    diagonal = [entry(i, i) for i in range(n)]
    ratio = [-above[i] / diagonal[i + 1] for i in range(n - 1)]
    ratio.append(-entry(n - 1, n - 2) / diagonal[n - 2] * diagonal[n - 1])
    for k in range(n):
        if k == 0:
            source = metric[k]
        elif k == n - 1:
            source = diagonal[k] * metric[k]
        else:
            source = (1.0 + ratio[k] * ratio[k - 1]) * metric[k]
        table_ref[table.source + k] = FAR * source
        table_ref[table.forward + k] = ratio[k] * metric[k] / metric[k - 1] if k > 0 else metric[k]
        table_ref[table.backward + k] = ratio[k] * metric[k] / metric[k + 1] if k < n - 1 else metric[k]

    top = [entry(0, k) for k in range(n)]
    bottom = [entry(n - 1, k) for k in range(n)]
    outer = [jnp.where(first, top[k], bottom[k]) for k in range(n)]
    inner = [jnp.where(first, bottom[k], top[k]) for k in range(n)]
    sign_o, sign_q = ends.sign_o, ends.sign_q
    for base, row, factor in ((table.send, outer, -COUPLING), (table.last, inner, 1.0)):

        def at(k):
            return row[k] if 0 <= k < n else jnp.zeros_like(row[0])

        for k in range(n):
            value = factor * (NEAR * (at(k - 1) - at(k + 1)) + FAR * (at(k - 2) - at(k + 2)))
            if base == table.send:
                if k == 0:
                    value = value + jnp.where(first, NEAR, 0.0)
                elif k == 1:
                    value = value + jnp.where(first, FAR, 0.0)
                elif k == n - 2:
                    value = value - jnp.where(first, 0.0, FAR)
                elif k == n - 1:
                    value = value - jnp.where(first, 0.0, NEAR)
            table_ref[base + k] = value
        at_q = jnp.where(first, row[n - 1], row[0])
        at_q1 = jnp.where(first, row[n - 2], row[1])
        near = factor * sign_q * (NEAR * at_q + FAR * at_q1)
        far = factor * sign_q * FAR * at_q
        table_ref[base + n] = jnp.where(first, near, far)
        table_ref[base + n + 1] = jnp.where(first, far, near)
    table_ref[table.oo] = jnp.where(first, outer[0], outer[n - 1])
    table_ref[table.oo1] = jnp.where(first, outer[1], outer[n - 2])
    table_ref[table.qo] = jnp.where(first, inner[0], inner[n - 1])
    table_ref[table.qo1] = jnp.where(first, inner[1], inner[n - 2])
    table_ref[table.qq] = jnp.where(first, inner[n - 1], inner[0])
    for copy in copies:
        copy.wait()


def tables(x_inverse, metric_x, y_inverse, metric_y, z_inverse, metric_z, after):
    n, ny, nz = x_inverse.shape[0], y_inverse.shape[0], z_inverse.shape[0]
    inputs = (x_inverse, metric_x, y_inverse, metric_y, z_inverse, metric_z)
    return pl.pallas_call(
        functools.partial(tables_kernel, n),
        in_specs=[ANY] * 7,
        out_specs=[WHOLE] * 5,
        out_shape=[
            in_vmem(Table(n).size, 8, nz),
            in_vmem(ny, ny),
            in_vmem(1, ny),
            in_vmem(nz, nz),
            in_vmem(1, nz),
        ],
        scratch_shapes=[pltpu.VMEM((n, n), F32), pltpu.VMEM((1, n), F32), pltpu.SemaphoreType.DMA((6,))],
        compiler_params=params(),
        name="tables",
    )(*(pltpu.with_memory_space_constraint(value, pltpu.HBM) for value in inputs), after)


def x_ends_kernel(n, ny, table_ref, v_ref, halo_ref, w_ref, l_ref):
    table = Table(n)

    def tile(index, carry):
        start = pl.multiple_of(index * 8, 8)
        rows = pl.ds(start, 8)
        w = [None] * 6
        l = [None] * 6
        for k in range(n + 2):
            if k < n:
                fields = six([v_ref[i, k, rows, :] for i in range(3)], 0)
            else:
                fields = six([halo_ref[i, k - n, rows, :] for i in range(3)], 0)
            a, b = table_ref[table.send + k], table_ref[table.last + k]
            for f in range(6):
                w[f] = a * fields[f] if k == 0 else w[f] + a * fields[f]
                l[f] = b * fields[f] if k == 0 else l[f] + b * fields[f]
        for f in range(6):
            w_ref[pl.ds(f * ny + start, 8), :] = w[f]
            l_ref[f, rows, :] = l[f]
        return carry

    lax.fori_loop(0, ny // 8, tile, 0)
    index = lax.broadcasted_iota(jnp.int32, (8, w_ref.shape[1]), 0)
    w_ref[6 * ny : 6 * ny + 8, :] = jnp.where(index == 0, table_ref[table.oo], table_ref[table.oo1])


def x_ends(table, velocity, halo):
    _, n, ny, nz = velocity.shape
    return pl.pallas_call(
        functools.partial(x_ends_kernel, n, ny),
        in_specs=[WHOLE] * 3,
        out_specs=[WHOLE, WHOLE],
        out_shape=[layer_shape(6 * ny + 8, nz), layer_shape(6, ny, nz)],
        compiler_params=params(),
        cost_estimate=cost(velocity, 3),
        name="x_ends",
    )(table, velocity, halo)


def x_face_kernel(n, ny, table_ref, wr_ref, ws_ref, l_ref, own_ref, near_ref, after_ref, w_ref, e_ref):
    ends = Ends(n)
    table = Table(n)
    shape = (8, wr_ref.shape[1])
    p_oo = jnp.broadcast_to(wr_ref[6 * ny : 6 * ny + 1, :], shape)
    p_oo1 = jnp.broadcast_to(wr_ref[6 * ny + 1 : 6 * ny + 2, :], shape)
    x_qo = table_ref[table.qo]
    inverse_den = 1.0 / (1.0 - COUPLING * COUPLING * table_ref[table.oo] * p_oo)
    sent_weight = COUPLING * p_oo
    own_weight = COUPLING * FAR * ends.sign_o * p_oo1
    near_weight = COUPLING * FAR * ends.sign_o * COUPLING * table_ref[table.oo1] * p_oo
    end_weight = ends.sign_o * FAR * table_ref[table.qo1]

    def tile(index, carry):
        start = pl.multiple_of(index * 8, 8)
        rows = pl.ds(start, 8)
        own = six([own_ref[i, rows, :] for i in range(3)], 0)
        near = six([near_ref[i, rows, :] for i in range(3)], 0)
        for f in range(6):
            field = pl.ds(f * ny + start, 8)
            w = wr_ref[field, :] - sent_weight * ws_ref[field, :]
            w = (w + own_weight * own[f] + near_weight * near[f]) * inverse_den
            w_ref[f, rows, :] = 36.0 * w
            e_ref[field, :] = l_ref[f, rows, :] + x_qo * w + end_weight * near[f]
        return carry

    lax.fori_loop(0, ny // 8, tile, 0)
    e_ref[6 * ny : 6 * ny + 8, :] = table_ref[table.qq]


def x_face(table, received, sent, partial, own, near, after, n):
    _, ny, nz = own.shape
    return pl.pallas_call(
        functools.partial(x_face_kernel, n, ny),
        in_specs=[WHOLE] * 6 + [ANY],
        out_specs=[WHOLE, WHOLE],
        out_shape=[layer_shape(6, ny, nz), layer_shape(6 * ny + 8, nz)],
        compiler_params=params(),
        cost_estimate=cost(received, 1),
        name="x_face",
    )(table, received, sent, partial, own, near, after)


def x_solve_kernel(
    n, ny, table_ref, v_ref, near_ref, halo_ref, w_ref, e_ref, r_ref, part_ref, z_ref, held_ref,
    gradient_ref, convection_ref, g_ref, c_ref, sem,
):
    table = Table(n)
    parts = sem.shape[1]
    share = ny // parts
    z_copy = pltpu.make_async_copy(z_ref, gradient_ref.at[:, 2], sem.at[2, 0])
    z_copy.start()
    p_qq = r_ref[6 * ny : 6 * ny + 8, :]
    weight = COUPLING * p_qq
    scale = -36.0 * COUPLING / (1.0 - COUPLING * COUPLING * table_ref[table.qq] * p_qq)

    def copies(part):
        rows = pl.ds(pl.multiple_of(part * share, 8), share)
        return (
            pltpu.make_async_copy(g_ref.at[:, :, rows], gradient_ref.at[:, 0, :, rows], sem.at[0, part]),
            pltpu.make_async_copy(c_ref.at[:, :, rows], convection_ref.at[:, :, rows], sem.at[1, part]),
        )

    def run(first):
        sign_o = -1.0 if first else 1.0
        near_j, far_j = (0, 1) if first else (1, 0)

        def tile(index, carry):
            start = pl.multiple_of(index * 8, 8)
            rows = pl.ds(start, 8)
            near = six([near_ref[i, rows, :] for i in range(3)], 0)
            inner_near = six([halo_ref[i, near_j, rows, :] for i in range(3)], 0)
            inner_far = six([halo_ref[i, far_j, rows, :] for i in range(3)], 0)
            for f in range(6):
                if f < 3:
                    line = [v_ref[f, k, rows, :] for k in range(n)]
                else:
                    line = [v_ref[f - 3, k, rows, :] * v_ref[0, k, rows, :] for k in range(n)]
                field = pl.ds(f * ny + start, 8)
                inner = -sign_o * (28.0 * inner_near[f] + inner_far[f])
                inner = inner + scale * (r_ref[field, :] - weight * e_ref[field, :])
                outer = w_ref[f, rows, :]
                forward = []
                for k in range(n):
                    if k == 0:
                        source = 28.0 * line[1] + line[2] + (outer if first else inner)
                    elif k == 1:
                        source = 28.0 * (line[2] - line[0]) + (line[3] - (near[f] if first else inner_near[f]))
                    elif k == n - 1:
                        source = (inner if first else outer) - 28.0 * line[n - 2] - line[n - 3]
                    elif k == n - 2:
                        source = 28.0 * (line[n - 1] - line[n - 3]) + (
                            (inner_near[f] if first else near[f]) - line[n - 4]
                        )
                    else:
                        source = 28.0 * (line[k + 1] - line[k - 1]) + (line[k + 2] - line[k - 2])
                    value = table_ref[table.source + k] * source
                    if k > 0:
                        value = value - table_ref[table.forward + k] * forward[k - 1]
                    forward.append(value)
                solved = None
                for k in reversed(range(n)):
                    solved = forward[k] if k == n - 1 else forward[k] - table_ref[table.backward + k] * solved
                    if f < 3:
                        g_ref[f, k, rows, :] = solved
                    else:
                        c_ref[f - 3, k, rows, :] = solved + part_ref[f - 3, k, rows, :]
            return carry

        def step(part, carry):
            lax.fori_loop(part * (share // 8), (part + 1) * (share // 8), tile, 0)
            for copy in copies(part):
                copy.start()
            return carry

        lax.fori_loop(0, parts, step, 0)

    is_first = lax.axis_index("gy") == 0
    pl.when(is_first)(functools.partial(run, True))
    pl.when(jnp.logical_not(is_first))(functools.partial(run, False))

    def drain(part, carry):
        for copy in copies(part):
            copy.wait()
        return carry

    z_copy.wait()
    lax.fori_loop(0, parts, drain, 0)


def x_solve(table, velocity, near, halo, outer, ends, received, partial, z_gradient, gradient, parts=12):
    _, n, ny, nz = velocity.shape
    return pl.pallas_call(
        functools.partial(x_solve_kernel, n, ny),
        in_specs=[WHOLE] * 9 + [ANY],
        out_specs=[ANY, ANY],
        out_shape=[layer_shape(*gradient.shape), layer_shape(3, n, ny, nz)],
        scratch_shapes=[
            pltpu.VMEM((3, n, ny, nz), F32),
            pltpu.VMEM((3, n, ny, nz), F32),
            pltpu.SemaphoreType.DMA((3, parts)),
        ],
        input_output_aliases={9: 0},
        compiler_params=params(),
        cost_estimate=cost(velocity, 5),
        name="x_solve",
    )(table, velocity, near, halo, outer, ends, received, partial, z_gradient, gradient)


def y_kernel(n, inv_ref, m_ref, v_ref, part_ref, after_ref, g_ref, c_ref, high_ref, low_ref):
    ny = inv_ref.shape[0]
    nz = v_ref.shape[3]
    row = lax.broadcasted_iota(jnp.int32, (ny, ny), 0)
    column = lax.broadcasted_iota(jnp.int32, (ny, ny), 1)
    metric = jnp.sum(jnp.where(row == column, m_ref[...], 0.0), axis=1, keepdims=True)
    high, low = split(times_stencil(inv_ref[...]) * metric)
    high_ref[...] = high
    low_ref[...] = low

    def step(group, carry):
        for u in range(GROUP):
            p = group * GROUP + u
            fields = six([v_ref[i, p] for i in range(3)], 1)
            for a in (0, 2, 4):
                high, low = split(jnp.concatenate(fields[a : a + 2], axis=1))
                result = dot(high_ref[...], high) + dot(low_ref[...], high) + dot(high_ref[...], low)
                for j in range(2):
                    f = a + j
                    value = result[:, j * nz : (j + 1) * nz]
                    if f < 3:
                        g_ref[f, p] = value
                    else:
                        c_ref[f - 3, p] = value + part_ref[f - 3, p]
        return carry

    lax.fori_loop(0, n // GROUP, step, 0)


def y_solve(y_inverse, metric, velocity, partial, after):
    _, n, ny, nz = velocity.shape
    return pl.pallas_call(
        functools.partial(y_kernel, n),
        in_specs=[WHOLE] * 4 + [ANY],
        out_specs=[WHOLE, WHOLE],
        out_shape=[in_vmem(3, n, ny, nz), in_vmem(3, n, ny, nz)],
        scratch_shapes=[pltpu.VMEM((ny, ny), BF16), pltpu.VMEM((ny, ny), BF16)],
        input_output_aliases={3: 1},
        compiler_params=params(),
        cost_estimate=cost(velocity, Y_COST),
        name="y_solve",
    )(y_inverse, metric, velocity, partial, after)


LINES = 128
PACK = 4


def z_own_kernel(
    n, inv_ref, m_ref, v_ref, after_ref, g_ref, c_ref, right_ref, left_ref, far_ref, main_ref, turned_ref
):
    nz = inv_ref.shape[0]
    ny = v_ref.shape[2]
    high, low = split(times_stencil(inv_ref[...]).T * m_ref[...])
    both = jnp.concatenate([high, low], axis=1)
    main_ref[...] = jnp.concatenate([both, both], axis=0)
    first_scale = 1.0 / m_ref[0:1, 0:1]
    last_scale = 1.0 / m_ref[0:1, nz - 1 : nz]
    lane = lax.broadcasted_iota(jnp.int32, (ny, nz), 1)

    m = nz - 1
    index = lax.broadcasted_iota(jnp.int32, right_ref.shape[1:], 0)
    for ref, corners in ((right_ref, ((m, m), (m, m - 1), (m, 0), (m, 1))), (left_ref, ((0, 0), (0, 1), (0, m), (0, m - 1)))):
        row = jnp.zeros(right_ref.shape[1:], F32)
        for position, (i, j) in enumerate(corners):
            row = jnp.where(index == position, inv_ref[i : i + 1, j : j + 1], row)
        ref[12] = row

    def segments(u):
        start = u * ny
        while start < (u + 1) * ny:
            stop = min((start // LINES + 1) * LINES, (u + 1) * ny)
            yield start // LINES, start - u * ny, stop - u * ny
            start = stop

    def step(group, carry):
        pieces = [[] for _ in range(GROUP * ny // LINES)]
        for u in range(GROUP):
            p = group * GROUP + u
            velocities = [v_ref[i, p] for i in range(3)]
            values = []
            for f, field in enumerate(six(velocities, 2)):
                high, low = split(field)
                both = dot(jnp.concatenate([high, low], axis=1), main_ref[...])
                value = both[:, :nz] + both[:, nz:]
                if f < 3:
                    g_ref[f, p] = value
                else:
                    c_ref[f - 3, p] = value
                values.append(value)
            for block, start, stop in segments(u):
                base = block % PACK * 32
                columns = pltpu.roll(values[0][start:stop], base + 1, axis=1)
                for f in range(1, 6):
                    moved = pltpu.roll(values[f][start:stop], (base + 1 + 2 * f) % nz, axis=1)
                    columns = jnp.where(lane[start:stop] // 2 == base // 2 + f, moved, columns)
                for i in range(3):
                    moved = pltpu.roll(velocities[i][start:stop], (base + 14 + 4 * i) % nz, axis=1)
                    columns = jnp.where(lane[start:stop] // 4 == base // 4 + 3 + i, moved, columns)
                pieces[block].append(columns)
        for j, parts in enumerate(pieces):
            if j % PACK == 0:
                packed = jnp.concatenate(parts, axis=0)
                for other in range(1, PACK):
                    columns = jnp.concatenate(pieces[j + other], axis=0)
                    packed = jnp.where(lane[0:LINES] // 32 == other, columns, packed)
                turned_ref[j // PACK] = packed.T
                blocks = pl.ds(group * len(pieces) + j, PACK)

                def rows(position):
                    return turned_ref[j // PACK, pl.ds(position, PACK, stride=32), :]

                for f in range(6):
                    right_ref[f, blocks, :] = rows(2 * f) * last_scale
                    left_ref[f, blocks, :] = rows(2 * f + 1) * first_scale
                for column in range(4):
                    for i in range(3):
                        values = rows(12 + 4 * i + column)
                        ref = right_ref if column < 2 else left_ref
                        ref[6 + 3 * (column % 2) + i, blocks, :] = values
                        far_ref[3 * column + i, blocks, :] = values
        return carry

    lax.fori_loop(0, n // GROUP, step, 0)


def z_own(z_inverse, metric, velocity, after):
    _, n, ny, nz = velocity.shape
    return pl.pallas_call(
        functools.partial(z_own_kernel, n),
        in_specs=[WHOLE, WHOLE, WHOLE, ANY],
        out_specs=[WHOLE] * 5,
        out_shape=[in_vmem(3, n, ny, nz)] * 2 + [layer_shape(13, n * ny // LINES, LINES)] * 2
        + [layer_shape(12, n * ny // LINES, LINES)],
        scratch_shapes=[
            pltpu.VMEM((2 * nz, 2 * nz), BF16),
            pltpu.VMEM((GROUP * ny // LINES // PACK, LINES, LINES), F32),
        ],
        compiler_params=params(),
        cost_estimate=cost(velocity, 3),
        name="z_own",
    )(z_inverse, metric, velocity, after)


def z_side(own_right, own_left, left, right, left_2, right_2, out_ref):
    blocks = own_left.shape[1]
    shape = own_left.shape[1:]

    def pair(ref, start):
        return six([ref[start + i] for i in range(3)], 2), six([ref[start + 3 + i] for i in range(3)], 2)

    def from_left(ref, start):
        far, near = pair(ref, start)
        return [(-NEAR * near[f] - FAR * far[f], -FAR * near[f]) for f in range(6)]

    def from_right(ref, start):
        near, far = pair(ref, start)
        return [(NEAR * near[f] + FAR * far[f], FAR * near[f]) for f in range(6)]

    def entries(ref):
        return [jnp.broadcast_to(ref[12, i : i + 1], shape) for i in range(4)]

    def first_value(ref, corners, f, at_left, at_right):
        x_00, x_01, x_0m, x_0l = corners
        return ref[f] + x_00 * at_left[f][0] + x_01 * at_left[f][1] + x_0m * at_right[f][0] + x_0l * at_right[f][1]

    def last_value(ref, corners, f, at_left, at_right):
        x_mm, x_ml, x_m0, x_m1 = corners
        return ref[f] + x_m0 * at_left[f][0] + x_m1 * at_left[f][1] + x_mm * at_right[f][0] + x_ml * at_right[f][1]

    own_first_row, own_last_row, left_row, right_row = (entries(ref) for ref in (own_left, own_right, left, right))
    at_left, at_right = from_left(left, 6), from_right(right, 6)
    left_at_left, left_at_right = from_left(left_2, 0), from_right(own_left, 6)
    right_at_left, right_at_right = from_left(own_right, 6), from_right(right_2, 6)
    left_den = 1.0 / (1.0 - COUPLING * COUPLING * left_row[0] * own_first_row[0])
    right_den = 1.0 / (1.0 - COUPLING * COUPLING * right_row[0] * own_last_row[0])
    for f in range(8):
        if f < 6:
            own_first = first_value(own_left, own_first_row, f, at_left, at_right)
            own_last = last_value(own_right, own_last_row, f, at_left, at_right)
            left_value = last_value(left, left_row, f, left_at_left, left_at_right)
            right_value = first_value(right, right_row, f, right_at_left, right_at_right)
            left_final = (left_value - COUPLING * left_row[0] * own_first) * left_den
            right_start = (right_value - COUPLING * right_row[0] * own_last) * right_den
            kinds = (
                at_left[f][0] - COUPLING * left_final,
                at_left[f][1],
                at_right[f][0] - COUPLING * right_start,
                at_right[f][1],
            )
        else:
            kinds = (jnp.zeros(shape, F32),) * 4
        for kind, values in enumerate(kinds):
            start = (8 * kind + f) * blocks
            out_ref[start : start + blocks, :] = values


def z_gradient_kernel(
    n, inv_ref, m_ref, g_ref, own_right_ref, own_left_ref, left_ref, right_ref, left_2_ref, right_2_ref, y_ref,
    gradient_ref, out_ref, lines_ref, side_ref, beside_ref, sem,
):
    nz = inv_ref.shape[0]
    ny = g_ref.shape[2]
    y_copy = pltpu.make_async_copy(y_ref, gradient_ref.at[:, 1], sem)
    y_copy.start()
    columns = inv_ref[...].T * m_ref[...]
    index = lax.broadcasted_iota(jnp.int32, (32, nz), 0)
    kind = index // 8
    picked = jnp.where(
        kind == 0,
        columns[0:1],
        jnp.where(kind == 1, columns[1:2], jnp.where(kind == 2, columns[nz - 1 : nz], columns[nz - 2 : nz - 1])),
    )
    wide = jnp.concatenate([jnp.where(index % 8 == f, picked, 0.0) for f in range(6)], axis=1)
    high, low = split(wide)
    side_ref[...] = jnp.concatenate([high, high, low], axis=0)
    blocks = GROUP * ny // LINES
    all_blocks = n * ny // LINES
    z_side(own_right_ref, own_left_ref, left_ref, right_ref, left_2_ref, right_2_ref, beside_ref)

    def step(group, carry):
        sides = []
        for j in range(blocks):
            beside = beside_ref[pl.ds(group * blocks + j, 32, stride=all_blocks), :]
            high, low = split(beside.T)
            sides.append(jnp.concatenate([high, low, high], axis=1))
        for pair in range(GROUP // 2):
            half = blocks // (GROUP // 2)
            lines = jnp.concatenate(sides[pair * half : (pair + 1) * half], axis=0)
            lines_ref[group * (GROUP // 2) + pair] = lines
            for f in range(0, 3):
                added = dot(lines, side_ref[:, f * nz : (f + 1) * nz])
                for u in range(2):
                    p = group * GROUP + 2 * pair + u
                    out_ref[f, p] = added[u * ny : (u + 1) * ny] + g_ref[f, p]
        return carry

    lax.fori_loop(0, n // GROUP, step, 0)
    y_copy.wait()


def z_gradient_join(z_inverse, metric, own, lines, y_gradient):
    _, n, ny, nz = own.shape
    return pl.pallas_call(
        functools.partial(z_gradient_kernel, n),
        in_specs=[WHOLE] * 10,
        out_specs=[ANY, WHOLE, WHOLE, WHOLE],
        out_shape=[
            layer_shape(3, 3, n, ny, nz),
            in_vmem(3, n, ny, nz),
            pltpu.VMEM((n // 2, 2 * ny, 96), BF16),
            pltpu.VMEM((96, 6 * nz), BF16),
        ],
        scratch_shapes=[pltpu.VMEM((32 * (n * ny // LINES), LINES), F32), pltpu.SemaphoreType.DMA],
        input_output_aliases={2: 1},
        compiler_params=params(),
        cost_estimate=cost(own, Z_COST),
        name="z_gradient_join",
    )(z_inverse, metric, own, *lines, y_gradient)


def z_convection_kernel(n, part_ref, lines_ref, side_ref, after_ref, c_ref):
    _, _, ny, nz = part_ref.shape

    def step(group, carry):
        for pair in range(GROUP // 2):
            lines = lines_ref[group * (GROUP // 2) + pair]
            for f in range(3):
                added = dot(lines, side_ref[:, (3 + f) * nz : (4 + f) * nz])
                for u in range(2):
                    p = group * GROUP + 2 * pair + u
                    c_ref[f, p] = added[u * ny : (u + 1) * ny] + part_ref[f, p]
        return carry

    lax.fori_loop(0, n // GROUP, step, 0)


def z_convection_join(partial, lines, side, after):
    _, n, ny, nz = partial.shape
    return pl.pallas_call(
        functools.partial(z_convection_kernel, n),
        in_specs=[WHOLE] * 3 + [ANY],
        out_specs=WHOLE,
        out_shape=in_vmem(3, n, ny, nz),
        input_output_aliases={0: 0},
        compiler_params=params(),
        cost_estimate=cost(partial, Z_COST),
        name="z_convection_join",
    )(partial, lines, side, after)


def on_device(mesh, velocity, metric_x, metric_y, metric_z, x_inverse, y_inverse, z_inverse):
    n = velocity.shape[1]
    blocks = mesh.shape["gx"] * 2
    across = [(i, (i + 1) % blocks) for i in range(1, blocks, 2)]
    across = across + [(j, i) for i, j in across]
    beside = [(0, 1), (1, 0)]
    count = mesh.shape["gz"]

    def shift(by):
        return [(i, (i + by) % count) for i in range(count)]

    own, inner = prepare(velocity)
    near = lax.ppermute(own, ("gx", "gy"), across)
    halo = lax.ppermute(inner, "gy", beside)
    held = pltpu.with_memory_space_constraint(velocity, pltpu.VMEM)
    table, y_inverse, metric_y, z_inverse, metric_z = tables(
        x_inverse, metric_x[None], y_inverse, metric_y[None], z_inverse, metric_z[None], own
    )

    x_sent, x_partial = x_ends(table, held, halo)
    x_received = lax.ppermute(x_sent, ("gx", "gy"), across)

    z_gradient, convection, to_right, to_left, to_far = z_own(z_inverse, metric_z, held, x_sent)
    left_far = lax.ppermute(to_far, "gz", shift(2))
    right_far = left_far if shift(2) == shift(-2) else lax.ppermute(to_far, "gz", shift(-2))
    z_lines = (
        to_right,
        to_left,
        lax.ppermute(to_right, "gz", shift(1)),
        lax.ppermute(to_left, "gz", shift(-1)),
        left_far,
        right_far,
    )

    y_gradient, convection = y_solve(y_inverse, metric_y, held, convection, near)
    gradient, z_gradient, lines, side = z_gradient_join(z_inverse, metric_z, z_gradient, z_lines, y_gradient)
    outer, x_end = x_face(table, x_received, x_sent, x_partial, own, near, z_gradient, n)
    x_other = lax.ppermute(x_end, "gy", beside)

    convection = z_convection_join(convection, lines, side, x_end)
    return tuple(
        x_solve(table, held, near, halo, outer, x_end, x_other, convection, z_gradient, gradient)
    )


def solution(mesh):
    return jax.shard_map(
        functools.partial(on_device, mesh),
        mesh=mesh,
        in_specs=(
            P(None, ("gx", "gy"), None, "gz"),
            P(("gx", "gy")),
            P(),
            P("gz"),
            P(("gx", "gy"), None),
            P(),
            P("gz", None),
        ),
        out_specs=(P(None, None, ("gx", "gy"), None, "gz"), P(None, ("gx", "gy"), None, "gz")),
        check_vma=False,
    )
```

```python
import functools

import jax
import jax.numpy as jnp
from jax import lax
from jax.experimental import pallas as pl
from jax.experimental.pallas import tpu as pltpu
from jax.sharding import PartitionSpec as P

COUPLING = 1.0 / 3.0
NEAR = 7.0 / 9.0
FAR = 1.0 / 36.0
F32 = jnp.float32
BF16 = jnp.bfloat16
SMEM = pltpu.SMEM
VMEM_LIMIT = 20 * 1024 * 1024
GROUP = 8
EARLY = 3
SHORT, LONG = 4, 20_000_000_000


def split(values):
    high = values.astype(BF16)
    low = (values - high.astype(F32)).astype(BF16)
    return high, low


def dot(a, b):
    return lax.dot_general(a, b, (((1,), (0,)), ((), ())), preferred_element_type=F32)


def dot_nt(a, b):
    return lax.dot_general(a, b, (((1,), (1,)), ((), ())), preferred_element_type=F32)


def params():
    return pltpu.CompilerParams(vmem_limit_bytes=VMEM_LIMIT)


def six(velocity, direction):
    return list(velocity) + [velocity[i] * velocity[direction] for i in range(3)]


def times_stencil(inverse):
    rows, length = inverse.shape
    zeros = jnp.zeros((rows, 2), F32)
    wide = jnp.concatenate([zeros, inverse, zeros], axis=1)

    def column(offset):
        return wide[:, 2 + offset : 2 + offset + length]

    return NEAR * (column(-1) - column(1)) + FAR * (column(-2) - column(2))


def in_vmem(*shape):
    return pltpu.VMEM(shape, F32)


ANY = pl.BlockSpec(memory_space=pl.ANY)
WHOLE = pl.BlockSpec(memory_space=pltpu.VMEM)
SCALARS = pl.BlockSpec(memory_space=SMEM)


def cost(flops):
    return pl.CostEstimate(flops=flops, bytes_accessed=1, transcendentals=0)


def layer_shape(*shape):
    return jax.ShapeDtypeStruct(shape, F32)


class Ends:
    def __init__(self, n):
        self.first = lax.axis_index("gy") == 0
        self.n = n
        self.o = jnp.where(self.first, 0, n - 1)
        self.o1 = jnp.where(self.first, 1, n - 2)
        self.q = jnp.where(self.first, n - 1, 0)
        self.q1 = jnp.where(self.first, n - 2, 1)
        self.sign_o = jnp.where(self.first, -1.0, 1.0).astype(F32)
        self.sign_q = -self.sign_o


class Table:
    def __init__(self, n):
        self.source, self.forward, self.backward = 0, n, 2 * n
        self.send, self.last = 3 * n, 4 * n + 2
        self.outer, self.inner = 5 * n + 4, 6 * n + 4
        self.oo, self.oo1, self.qo, self.qo1, self.qq = range(7 * n + 4, 7 * n + 9)
        self.size = 7 * n + 9


def prepare_kernel(n, v_ref, own_ref, halo_ref, sem):
    ends = Ends(n)
    copies = []
    for i in range(3):
        copies.append(pltpu.make_async_copy(v_ref.at[i, ends.o], own_ref.at[i], sem.at[3 * i]))
        for j in range(2):
            plane = jnp.where(ends.first, n - 2 + j, j)
            copies.append(pltpu.make_async_copy(v_ref.at[i, plane], halo_ref.at[i, j], sem.at[3 * i + 1 + j]))
    for copy in copies:
        copy.start()
    for copy in copies:
        copy.wait()


def prepare(velocity):
    _, n, ny, nz = velocity.shape
    return pl.pallas_call(
        functools.partial(prepare_kernel, n),
        in_specs=[ANY],
        out_specs=[WHOLE] * 2,
        out_shape=[layer_shape(3, ny, nz), layer_shape(3, 2, ny, nz)],
        scratch_shapes=[pltpu.SemaphoreType.DMA((9,))],
        compiler_params=params(),
        name="prepare",
    )(pltpu.with_memory_space_constraint(velocity, pltpu.HBM))


def tables_kernel(
    n, xi_ref, mx_ref, yi_ref, my_ref, zi_ref, mz_ref, after_ref,
    table_ref, y_high_ref, y_low_ref, z_main_ref, z_ref, z_metric_ref, x_ref, m_ref, y_ref, y_metric_ref, sem,
):
    ends = Ends(n)
    nz = table_ref.shape[2]
    small = [pltpu.make_async_copy(xi_ref, x_ref, sem.at[0]), pltpu.make_async_copy(mx_ref, m_ref, sem.at[1])]
    copies = [
        pltpu.make_async_copy(zi_ref, z_ref, sem.at[2]),
        pltpu.make_async_copy(mz_ref, z_metric_ref, sem.at[3]),
        pltpu.make_async_copy(yi_ref, y_ref, sem.at[4]),
        pltpu.make_async_copy(my_ref, y_metric_ref, sem.at[5]),
    ]
    for copy in small + copies:
        copy.start()
    for copy in small:
        copy.wait()

    table = Table(n)
    first = ends.first

    def spread(value):
        return jnp.broadcast_to(value, (8, nz))

    def entry(i, j):
        return spread(x_ref[i : i + 1, j : j + 1])

    metric = [spread(m_ref[0:1, k : k + 1]) for k in range(n)]
    above = [entry(i, i + 1) for i in range(n - 1)]
    diagonal = [entry(i, i) for i in range(n)]
    ratio = [-above[i] / diagonal[i + 1] for i in range(n - 1)]
    ratio.append(-entry(n - 1, n - 2) / diagonal[n - 2] * diagonal[n - 1])
    for k in range(n):
        if k == 0:
            source = metric[k]
        elif k == n - 1:
            source = diagonal[k] * metric[k]
        else:
            source = (1.0 + ratio[k] * ratio[k - 1]) * metric[k]
        table_ref[table.source + k] = FAR * source
        table_ref[table.forward + k] = ratio[k] * metric[k] / metric[k - 1] if k > 0 else metric[k]
        table_ref[table.backward + k] = ratio[k] * metric[k] / metric[k + 1] if k < n - 1 else metric[k]

    top = [entry(0, k) for k in range(n)]
    bottom = [entry(n - 1, k) for k in range(n)]
    outer = [jnp.where(first, top[k], bottom[k]) for k in range(n)]
    inner = [jnp.where(first, bottom[k], top[k]) for k in range(n)]
    sign_o, sign_q = ends.sign_o, ends.sign_q
    for base, row, factor in ((table.send, outer, -COUPLING), (table.last, inner, 1.0)):

        def at(k):
            return row[k] if 0 <= k < n else jnp.zeros_like(row[0])

        for k in range(n):
            value = factor * (NEAR * (at(k - 1) - at(k + 1)) + FAR * (at(k - 2) - at(k + 2)))
            if base == table.send:
                if k == 0:
                    value = value + jnp.where(first, NEAR, 0.0)
                elif k == 1:
                    value = value + jnp.where(first, FAR, 0.0)
                elif k == n - 2:
                    value = value - jnp.where(first, 0.0, FAR)
                elif k == n - 1:
                    value = value - jnp.where(first, 0.0, NEAR)
            table_ref[base + k] = value
        at_q = jnp.where(first, row[n - 1], row[0])
        at_q1 = jnp.where(first, row[n - 2], row[1])
        near = factor * sign_q * (NEAR * at_q + FAR * at_q1)
        far = factor * sign_q * FAR * at_q
        table_ref[base + n] = jnp.where(first, near, far)
        table_ref[base + n + 1] = jnp.where(first, far, near)
    for k in range(n):
        left, right = FAR * metric[k] * entry(k, 0), FAR * metric[k] * entry(k, n - 1)
        table_ref[table.outer + k] = jnp.where(first, left, right)
        table_ref[table.inner + k] = jnp.where(first, right, left)
    table_ref[table.oo] = jnp.where(first, outer[0], outer[n - 1])
    table_ref[table.oo1] = jnp.where(first, outer[1], outer[n - 2])
    table_ref[table.qo] = jnp.where(first, inner[0], inner[n - 1])
    table_ref[table.qo1] = jnp.where(first, inner[1], inner[n - 2])
    table_ref[table.qq] = jnp.where(first, inner[n - 1], inner[0])
    for copy in copies:
        copy.wait()
    ny = y_ref.shape[0]
    row = lax.broadcasted_iota(jnp.int32, (ny, ny), 0)
    column = lax.broadcasted_iota(jnp.int32, (ny, ny), 1)
    y_metric = jnp.sum(jnp.where(row == column, y_metric_ref[...], 0.0), axis=1, keepdims=True)
    y_high_ref[...], y_low_ref[...] = split(times_stencil(y_ref[...]) * y_metric)
    high, low = split(times_stencil(z_ref[...]).T * z_metric_ref[...])
    both = jnp.concatenate([high, low], axis=1)
    z_main_ref[...] = jnp.concatenate([both, both], axis=0)


def tables(x_inverse, metric_x, y_inverse, metric_y, z_inverse, metric_z, after):
    n, ny, nz = x_inverse.shape[0], y_inverse.shape[0], z_inverse.shape[0]
    inputs = (x_inverse, metric_x, y_inverse, metric_y, z_inverse, metric_z)
    return pl.pallas_call(
        functools.partial(tables_kernel, n),
        in_specs=[ANY] * 7,
        out_specs=[WHOLE] * 6,
        out_shape=[
            in_vmem(Table(n).size, 8, nz),
            pltpu.VMEM((ny, ny), BF16),
            pltpu.VMEM((ny, ny), BF16),
            pltpu.VMEM((2 * nz, 2 * nz), BF16),
            in_vmem(nz, nz),
            in_vmem(1, nz),
        ],
        scratch_shapes=[
            pltpu.VMEM((n, n), F32),
            pltpu.VMEM((1, n), F32),
            pltpu.VMEM((ny, ny), F32),
            pltpu.VMEM((1, ny), F32),
            pltpu.SemaphoreType.DMA((6,)),
        ],
        compiler_params=params(),
        cost_estimate=cost(LONG),
        name="tables",
    )(*(pltpu.with_memory_space_constraint(value, pltpu.HBM) for value in inputs), after)


def x_ends_kernel(n, ny, table_ref, v_ref, halo_ref, w_ref, l_ref):
    table = Table(n)

    def tile(index, carry):
        start = pl.multiple_of(index * 8, 8)
        rows = pl.ds(start, 8)
        w = [None] * 6
        l = [None] * 6
        for k in range(n + 2):
            if k < n:
                fields = six([v_ref[i, k, rows, :] for i in range(3)], 0)
            else:
                fields = six([halo_ref[i, k - n, rows, :] for i in range(3)], 0)
            a, b = table_ref[table.send + k], table_ref[table.last + k]
            for f in range(6):
                w[f] = a * fields[f] if k == 0 else w[f] + a * fields[f]
                l[f] = b * fields[f] if k == 0 else l[f] + b * fields[f]
        for f in range(6):
            w_ref[pl.ds(f * ny + start, 8), :] = w[f]
            l_ref[f, rows, :] = l[f]
        return carry

    lax.fori_loop(0, ny // 8, tile, 0)
    index = lax.broadcasted_iota(jnp.int32, (8, w_ref.shape[1]), 0)
    w_ref[6 * ny : 6 * ny + 8, :] = jnp.where(index == 0, table_ref[table.oo], table_ref[table.oo1])


def x_ends(table, velocity, halo):
    _, n, ny, nz = velocity.shape
    return pl.pallas_call(
        functools.partial(x_ends_kernel, n, ny),
        in_specs=[WHOLE] * 3,
        out_specs=[WHOLE, WHOLE],
        out_shape=[layer_shape(6 * ny + 8, nz), layer_shape(6, ny, nz)],
        compiler_params=params(),
        cost_estimate=cost(SHORT),
        name="x_ends",
    )(table, velocity, halo)


def x_face_kernel(n, ny, table_ref, wr_ref, ws_ref, l_ref, own_ref, near_ref, after_ref, w_ref, e_ref):
    ends = Ends(n)
    table = Table(n)
    shape = (8, wr_ref.shape[1])
    p_oo = jnp.broadcast_to(wr_ref[6 * ny : 6 * ny + 1, :], shape)
    p_oo1 = jnp.broadcast_to(wr_ref[6 * ny + 1 : 6 * ny + 2, :], shape)
    x_qo = table_ref[table.qo]
    inverse_den = 1.0 / (1.0 - COUPLING * COUPLING * table_ref[table.oo] * p_oo)
    sent_weight = COUPLING * p_oo
    own_weight = COUPLING * FAR * ends.sign_o * p_oo1
    near_weight = COUPLING * FAR * ends.sign_o * COUPLING * table_ref[table.oo1] * p_oo
    end_weight = ends.sign_o * FAR * table_ref[table.qo1]

    def tile(index, carry):
        start = pl.multiple_of(index * 8, 8)
        rows = pl.ds(start, 8)
        own = six([own_ref[i, rows, :] for i in range(3)], 0)
        near = six([near_ref[i, rows, :] for i in range(3)], 0)
        for f in range(6):
            field = pl.ds(f * ny + start, 8)
            w = wr_ref[field, :] - sent_weight * ws_ref[field, :]
            w = (w + own_weight * own[f] + near_weight * near[f]) * inverse_den
            w_ref[f, rows, :] = 36.0 * w
            e_ref[field, :] = l_ref[f, rows, :] + x_qo * w + end_weight * near[f]
        return carry

    lax.fori_loop(0, ny // 8, tile, 0)
    e_ref[6 * ny : 6 * ny + 8, :] = table_ref[table.qq]


def x_face(table, received, sent, partial, own, near, after, n):
    _, ny, nz = own.shape
    return pl.pallas_call(
        functools.partial(x_face_kernel, n, ny),
        in_specs=[WHOLE] * 6 + [ANY],
        out_specs=[WHOLE, WHOLE],
        out_shape=[layer_shape(6, ny, nz), layer_shape(6 * ny + 8, nz)],
        compiler_params=params(),
        cost_estimate=cost(SHORT),
        name="x_face",
    )(table, received, sent, partial, own, near, after)


def x_sweeps(n, table, table_ref, line, at_first, at_second, at_last_but_one, at_last):
    forward = []
    for k in range(n):
        if k == 0:
            source = 28.0 * line[1] + (line[2] + at_first)
        elif k == 1:
            source = 28.0 * (line[2] - line[0]) + (line[3] + at_second)
        elif k == n - 1:
            source = (at_last - line[n - 3]) - 28.0 * line[n - 2]
        elif k == n - 2:
            source = 28.0 * (line[n - 1] - line[n - 3]) + (at_last_but_one - line[n - 4])
        else:
            source = 28.0 * (line[k + 1] - line[k - 1]) + (line[k + 2] - line[k - 2])
        value = table_ref[table.source + k] * source
        if k > 0:
            value = value - table_ref[table.forward + k] * forward[k - 1]
        forward.append(value)
    solved = [None] * (n - 1) + [forward[n - 1]]
    for k in reversed(range(n - 1)):
        solved[k] = forward[k] - table_ref[table.backward + k] * solved[k + 1]
    return solved


def each_side(run):
    first = lax.axis_index("gy") == 0
    pl.when(first)(functools.partial(run, True))
    pl.when(jnp.logical_not(first))(functools.partial(run, False))


def x_gradient_kernel(n, ny, table_ref, v_ref, near_ref, halo_ref, y_ref, gradient_ref, g_ref, sem):
    table = Table(n)
    y_copy = pltpu.make_async_copy(y_ref, gradient_ref.at[:, 1], sem)
    y_copy.start()

    def run(first):
        sign = -1.0 if first else 1.0
        near_j, far_j = (0, 1) if first else (1, 0)

        def tile(index, carry):
            rows = pl.ds(pl.multiple_of(index * 8, 8), 8)
            for f in range(3):
                line = [v_ref[f, k, rows, :] for k in range(n)]
                inner_near = -sign * halo_ref[f, near_j, rows, :]
                inner = 28.0 * inner_near - sign * halo_ref[f, far_j, rows, :]
                near = sign * near_ref[f, rows, :]
                zero = jnp.zeros_like(near)
                ends = (zero, near, inner_near, inner) if first else (inner, inner_near, near, zero)
                for k, value in enumerate(x_sweeps(n, table, table_ref, line, *ends)):
                    g_ref[f, k, rows, :] = value
            return carry

        lax.fori_loop(0, ny // 8, tile, 0)

    each_side(run)
    y_copy.wait()


def x_gradient_own(table, velocity, near, halo, y_gradient):
    _, n, ny, nz = velocity.shape
    return pl.pallas_call(
        functools.partial(x_gradient_kernel, n, ny),
        in_specs=[WHOLE] * 5,
        out_specs=[ANY, WHOLE],
        out_shape=[layer_shape(3, 3, n, ny, nz), in_vmem(3, n, ny, nz)],
        scratch_shapes=[pltpu.SemaphoreType.DMA],
        compiler_params=params(),
        cost_estimate=cost(SHORT),
        name="x_gradient_own",
    )(table, velocity, near, halo, y_gradient)


def x_solve_kernel(
    n, ny, table_ref, v_ref, near_ref, halo_ref, w_ref, e_ref, r_ref, own_ref, part_ref, lines_ref, side_ref, z_ref, held_ref,
    gradient_ref, convection_ref, g_ref, c_ref, beside_ref, sem,
):
    table = Table(n)
    nz = v_ref.shape[3]
    parts = sem.shape[1]
    share = ny // parts
    z_copy = pltpu.make_async_copy(z_ref, gradient_ref.at[:, 2], sem.at[2, 0])
    z_copy.start()
    p_qq = r_ref[6 * ny : 6 * ny + 8, :]
    weight = COUPLING * p_qq
    scale = -36.0 * COUPLING / (1.0 - COUPLING * COUPLING * table_ref[table.qq] * p_qq)

    def copies(part):
        rows = pl.ds(pl.multiple_of(part * share, 8), share)
        return (
            pltpu.make_async_copy(g_ref.at[:, :, rows], gradient_ref.at[:, 0, :, rows], sem.at[0, part]),
            pltpu.make_async_copy(c_ref.at[:, :, rows], convection_ref.at[:, :, rows], sem.at[1, part]),
        )

    def run(first):
        sign = -1.0 if first else 1.0
        near_j, far_j = (0, 1) if first else (1, 0)

        def step(part, carry):
            base = pl.multiple_of(part * share, 16)
            lines = lines_ref[:, pl.ds(base, share), :].reshape(n * share, lines_ref.shape[2])
            beside_ref[...] = dot(lines, side_ref[:, 3 * nz :])
            for offset in range(0, share, 8):
                start = base + offset
                rows = pl.ds(start, 8)
                near = six([near_ref[i, rows, :] for i in range(3)], 0)
                inner_near = six([halo_ref[i, near_j, rows, :] for i in range(3)], 0)
                inner_far = six([halo_ref[i, far_j, rows, :] for i in range(3)], 0)
                for f in range(6):
                    field = pl.ds(f * ny + start, 8)
                    outer = w_ref[f, rows, :]
                    inner = scale * (r_ref[field, :] - weight * e_ref[field, :])
                    if f < 3:
                        for k in range(n):
                            g_ref[f, k, rows, :] = (
                                own_ref[f, k, rows, :]
                                + table_ref[table.outer + k] * outer
                                + table_ref[table.inner + k] * inner
                            )
                        continue
                    line = [v_ref[f - 3, k, rows, :] * v_ref[0, k, rows, :] for k in range(n)]
                    inner = inner - sign * (28.0 * inner_near[f] + inner_far[f])
                    ends = (outer, sign * near[f], -sign * inner_near[f], inner)
                    ends = ends if first else ends[::-1]
                    for k, value in enumerate(x_sweeps(n, table, table_ref, line, *ends)):
                        row = k * share + offset
                        beside = beside_ref[row : row + 8, (f - 3) * nz : (f - 2) * nz]
                        c_ref[f - 3, k, rows, :] = value + (part_ref[f - 3, k, rows, :] + beside)
            for copy in copies(part):
                copy.start()
            return carry

        lax.fori_loop(0, parts, step, 0)

    each_side(run)

    def drain(part, carry):
        for copy in copies(part):
            copy.wait()
        return carry

    z_copy.wait()
    lax.fori_loop(0, parts, drain, 0)


def x_solve(table, velocity, near, halo, outer, ends, received, own, partial, lines, side, z_gradient, gradient, share=16):
    _, n, ny, nz = velocity.shape
    return pl.pallas_call(
        functools.partial(x_solve_kernel, n, ny),
        in_specs=[WHOLE] * 12 + [ANY],
        out_specs=[ANY, ANY],
        out_shape=[layer_shape(*gradient.shape), layer_shape(3, n, ny, nz)],
        scratch_shapes=[
            pltpu.VMEM((3, n, ny, nz), F32),
            pltpu.VMEM((3, n, ny, nz), F32),
            pltpu.VMEM((n * share, 3 * nz), F32),
            pltpu.SemaphoreType.DMA((3, ny // share)),
        ],
        input_output_aliases={12: 0},
        compiler_params=params(),
        cost_estimate=cost(SHORT),
        name="x_solve",
    )(table, velocity, near, halo, outer, ends, received, own, partial, lines, side, z_gradient, gradient)


def y_plane(velocities, high_ref, low_ref):
    fields = six(velocities, 1)
    nz = fields[0].shape[1]
    values = []
    for a in (0, 2, 4):
        high, low = split(jnp.concatenate(fields[a : a + 2], axis=1))
        result = dot(high_ref[...], high) + dot(low_ref[...], high) + dot(high_ref[...], low)
        values = values + [result[:, :nz], result[:, nz:]]
    return values


def y_kernel(n, high_ref, low_ref, v_ref, held_ref, part_ref, after_ref, g_ref, c_ref):
    def step(group, carry):
        for u in range(EARLY, GROUP):
            p = group * GROUP + u
            values = y_plane([v_ref[i, p] for i in range(3)], high_ref, low_ref)
            for f in range(3):
                g_ref[f, p] = values[f]
                c_ref[f, p] = values[3 + f] + part_ref[f, p]
        return carry

    lax.fori_loop(0, n // GROUP, step, 0)


def y_solve(high, low, velocity, early, partial, after):
    _, n, ny, nz = velocity.shape
    return pl.pallas_call(
        functools.partial(y_kernel, n),
        in_specs=[WHOLE] * 5 + [ANY],
        out_specs=[WHOLE, WHOLE],
        out_shape=[in_vmem(3, n, ny, nz), in_vmem(3, n, ny, nz)],
        input_output_aliases={3: 0, 4: 1},
        compiler_params=params(),
        cost_estimate=cost(LONG),
        name="y_solve",
    )(high, low, velocity, early, partial, after)


LINES = 128
PACK = 4


def z_own_kernel(
    n, inv_ref, m_ref, main_ref, high_ref, low_ref, v_ref, after_ref,
    g_ref, c_ref, y_ref, right_ref, left_ref, far_ref, turned_ref,
):
    nz = inv_ref.shape[0]
    ny = v_ref.shape[2]
    first_scale = 1.0 / m_ref[0:1, 0:1]
    last_scale = 1.0 / m_ref[0:1, nz - 1 : nz]
    lane = lax.broadcasted_iota(jnp.int32, (ny, nz), 1)

    m = nz - 1
    index = lax.broadcasted_iota(jnp.int32, right_ref.shape[1:], 0)
    for ref, corners in ((right_ref, ((m, m), (m, m - 1), (m, 0), (m, 1))), (left_ref, ((0, 0), (0, 1), (0, m), (0, m - 1)))):
        row = jnp.zeros(right_ref.shape[1:], F32)
        for position, (i, j) in enumerate(corners):
            row = jnp.where(index == position, inv_ref[i : i + 1, j : j + 1], row)
        ref[12] = row

    def segments(u):
        start = u * ny
        while start < (u + 1) * ny:
            stop = min((start // LINES + 1) * LINES, (u + 1) * ny)
            yield start // LINES, start - u * ny, stop - u * ny
            start = stop

    def step(group, carry):
        pieces = [[] for _ in range(GROUP * ny // LINES)]
        for u in range(GROUP):
            p = group * GROUP + u
            velocities = [v_ref[i, p] for i in range(3)]
            values = []
            y_values = [None] * 6
            if u < EARLY:
                y_values = y_plane(velocities, high_ref, low_ref)
                for f in range(3):
                    y_ref[f, p] = y_values[f]
            for f, field in enumerate(six(velocities, 2)):
                high, low = split(field)
                both = dot(jnp.concatenate([high, low], axis=1), main_ref[...])
                value = both[:, :nz] + both[:, nz:]
                if f < 3:
                    g_ref[f, p] = value
                else:
                    c_ref[f - 3, p] = value if u >= EARLY else value + y_values[f]
                values.append(value)
            for block, start, stop in segments(u):
                base = block % PACK * 32
                columns = pltpu.roll(values[0][start:stop], base + 1, axis=1)
                for f in range(1, 6):
                    moved = pltpu.roll(values[f][start:stop], (base + 1 + 2 * f) % nz, axis=1)
                    columns = jnp.where(lane[start:stop] // 2 == base // 2 + f, moved, columns)
                for i in range(3):
                    moved = pltpu.roll(velocities[i][start:stop], (base + 14 + 4 * i) % nz, axis=1)
                    columns = jnp.where(lane[start:stop] // 4 == base // 4 + 3 + i, moved, columns)
                pieces[block].append(columns)
        for j, parts in enumerate(pieces):
            if j % PACK == 0:
                packed = jnp.concatenate(parts, axis=0)
                for other in range(1, PACK):
                    columns = jnp.concatenate(pieces[j + other], axis=0)
                    packed = jnp.where(lane[0:LINES] // 32 == other, columns, packed)
                turned_ref[j // PACK] = packed.T
                blocks = pl.ds(group * len(pieces) + j, PACK)

                def rows(position):
                    return turned_ref[j // PACK, pl.ds(position, PACK, stride=32), :]

                for f in range(6):
                    right_ref[f, blocks, :] = rows(2 * f) * last_scale
                    left_ref[f, blocks, :] = rows(2 * f + 1) * first_scale
                for column in range(4):
                    for i in range(3):
                        values = rows(12 + 4 * i + column)
                        ref = right_ref if column < 2 else left_ref
                        ref[6 + 3 * (column % 2) + i, blocks, :] = values
                        far_ref[3 * column + i, blocks, :] = values
        return carry

    lax.fori_loop(0, n // GROUP, step, 0)


def z_own(z_inverse, metric, main, high, low, velocity, after):
    _, n, ny, nz = velocity.shape
    return pl.pallas_call(
        functools.partial(z_own_kernel, n),
        in_specs=[WHOLE] * 6 + [ANY],
        out_specs=[WHOLE] * 6,
        out_shape=[in_vmem(3, n, ny, nz)] * 3 + [layer_shape(13, n * ny // LINES, LINES)] * 2
        + [layer_shape(12, n * ny // LINES, LINES)],
        scratch_shapes=[pltpu.VMEM((GROUP * ny // LINES // PACK, LINES, LINES), F32)],
        compiler_params=params(),
        cost_estimate=cost(SHORT),
        name="z_own",
    )(z_inverse, metric, main, high, low, velocity, after)


def z_side(own_right, own_left, left, right, left_2, right_2, out_ref):
    blocks = own_left.shape[1]
    shape = own_left.shape[1:]

    def pair(ref, start):
        return six([ref[start + i] for i in range(3)], 2), six([ref[start + 3 + i] for i in range(3)], 2)

    def from_left(ref, start):
        far, near = pair(ref, start)
        return [(-NEAR * near[f] - FAR * far[f], -FAR * near[f]) for f in range(6)]

    def from_right(ref, start):
        near, far = pair(ref, start)
        return [(NEAR * near[f] + FAR * far[f], FAR * near[f]) for f in range(6)]

    def entries(ref):
        return [jnp.broadcast_to(ref[12, i : i + 1], shape) for i in range(4)]

    def first_value(ref, corners, f, at_left, at_right):
        x_00, x_01, x_0m, x_0l = corners
        return ref[f] + x_00 * at_left[f][0] + x_01 * at_left[f][1] + x_0m * at_right[f][0] + x_0l * at_right[f][1]

    def last_value(ref, corners, f, at_left, at_right):
        x_mm, x_ml, x_m0, x_m1 = corners
        return ref[f] + x_m0 * at_left[f][0] + x_m1 * at_left[f][1] + x_mm * at_right[f][0] + x_ml * at_right[f][1]

    own_first_row, own_last_row, left_row, right_row = (entries(ref) for ref in (own_left, own_right, left, right))
    at_left, at_right = from_left(left, 6), from_right(right, 6)
    left_at_left, left_at_right = from_left(left_2, 0), from_right(own_left, 6)
    right_at_left, right_at_right = from_left(own_right, 6), from_right(right_2, 6)
    left_den = 1.0 / (1.0 - COUPLING * COUPLING * left_row[0] * own_first_row[0])
    right_den = 1.0 / (1.0 - COUPLING * COUPLING * right_row[0] * own_last_row[0])
    for f in range(8):
        if f < 6:
            own_first = first_value(own_left, own_first_row, f, at_left, at_right)
            own_last = last_value(own_right, own_last_row, f, at_left, at_right)
            left_value = last_value(left, left_row, f, left_at_left, left_at_right)
            right_value = first_value(right, right_row, f, right_at_left, right_at_right)
            left_final = (left_value - COUPLING * left_row[0] * own_first) * left_den
            right_start = (right_value - COUPLING * right_row[0] * own_last) * right_den
            kinds = (
                at_left[f][0] - COUPLING * left_final,
                at_left[f][1],
                at_right[f][0] - COUPLING * right_start,
                at_right[f][1],
            )
        else:
            kinds = (jnp.zeros(shape, F32),) * 4
        for kind, values in enumerate(kinds):
            start = (8 * kind + f) * blocks
            out_ref[start : start + blocks, :] = values


def z_gradient_kernel(
    n, inv_ref, m_ref, g_ref, own_right_ref, own_left_ref, left_ref, right_ref, left_2_ref, right_2_ref,
    after_ref, out_ref, lines_ref, side_ref, beside_ref,
):
    nz = inv_ref.shape[0]
    ny = g_ref.shape[2]
    columns = inv_ref[...].T * m_ref[...]
    index = lax.broadcasted_iota(jnp.int32, (32, nz), 0)
    kind = index // 8
    picked = jnp.where(
        kind == 0,
        columns[0:1],
        jnp.where(kind == 1, columns[1:2], jnp.where(kind == 2, columns[nz - 1 : nz], columns[nz - 2 : nz - 1])),
    )
    wide = jnp.concatenate([jnp.where(index % 8 == f, picked, 0.0) for f in range(6)], axis=1)
    high, low = split(wide)
    side_ref[...] = jnp.concatenate([high, high, low], axis=0)
    planes = GROUP
    blocks = planes * ny // LINES
    all_blocks = n * ny // LINES
    z_side(own_right_ref, own_left_ref, left_ref, right_ref, left_2_ref, right_2_ref, beside_ref)

    def step(group, carry):
        sides = []
        for j in range(blocks):
            beside = beside_ref[pl.ds(group * blocks + j, 32, stride=all_blocks), :]
            high, low = split(beside.T)
            sides.append(jnp.concatenate([high, low, high], axis=1))
        for pair in range(planes // 2):
            half = blocks // (planes // 2)
            lines = jnp.concatenate(sides[pair * half : (pair + 1) * half], axis=0)
            for u in range(2):
                lines_ref[group * planes + 2 * pair + u] = lines[u * ny : (u + 1) * ny]
            for f in range(0, 3):
                added = dot(lines, side_ref[:, f * nz : (f + 1) * nz])
                for u in range(2):
                    p = group * planes + 2 * pair + u
                    out_ref[f, p] = added[u * ny : (u + 1) * ny] + g_ref[f, p]
        return carry

    lax.fori_loop(0, n // planes, step, 0)


def z_gradient_join(z_inverse, metric, own, lines, after):
    _, n, ny, nz = own.shape
    return pl.pallas_call(
        functools.partial(z_gradient_kernel, n),
        in_specs=[WHOLE] * 9 + [ANY],
        out_specs=[WHOLE, WHOLE, WHOLE],
        out_shape=[
            in_vmem(3, n, ny, nz),
            pltpu.VMEM((n, ny, 96), BF16),
            pltpu.VMEM((96, 6 * nz), BF16),
        ],
        scratch_shapes=[pltpu.VMEM((32 * (n * ny // LINES), LINES), F32)],
        input_output_aliases={2: 0},
        compiler_params=params(),
        cost_estimate=cost(LONG),
        name="z_gradient_join",
    )(z_inverse, metric, own, *lines, after)


def on_device(mesh, velocity, metric_x, metric_y, metric_z, x_inverse, y_inverse, z_inverse):
    n = velocity.shape[1]
    blocks = mesh.shape["gx"] * 2
    across = [(i, (i + 1) % blocks) for i in range(1, blocks, 2)]
    across = across + [(j, i) for i, j in across]
    beside = [(0, 1), (1, 0)]
    count = mesh.shape["gz"]

    def shift(by):
        return [(i, (i + by) % count) for i in range(count)]

    own, inner = prepare(velocity)
    near = lax.ppermute(own, ("gx", "gy"), across)
    halo = lax.ppermute(inner, "gy", beside)
    held = pltpu.with_memory_space_constraint(velocity, pltpu.VMEM)
    table, y_high, y_low, z_main, z_inverse, metric_z = tables(
        x_inverse, metric_x[None], y_inverse, metric_y[None], z_inverse, metric_z[None], own
    )

    x_sent, x_partial = x_ends(table, held, halo)
    x_received = lax.ppermute(x_sent, ("gx", "gy"), across)

    z_gradient, convection, y_gradient, to_right, to_left, to_far = z_own(
        z_inverse, metric_z, z_main, y_high, y_low, held, x_sent
    )
    left_far = lax.ppermute(to_far, "gz", shift(2))
    right_far = left_far if shift(2) == shift(-2) else lax.ppermute(to_far, "gz", shift(-2))
    z_lines = (
        to_right,
        to_left,
        lax.ppermute(to_right, "gz", shift(1)),
        lax.ppermute(to_left, "gz", shift(-1)),
        left_far,
        right_far,
    )

    y_gradient, convection = y_solve(y_high, y_low, held, y_gradient, convection, near)
    gradient, x_gradient = x_gradient_own(table, held, near, halo, y_gradient)
    outer, x_end = x_face(table, x_received, x_sent, x_partial, own, near, x_gradient, n)
    x_other = lax.ppermute(x_end, "gy", beside)
    z_gradient, lines, side = z_gradient_join(z_inverse, metric_z, z_gradient, z_lines, x_end)
    return tuple(
        x_solve(
            table, held, near, halo, outer, x_end, x_other, x_gradient, convection, lines, side, z_gradient, gradient
        )
    )


def solution(mesh):
    return jax.shard_map(
        functools.partial(on_device, mesh),
        mesh=mesh,
        in_specs=(
            P(None, ("gx", "gy"), None, "gz"),
            P(("gx", "gy")),
            P(),
            P("gz"),
            P(("gx", "gy"), None),
            P(),
            P("gz", None),
        ),
        out_specs=(P(None, None, ("gx", "gy"), None, "gz"), P(None, ("gx", "gy"), None, "gz")),
        check_vma=False,
    )
```

```python
import functools

import jax
import jax.numpy as jnp
from jax import lax
from jax.experimental import pallas as pl
from jax.experimental.pallas import tpu as pltpu
from jax.sharding import PartitionSpec as P

COUPLING = 1.0 / 3.0
NEAR = 7.0 / 9.0
FAR = 1.0 / 36.0
F32 = jnp.float32
BF16 = jnp.bfloat16
SMEM = pltpu.SMEM
VMEM_LIMIT = 20 * 1024 * 1024
GROUP = 8
EARLY = 4
SHORT, LONG = 4, 20_000_000_000


def split(values):
    high = values.astype(BF16)
    low = (values - high.astype(F32)).astype(BF16)
    return high, low


def dot(a, b):
    return lax.dot_general(a, b, (((1,), (0,)), ((), ())), preferred_element_type=F32)


def dot_nt(a, b):
    return lax.dot_general(a, b, (((1,), (1,)), ((), ())), preferred_element_type=F32)


def params():
    return pltpu.CompilerParams(vmem_limit_bytes=VMEM_LIMIT)


def six(velocity, direction):
    return list(velocity) + [velocity[i] * velocity[direction] for i in range(3)]


def times_stencil(inverse):
    rows, length = inverse.shape
    zeros = jnp.zeros((rows, 2), F32)
    wide = jnp.concatenate([zeros, inverse, zeros], axis=1)

    def column(offset):
        return wide[:, 2 + offset : 2 + offset + length]

    return NEAR * (column(-1) - column(1)) + FAR * (column(-2) - column(2))


def in_vmem(*shape):
    return pltpu.VMEM(shape, F32)


ANY = pl.BlockSpec(memory_space=pl.ANY)
WHOLE = pl.BlockSpec(memory_space=pltpu.VMEM)
SCALARS = pl.BlockSpec(memory_space=SMEM)


def cost(flops):
    return pl.CostEstimate(flops=flops, bytes_accessed=1, transcendentals=0)


def layer_shape(*shape):
    return jax.ShapeDtypeStruct(shape, F32)


class Ends:
    def __init__(self, n):
        self.first = lax.axis_index("gy") == 0
        self.n = n
        self.o = jnp.where(self.first, 0, n - 1)
        self.o1 = jnp.where(self.first, 1, n - 2)
        self.q = jnp.where(self.first, n - 1, 0)
        self.q1 = jnp.where(self.first, n - 2, 1)
        self.sign_o = jnp.where(self.first, -1.0, 1.0).astype(F32)
        self.sign_q = -self.sign_o


class Table:
    def __init__(self, n):
        self.source, self.forward, self.backward = 0, n, 2 * n
        self.send, self.last = 3 * n, 4 * n + 2
        self.outer, self.inner = 5 * n + 4, 6 * n + 4
        self.oo, self.oo1, self.qo, self.qo1, self.qq = range(7 * n + 4, 7 * n + 9)
        self.size = 7 * n + 9


def prepare_kernel(n, v_ref, own_ref, halo_ref, sem):
    ends = Ends(n)
    copies = []
    for i in range(3):
        copies.append(pltpu.make_async_copy(v_ref.at[i, ends.o], own_ref.at[i], sem.at[3 * i]))
        for j in range(2):
            plane = jnp.where(ends.first, n - 2 + j, j)
            copies.append(pltpu.make_async_copy(v_ref.at[i, plane], halo_ref.at[i, j], sem.at[3 * i + 1 + j]))
    for copy in copies:
        copy.start()
    for copy in copies:
        copy.wait()


def prepare(velocity):
    _, n, ny, nz = velocity.shape
    return pl.pallas_call(
        functools.partial(prepare_kernel, n),
        in_specs=[ANY],
        out_specs=[WHOLE] * 2,
        out_shape=[layer_shape(3, ny, nz), layer_shape(3, 2, ny, nz)],
        scratch_shapes=[pltpu.SemaphoreType.DMA((9,))],
        compiler_params=params(),
        name="prepare",
    )(pltpu.with_memory_space_constraint(velocity, pltpu.HBM))


def tables_kernel(
    n, xi_ref, mx_ref, yi_ref, my_ref, zi_ref, mz_ref, after_ref,
    table_ref, y_ref, y_metric_ref, z_ref, z_metric_ref, x_ref, m_ref, sem,
):
    ends = Ends(n)
    nz = table_ref.shape[2]
    small = [pltpu.make_async_copy(xi_ref, x_ref, sem.at[0]), pltpu.make_async_copy(mx_ref, m_ref, sem.at[1])]
    copies = [
        pltpu.make_async_copy(zi_ref, z_ref, sem.at[2]),
        pltpu.make_async_copy(mz_ref, z_metric_ref, sem.at[3]),
        pltpu.make_async_copy(yi_ref, y_ref, sem.at[4]),
        pltpu.make_async_copy(my_ref, y_metric_ref, sem.at[5]),
    ]
    for copy in small + copies:
        copy.start()
    for copy in small:
        copy.wait()

    table = Table(n)
    first = ends.first

    def spread(value):
        return jnp.broadcast_to(value, (8, nz))

    def entry(i, j):
        return spread(x_ref[i : i + 1, j : j + 1])

    metric = [spread(m_ref[0:1, k : k + 1]) for k in range(n)]
    above = [entry(i, i + 1) for i in range(n - 1)]
    diagonal = [entry(i, i) for i in range(n)]
    ratio = [-above[i] / diagonal[i + 1] for i in range(n - 1)]
    ratio.append(-entry(n - 1, n - 2) / diagonal[n - 2] * diagonal[n - 1])
    for k in range(n):
        if k == 0:
            source = metric[k]
        elif k == n - 1:
            source = diagonal[k] * metric[k]
        else:
            source = (1.0 + ratio[k] * ratio[k - 1]) * metric[k]
        table_ref[table.source + k] = FAR * source
        table_ref[table.forward + k] = ratio[k] * metric[k] / metric[k - 1] if k > 0 else metric[k]
        table_ref[table.backward + k] = ratio[k] * metric[k] / metric[k + 1] if k < n - 1 else metric[k]

    top = [entry(0, k) for k in range(n)]
    bottom = [entry(n - 1, k) for k in range(n)]
    outer = [jnp.where(first, top[k], bottom[k]) for k in range(n)]
    inner = [jnp.where(first, bottom[k], top[k]) for k in range(n)]
    sign_o, sign_q = ends.sign_o, ends.sign_q
    for base, row, factor in ((table.send, outer, -COUPLING), (table.last, inner, 1.0)):

        def at(k):
            return row[k] if 0 <= k < n else jnp.zeros_like(row[0])

        for k in range(n):
            value = factor * (NEAR * (at(k - 1) - at(k + 1)) + FAR * (at(k - 2) - at(k + 2)))
            if base == table.send:
                if k == 0:
                    value = value + jnp.where(first, NEAR, 0.0)
                elif k == 1:
                    value = value + jnp.where(first, FAR, 0.0)
                elif k == n - 2:
                    value = value - jnp.where(first, 0.0, FAR)
                elif k == n - 1:
                    value = value - jnp.where(first, 0.0, NEAR)
            table_ref[base + k] = value
        at_q = jnp.where(first, row[n - 1], row[0])
        at_q1 = jnp.where(first, row[n - 2], row[1])
        near = factor * sign_q * (NEAR * at_q + FAR * at_q1)
        far = factor * sign_q * FAR * at_q
        table_ref[base + n] = jnp.where(first, near, far)
        table_ref[base + n + 1] = jnp.where(first, far, near)
    for k in range(n):
        left, right = FAR * metric[k] * entry(k, 0), FAR * metric[k] * entry(k, n - 1)
        table_ref[table.outer + k] = jnp.where(first, left, right)
        table_ref[table.inner + k] = jnp.where(first, right, left)
    table_ref[table.oo] = jnp.where(first, outer[0], outer[n - 1])
    table_ref[table.oo1] = jnp.where(first, outer[1], outer[n - 2])
    table_ref[table.qo] = jnp.where(first, inner[0], inner[n - 1])
    table_ref[table.qo1] = jnp.where(first, inner[1], inner[n - 2])
    table_ref[table.qq] = jnp.where(first, inner[n - 1], inner[0])
    for copy in copies:
        copy.wait()


def tables(x_inverse, metric_x, y_inverse, metric_y, z_inverse, metric_z, after):
    n, ny, nz = x_inverse.shape[0], y_inverse.shape[0], z_inverse.shape[0]
    inputs = (x_inverse, metric_x, y_inverse, metric_y, z_inverse, metric_z)
    return pl.pallas_call(
        functools.partial(tables_kernel, n),
        in_specs=[ANY] * 7,
        out_specs=[WHOLE] * 5,
        out_shape=[
            in_vmem(Table(n).size, 8, nz),
            in_vmem(ny, ny),
            in_vmem(1, ny),
            in_vmem(nz, nz),
            in_vmem(1, nz),
        ],
        scratch_shapes=[pltpu.VMEM((n, n), F32), pltpu.VMEM((1, n), F32), pltpu.SemaphoreType.DMA((6,))],
        compiler_params=params(),
        cost_estimate=cost(LONG),
        name="tables",
    )(*(pltpu.with_memory_space_constraint(value, pltpu.HBM) for value in inputs), after)


def x_ends_kernel(n, ny, table_ref, v_ref, halo_ref, w_ref, l_ref):
    table = Table(n)

    def tile(index, carry):
        start = pl.multiple_of(index * 8, 8)
        rows = pl.ds(start, 8)
        w = [None] * 6
        l = [None] * 6
        for k in range(n + 2):
            if k < n:
                fields = six([v_ref[i, k, rows, :] for i in range(3)], 0)
            else:
                fields = six([halo_ref[i, k - n, rows, :] for i in range(3)], 0)
            a, b = table_ref[table.send + k], table_ref[table.last + k]
            for f in range(6):
                w[f] = a * fields[f] if k == 0 else w[f] + a * fields[f]
                l[f] = b * fields[f] if k == 0 else l[f] + b * fields[f]
        for f in range(6):
            w_ref[pl.ds(f * ny + start, 8), :] = w[f]
            l_ref[f, rows, :] = l[f]
        return carry

    lax.fori_loop(0, ny // 8, tile, 0)
    index = lax.broadcasted_iota(jnp.int32, (8, w_ref.shape[1]), 0)
    w_ref[6 * ny : 6 * ny + 8, :] = jnp.where(index == 0, table_ref[table.oo], table_ref[table.oo1])


def x_ends(table, velocity, halo):
    _, n, ny, nz = velocity.shape
    return pl.pallas_call(
        functools.partial(x_ends_kernel, n, ny),
        in_specs=[WHOLE] * 3,
        out_specs=[WHOLE, WHOLE],
        out_shape=[layer_shape(6 * ny + 8, nz), layer_shape(6, ny, nz)],
        compiler_params=params(),
        cost_estimate=cost(SHORT),
        name="x_ends",
    )(table, velocity, halo)


def x_face_kernel(n, ny, table_ref, wr_ref, ws_ref, l_ref, own_ref, near_ref, after_ref, w_ref, e_ref):
    ends = Ends(n)
    table = Table(n)
    shape = (8, wr_ref.shape[1])
    p_oo = jnp.broadcast_to(wr_ref[6 * ny : 6 * ny + 1, :], shape)
    p_oo1 = jnp.broadcast_to(wr_ref[6 * ny + 1 : 6 * ny + 2, :], shape)
    x_qo = table_ref[table.qo]
    inverse_den = 1.0 / (1.0 - COUPLING * COUPLING * table_ref[table.oo] * p_oo)
    sent_weight = COUPLING * p_oo
    own_weight = COUPLING * FAR * ends.sign_o * p_oo1
    near_weight = COUPLING * FAR * ends.sign_o * COUPLING * table_ref[table.oo1] * p_oo
    end_weight = ends.sign_o * FAR * table_ref[table.qo1]

    def tile(index, carry):
        start = pl.multiple_of(index * 8, 8)
        rows = pl.ds(start, 8)
        own = six([own_ref[i, rows, :] for i in range(3)], 0)
        near = six([near_ref[i, rows, :] for i in range(3)], 0)
        for f in range(6):
            field = pl.ds(f * ny + start, 8)
            w = wr_ref[field, :] - sent_weight * ws_ref[field, :]
            w = (w + own_weight * own[f] + near_weight * near[f]) * inverse_den
            w_ref[f, rows, :] = 36.0 * w
            e_ref[field, :] = l_ref[f, rows, :] + x_qo * w + end_weight * near[f]
        return carry

    lax.fori_loop(0, ny // 8, tile, 0)
    e_ref[6 * ny : 6 * ny + 8, :] = table_ref[table.qq]


def x_face(table, received, sent, partial, own, near, after, n):
    _, ny, nz = own.shape
    return pl.pallas_call(
        functools.partial(x_face_kernel, n, ny),
        in_specs=[WHOLE] * 6 + [ANY],
        out_specs=[WHOLE, WHOLE],
        out_shape=[layer_shape(6, ny, nz), layer_shape(6 * ny + 8, nz)],
        compiler_params=params(),
        cost_estimate=cost(SHORT),
        name="x_face",
    )(table, received, sent, partial, own, near, after)


def x_sweeps(n, table, table_ref, line, at_first, at_second, at_last_but_one, at_last):
    forward = []
    for k in range(n):
        if k == 0:
            source = 28.0 * line[1] + (line[2] + at_first)
        elif k == 1:
            source = 28.0 * (line[2] - line[0]) + (line[3] + at_second)
        elif k == n - 1:
            source = (at_last - line[n - 3]) - 28.0 * line[n - 2]
        elif k == n - 2:
            source = 28.0 * (line[n - 1] - line[n - 3]) + (at_last_but_one - line[n - 4])
        else:
            source = 28.0 * (line[k + 1] - line[k - 1]) + (line[k + 2] - line[k - 2])
        value = table_ref[table.source + k] * source
        if k > 0:
            value = value - table_ref[table.forward + k] * forward[k - 1]
        forward.append(value)
    solved = [None] * (n - 1) + [forward[n - 1]]
    for k in reversed(range(n - 1)):
        solved[k] = forward[k] - table_ref[table.backward + k] * solved[k + 1]
    return solved


def each_side(run):
    first = lax.axis_index("gy") == 0
    pl.when(first)(functools.partial(run, True))
    pl.when(jnp.logical_not(first))(functools.partial(run, False))


def x_gradient_kernel(n, ny, table_ref, v_ref, near_ref, halo_ref, y_ref, gradient_ref, g_ref, sem):
    table = Table(n)
    y_copy = pltpu.make_async_copy(y_ref, gradient_ref.at[:, 1], sem)
    y_copy.start()

    def run(first):
        sign = -1.0 if first else 1.0
        near_j, far_j = (0, 1) if first else (1, 0)

        def tile(index, carry):
            rows = pl.ds(pl.multiple_of(index * 8, 8), 8)
            for f in range(3):
                line = [v_ref[f, k, rows, :] for k in range(n)]
                inner_near = -sign * halo_ref[f, near_j, rows, :]
                inner = 28.0 * inner_near - sign * halo_ref[f, far_j, rows, :]
                near = sign * near_ref[f, rows, :]
                zero = jnp.zeros_like(near)
                ends = (zero, near, inner_near, inner) if first else (inner, inner_near, near, zero)
                for k, value in enumerate(x_sweeps(n, table, table_ref, line, *ends)):
                    g_ref[f, k, rows, :] = value
            return carry

        lax.fori_loop(0, ny // 8, tile, 0)

    each_side(run)
    y_copy.wait()


def x_gradient_own(table, velocity, near, halo, y_gradient):
    _, n, ny, nz = velocity.shape
    return pl.pallas_call(
        functools.partial(x_gradient_kernel, n, ny),
        in_specs=[WHOLE] * 5,
        out_specs=[ANY, WHOLE],
        out_shape=[layer_shape(3, 3, n, ny, nz), in_vmem(3, n, ny, nz)],
        scratch_shapes=[pltpu.SemaphoreType.DMA],
        compiler_params=params(),
        cost_estimate=cost(SHORT),
        name="x_gradient_own",
    )(table, velocity, near, halo, y_gradient)


def x_solve_kernel(
    n, ny, table_ref, v_ref, near_ref, halo_ref, w_ref, e_ref, r_ref, own_ref, part_ref, lines_ref, side_ref, z_ref, held_ref,
    gradient_ref, convection_ref, g_ref, c_ref, beside_ref, sem,
):
    table = Table(n)
    nz = v_ref.shape[3]
    parts = sem.shape[1]
    share = ny // parts
    z_copy = pltpu.make_async_copy(z_ref, gradient_ref.at[:, 2], sem.at[2, 0])
    z_copy.start()
    p_qq = r_ref[6 * ny : 6 * ny + 8, :]
    weight = COUPLING * p_qq
    scale = -36.0 * COUPLING / (1.0 - COUPLING * COUPLING * table_ref[table.qq] * p_qq)

    def copies(part):
        rows = pl.ds(pl.multiple_of(part * share, 8), share)
        return (
            pltpu.make_async_copy(g_ref.at[:, :, rows], gradient_ref.at[:, 0, :, rows], sem.at[0, part]),
            pltpu.make_async_copy(c_ref.at[:, :, rows], convection_ref.at[:, :, rows], sem.at[1, part]),
        )

    def run(first):
        sign = -1.0 if first else 1.0
        near_j, far_j = (0, 1) if first else (1, 0)

        def step(part, carry):
            base = pl.multiple_of(part * share, 16)
            lines = lines_ref[:, pl.ds(base, share), :].reshape(n * share, lines_ref.shape[2])
            beside_ref[...] = dot(lines, side_ref[:, 3 * nz :])
            def inner_end(f, start):
                field = pl.ds(f * ny + start, 8)
                return scale * (r_ref[field, :] - weight * e_ref[field, :])

            added = []
            for offset in range(0, share, 8):
                rows = pl.ds(base + offset, 8)
                for f in range(3):
                    added.append((f, rows, w_ref[f, rows, :], inner_end(f, base + offset)))
            for k in range(n):
                a, b = table_ref[table.outer + k], table_ref[table.inner + k]
                for f, rows, outer, inner in added:
                    g_ref[f, k, rows, :] = own_ref[f, k, rows, :] + a * outer + b * inner
            for offset in range(0, share, 8):
                start = base + offset
                rows = pl.ds(start, 8)
                near = six([near_ref[i, rows, :] for i in range(3)], 0)
                inner_near = six([halo_ref[i, near_j, rows, :] for i in range(3)], 0)
                inner_far = six([halo_ref[i, far_j, rows, :] for i in range(3)], 0)
                for f in range(3, 6):
                    outer = w_ref[f, rows, :]
                    inner = inner_end(f, start)
                    line = [v_ref[f - 3, k, rows, :] * v_ref[0, k, rows, :] for k in range(n)]
                    inner = inner - sign * (28.0 * inner_near[f] + inner_far[f])
                    ends = (outer, sign * near[f], -sign * inner_near[f], inner)
                    ends = ends if first else ends[::-1]
                    for k, value in enumerate(x_sweeps(n, table, table_ref, line, *ends)):
                        row = k * share + offset
                        beside = beside_ref[row : row + 8, (f - 3) * nz : (f - 2) * nz]
                        c_ref[f - 3, k, rows, :] = value + (part_ref[f - 3, k, rows, :] + beside)
            for copy in copies(part):
                copy.start()
            return carry

        lax.fori_loop(0, parts, step, 0)

    each_side(run)

    def drain(part, carry):
        for copy in copies(part):
            copy.wait()
        return carry

    z_copy.wait()
    lax.fori_loop(0, parts, drain, 0)


def x_solve(table, velocity, near, halo, outer, ends, received, own, partial, lines, side, z_gradient, gradient, share=16):
    _, n, ny, nz = velocity.shape
    return pl.pallas_call(
        functools.partial(x_solve_kernel, n, ny),
        in_specs=[WHOLE] * 12 + [ANY],
        out_specs=[ANY, ANY],
        out_shape=[layer_shape(*gradient.shape), layer_shape(3, n, ny, nz)],
        scratch_shapes=[
            pltpu.VMEM((3, n, ny, nz), F32),
            pltpu.VMEM((3, n, ny, nz), F32),
            pltpu.VMEM((n * share, 3 * nz), F32),
            pltpu.SemaphoreType.DMA((3, ny // share)),
        ],
        input_output_aliases={12: 0},
        compiler_params=params(),
        cost_estimate=cost(SHORT),
        name="x_solve",
    )(table, velocity, near, halo, outer, ends, received, own, partial, lines, side, z_gradient, gradient)


def y_plane(velocities, high_ref, low_ref):
    fields = six(velocities, 1)
    nz = fields[0].shape[1]
    values = []
    for a in (0, 2, 4):
        high, low = split(jnp.concatenate(fields[a : a + 2], axis=1))
        result = dot(high_ref[...], high) + dot(low_ref[...], high) + dot(high_ref[...], low)
        values = values + [result[:, :nz], result[:, nz:]]
    return values


def y_kernel(n, high_ref, low_ref, v_ref, held_ref, part_ref, after_ref, g_ref, c_ref):
    def step(group, carry):
        for u in range(EARLY, GROUP):
            p = group * GROUP + u
            values = y_plane([v_ref[i, p] for i in range(3)], high_ref, low_ref)
            for f in range(3):
                g_ref[f, p] = values[f]
                c_ref[f, p] = values[3 + f] + part_ref[f, p]
        return carry

    lax.fori_loop(0, n // GROUP, step, 0)


def y_solve(high, low, velocity, early, partial, after):
    _, n, ny, nz = velocity.shape
    return pl.pallas_call(
        functools.partial(y_kernel, n),
        in_specs=[WHOLE] * 5 + [ANY],
        out_specs=[WHOLE, WHOLE],
        out_shape=[in_vmem(3, n, ny, nz), in_vmem(3, n, ny, nz)],
        input_output_aliases={3: 0, 4: 1},
        compiler_params=params(),
        cost_estimate=cost(LONG),
        name="y_solve",
    )(high, low, velocity, early, partial, after)


LINES = 128
PACK = 4


def z_own_kernel(
    n, y_inv_ref, y_m_ref, inv_ref, m_ref, v_ref, after_ref,
    g_ref, c_ref, y_ref, high_ref, low_ref, right_ref, left_ref, far_ref, main_ref, turned_ref,
):
    nz = inv_ref.shape[0]
    ny = v_ref.shape[2]
    row = lax.broadcasted_iota(jnp.int32, (ny, ny), 0)
    column = lax.broadcasted_iota(jnp.int32, (ny, ny), 1)
    y_metric = jnp.sum(jnp.where(row == column, y_m_ref[...], 0.0), axis=1, keepdims=True)
    high_ref[...], low_ref[...] = split(times_stencil(y_inv_ref[...]) * y_metric)
    high, low = split(times_stencil(inv_ref[...]).T * m_ref[...])
    both = jnp.concatenate([high, low], axis=1)
    main_ref[...] = jnp.concatenate([both, both], axis=0)
    first_scale = 1.0 / m_ref[0:1, 0:1]
    last_scale = 1.0 / m_ref[0:1, nz - 1 : nz]
    lane = lax.broadcasted_iota(jnp.int32, (ny, nz), 1)

    m = nz - 1
    index = lax.broadcasted_iota(jnp.int32, right_ref.shape[1:], 0)
    for ref, corners in ((right_ref, ((m, m), (m, m - 1), (m, 0), (m, 1))), (left_ref, ((0, 0), (0, 1), (0, m), (0, m - 1)))):
        row = jnp.zeros(right_ref.shape[1:], F32)
        for position, (i, j) in enumerate(corners):
            row = jnp.where(index == position, inv_ref[i : i + 1, j : j + 1], row)
        ref[12] = row

    def segments(u):
        start = u * ny
        while start < (u + 1) * ny:
            stop = min((start // LINES + 1) * LINES, (u + 1) * ny)
            yield start // LINES, start - u * ny, stop - u * ny
            start = stop

    def step(group, carry):
        pieces = [[] for _ in range(GROUP * ny // LINES)]
        for u in range(GROUP):
            p = group * GROUP + u
            velocities = [v_ref[i, p] for i in range(3)]
            values = []
            y_values = [None] * 6
            if u < EARLY:
                y_values = y_plane(velocities, high_ref, low_ref)
                for f in range(3):
                    y_ref[f, p] = y_values[f]
            for f, field in enumerate(six(velocities, 2)):
                high, low = split(field)
                both = dot(jnp.concatenate([high, low], axis=1), main_ref[...])
                value = both[:, :nz] + both[:, nz:]
                if f < 3:
                    g_ref[f, p] = value
                else:
                    c_ref[f - 3, p] = value if u >= EARLY else value + y_values[f]
                values.append(value)
            for block, start, stop in segments(u):
                base = block % PACK * 32
                columns = pltpu.roll(values[0][start:stop], base + 1, axis=1)
                for f in range(1, 6):
                    moved = pltpu.roll(values[f][start:stop], (base + 1 + 2 * f) % nz, axis=1)
                    columns = jnp.where(lane[start:stop] // 2 == base // 2 + f, moved, columns)
                for i in range(3):
                    moved = pltpu.roll(velocities[i][start:stop], (base + 14 + 4 * i) % nz, axis=1)
                    columns = jnp.where(lane[start:stop] // 4 == base // 4 + 3 + i, moved, columns)
                pieces[block].append(columns)
        for j, parts in enumerate(pieces):
            if j % PACK == 0:
                packed = jnp.concatenate(parts, axis=0)
                for other in range(1, PACK):
                    columns = jnp.concatenate(pieces[j + other], axis=0)
                    packed = jnp.where(lane[0:LINES] // 32 == other, columns, packed)
                turned_ref[j // PACK, 0:LINES, :] = packed.T
                blocks = pl.ds(group * len(pieces) + j, PACK)

                def rows(position):
                    return turned_ref[j // PACK, pl.ds(position, PACK, stride=32), :]

                for f in range(6):
                    right_ref[f, blocks, :] = rows(2 * f) * last_scale
                    left_ref[f, blocks, :] = rows(2 * f + 1) * first_scale
                for column in range(4):
                    for i in range(3):
                        values = rows(12 + 4 * i + column)
                        ref = right_ref if column < 2 else left_ref
                        ref[6 + 3 * (column % 2) + i, blocks, :] = values
                        far_ref[3 * column + i, blocks, :] = values
        return carry

    lax.fori_loop(0, n // GROUP, step, 0)


def z_own(y_inverse, y_metric, z_inverse, metric, velocity, after):
    _, n, ny, nz = velocity.shape
    return pl.pallas_call(
        functools.partial(z_own_kernel, n),
        in_specs=[WHOLE] * 5 + [ANY],
        out_specs=[WHOLE] * 8,
        out_shape=[in_vmem(3, n, ny, nz)] * 3
        + [pltpu.VMEM((ny, ny), BF16)] * 2
        + [layer_shape(13, n * ny // LINES, LINES)] * 2
        + [layer_shape(12, n * ny // LINES, LINES)],
        scratch_shapes=[
            pltpu.VMEM((2 * nz, 2 * nz), BF16),
            pltpu.VMEM((GROUP * ny // LINES // PACK, LINES + 32, LINES), F32),
        ],
        compiler_params=params(),
        cost_estimate=cost(SHORT),
        name="z_own",
    )(y_inverse, y_metric, z_inverse, metric, velocity, after)


def z_side(own_right, own_left, left, right, left_2, right_2, out_ref):
    blocks = own_left.shape[1]
    shape = own_left.shape[1:]

    def pair(ref, start):
        return six([ref[start + i] for i in range(3)], 2), six([ref[start + 3 + i] for i in range(3)], 2)

    def from_left(ref, start):
        far, near = pair(ref, start)
        return [(-NEAR * near[f] - FAR * far[f], -FAR * near[f]) for f in range(6)]

    def from_right(ref, start):
        near, far = pair(ref, start)
        return [(NEAR * near[f] + FAR * far[f], FAR * near[f]) for f in range(6)]

    def entries(ref):
        return [jnp.broadcast_to(ref[12, i : i + 1], shape) for i in range(4)]

    def first_value(ref, corners, f, at_left, at_right):
        x_00, x_01, x_0m, x_0l = corners
        return ref[f] + x_00 * at_left[f][0] + x_01 * at_left[f][1] + x_0m * at_right[f][0] + x_0l * at_right[f][1]

    def last_value(ref, corners, f, at_left, at_right):
        x_mm, x_ml, x_m0, x_m1 = corners
        return ref[f] + x_m0 * at_left[f][0] + x_m1 * at_left[f][1] + x_mm * at_right[f][0] + x_ml * at_right[f][1]

    own_first_row, own_last_row, left_row, right_row = (entries(ref) for ref in (own_left, own_right, left, right))
    at_left, at_right = from_left(left, 6), from_right(right, 6)
    left_at_left, left_at_right = from_left(left_2, 0), from_right(own_left, 6)
    right_at_left, right_at_right = from_left(own_right, 6), from_right(right_2, 6)
    left_den = 1.0 / (1.0 - COUPLING * COUPLING * left_row[0] * own_first_row[0])
    right_den = 1.0 / (1.0 - COUPLING * COUPLING * right_row[0] * own_last_row[0])
    for f in range(8):
        if f < 6:
            own_first = first_value(own_left, own_first_row, f, at_left, at_right)
            own_last = last_value(own_right, own_last_row, f, at_left, at_right)
            left_value = last_value(left, left_row, f, left_at_left, left_at_right)
            right_value = first_value(right, right_row, f, right_at_left, right_at_right)
            left_final = (left_value - COUPLING * left_row[0] * own_first) * left_den
            right_start = (right_value - COUPLING * right_row[0] * own_last) * right_den
            kinds = (
                at_left[f][0] - COUPLING * left_final,
                at_left[f][1],
                at_right[f][0] - COUPLING * right_start,
                at_right[f][1],
            )
        else:
            kinds = (jnp.zeros(shape, F32),) * 4
        for kind, values in enumerate(kinds):
            start = (8 * kind + f) * blocks
            out_ref[start : start + blocks, :] = values


def z_gradient_kernel(
    n, inv_ref, m_ref, g_ref, own_right_ref, own_left_ref, left_ref, right_ref, left_2_ref, right_2_ref,
    after_ref, out_ref, lines_ref, side_ref, beside_ref,
):
    nz = inv_ref.shape[0]
    ny = g_ref.shape[2]
    columns = inv_ref[...].T * m_ref[...]
    index = lax.broadcasted_iota(jnp.int32, (32, nz), 0)
    kind = index // 8
    picked = jnp.where(
        kind == 0,
        columns[0:1],
        jnp.where(kind == 1, columns[1:2], jnp.where(kind == 2, columns[nz - 1 : nz], columns[nz - 2 : nz - 1])),
    )
    wide = jnp.concatenate([jnp.where(index % 8 == f, picked, 0.0) for f in range(6)], axis=1)
    high, low = split(wide)
    side_ref[...] = jnp.concatenate([high, high, low], axis=0)
    planes = GROUP
    blocks = planes * ny // LINES
    all_blocks = n * ny // LINES
    z_side(own_right_ref, own_left_ref, left_ref, right_ref, left_2_ref, right_2_ref, beside_ref)

    def step(group, carry):
        sides = []
        for j in range(blocks):
            beside = beside_ref[pl.ds(group * blocks + j, 32, stride=all_blocks), :]
            high, low = split(beside.T)
            sides.append(jnp.concatenate([high, low, high], axis=1))
        for pair in range(planes // 2):
            half = blocks // (planes // 2)
            lines = jnp.concatenate(sides[pair * half : (pair + 1) * half], axis=0)
            for u in range(2):
                lines_ref[group * planes + 2 * pair + u] = lines[u * ny : (u + 1) * ny]
            for f in range(0, 3):
                added = dot(lines, side_ref[:, f * nz : (f + 1) * nz])
                for u in range(2):
                    p = group * planes + 2 * pair + u
                    out_ref[f, p] = added[u * ny : (u + 1) * ny] + g_ref[f, p]
        return carry

    lax.fori_loop(0, n // planes, step, 0)


def z_gradient_join(z_inverse, metric, own, lines, after):
    _, n, ny, nz = own.shape
    return pl.pallas_call(
        functools.partial(z_gradient_kernel, n),
        in_specs=[WHOLE] * 9 + [ANY],
        out_specs=[WHOLE, WHOLE, WHOLE],
        out_shape=[
            in_vmem(3, n, ny, nz),
            pltpu.VMEM((n, ny, 96), BF16),
            pltpu.VMEM((96, 6 * nz), BF16),
        ],
        scratch_shapes=[pltpu.VMEM((33 * (n * ny // LINES), LINES), F32)],
        input_output_aliases={2: 0},
        compiler_params=params(),
        cost_estimate=cost(LONG),
        name="z_gradient_join",
    )(z_inverse, metric, own, *lines, after)


def on_device(mesh, velocity, metric_x, metric_y, metric_z, x_inverse, y_inverse, z_inverse):
    n = velocity.shape[1]
    blocks = mesh.shape["gx"] * 2
    across = [(i, (i + 1) % blocks) for i in range(1, blocks, 2)]
    across = across + [(j, i) for i, j in across]
    beside = [(0, 1), (1, 0)]
    count = mesh.shape["gz"]

    def shift(by):
        return [(i, (i + by) % count) for i in range(count)]

    own, inner = prepare(velocity)
    near = lax.ppermute(own, ("gx", "gy"), across)
    halo = lax.ppermute(inner, "gy", beside)
    held = pltpu.with_memory_space_constraint(velocity, pltpu.VMEM)
    table, y_inverse, metric_y, z_inverse, metric_z = tables(
        x_inverse, metric_x[None], y_inverse, metric_y[None], z_inverse, metric_z[None], own
    )

    x_sent, x_partial = x_ends(table, held, halo)
    x_received = lax.ppermute(x_sent, ("gx", "gy"), across)

    z_gradient, convection, y_gradient, y_high, y_low, to_right, to_left, to_far = z_own(
        y_inverse, metric_y, z_inverse, metric_z, held, x_sent
    )
    left_far = lax.ppermute(to_far, "gz", shift(2))
    right_far = left_far if shift(2) == shift(-2) else lax.ppermute(to_far, "gz", shift(-2))
    z_lines = (
        to_right,
        to_left,
        lax.ppermute(to_right, "gz", shift(1)),
        lax.ppermute(to_left, "gz", shift(-1)),
        left_far,
        right_far,
    )

    y_gradient, convection = y_solve(y_high, y_low, held, y_gradient, convection, near)
    gradient, x_gradient = x_gradient_own(table, held, near, halo, y_gradient)
    outer, x_end = x_face(table, x_received, x_sent, x_partial, own, near, x_gradient, n)
    x_other = lax.ppermute(x_end, "gy", beside)
    z_gradient, lines, side = z_gradient_join(z_inverse, metric_z, z_gradient, z_lines, x_end)
    return tuple(
        x_solve(
            table, held, near, halo, outer, x_end, x_other, x_gradient, convection, lines, side, z_gradient, gradient
        )
    )


def solution(mesh):
    return jax.shard_map(
        functools.partial(on_device, mesh),
        mesh=mesh,
        in_specs=(
            P(None, ("gx", "gy"), None, "gz"),
            P(("gx", "gy")),
            P(),
            P("gz"),
            P(("gx", "gy"), None),
            P(),
            P("gz", None),
        ),
        out_specs=(P(None, None, ("gx", "gy"), None, "gz"), P(None, ("gx", "gy"), None, "gz")),
        check_vma=False,
    )
```

```python
import functools

import jax
import jax.numpy as jnp
from jax import lax
from jax.experimental import pallas as pl
from jax.experimental.pallas import tpu as pltpu
from jax.sharding import PartitionSpec as P

COUPLING = 1.0 / 3.0
NEAR = 7.0 / 9.0
FAR = 1.0 / 36.0
F32 = jnp.float32
BF16 = jnp.bfloat16
SMEM = pltpu.SMEM
VMEM_LIMIT = 20 * 1024 * 1024
GROUP = 8
EARLY = 4
SHORT, LONG = 4, 20_000_000_000


def split(values):
    high = values.astype(BF16)
    low = (values - high.astype(F32)).astype(BF16)
    return high, low


def dot(a, b):
    return lax.dot_general(a, b, (((1,), (0,)), ((), ())), preferred_element_type=F32)


def params():
    return pltpu.CompilerParams(vmem_limit_bytes=VMEM_LIMIT)


def six(velocity, direction):
    return list(velocity) + [velocity[i] * velocity[direction] for i in range(3)]


def times_stencil(inverse):
    rows, length = inverse.shape
    zeros = jnp.zeros((rows, 2), F32)
    wide = jnp.concatenate([zeros, inverse, zeros], axis=1)

    def column(offset):
        return wide[:, 2 + offset : 2 + offset + length]

    return NEAR * (column(-1) - column(1)) + FAR * (column(-2) - column(2))


def in_vmem(*shape):
    return pltpu.VMEM(shape, F32)


ANY = pl.BlockSpec(memory_space=pl.ANY)
WHOLE = pl.BlockSpec(memory_space=pltpu.VMEM)
SCALARS = pl.BlockSpec(memory_space=SMEM)


def cost(flops):
    return pl.CostEstimate(flops=flops, bytes_accessed=1, transcendentals=0)


def layer_shape(*shape):
    return jax.ShapeDtypeStruct(shape, F32)


class Ends:
    def __init__(self, n):
        self.first = lax.axis_index("gy") == 0
        self.n = n
        self.o = jnp.where(self.first, 0, n - 1)
        self.o1 = jnp.where(self.first, 1, n - 2)
        self.q = jnp.where(self.first, n - 1, 0)
        self.q1 = jnp.where(self.first, n - 2, 1)
        self.sign_o = jnp.where(self.first, -1.0, 1.0).astype(F32)
        self.sign_q = -self.sign_o


class Table:
    def __init__(self, n):
        self.source, self.forward, self.backward = 0, n, 2 * n
        self.send, self.last = 3 * n, 4 * n + 2
        self.outer, self.inner = 5 * n + 4, 6 * n + 4
        self.oo, self.oo1, self.qo, self.qo1, self.qq = range(7 * n + 4, 7 * n + 9)
        self.size = 7 * n + 9


def prepare_kernel(n, v_ref, own_ref, halo_ref, sem):
    ends = Ends(n)
    copies = []
    for i in range(3):
        copies.append(pltpu.make_async_copy(v_ref.at[i, ends.o], own_ref.at[i], sem.at[3 * i]))
        for j in range(2):
            plane = jnp.where(ends.first, n - 2 + j, j)
            copies.append(pltpu.make_async_copy(v_ref.at[i, plane], halo_ref.at[i, j], sem.at[3 * i + 1 + j]))
    for copy in copies:
        copy.start()
    for copy in copies:
        copy.wait()


def prepare(velocity):
    _, n, ny, nz = velocity.shape
    return pl.pallas_call(
        functools.partial(prepare_kernel, n),
        in_specs=[ANY],
        out_specs=[WHOLE] * 2,
        out_shape=[layer_shape(3, ny, nz), layer_shape(3, 2, ny, nz)],
        scratch_shapes=[pltpu.SemaphoreType.DMA((9,))],
        compiler_params=params(),
        name="prepare",
    )(pltpu.with_memory_space_constraint(velocity, pltpu.HBM))


def tables_kernel(
    n, xi_ref, mx_ref, yi_ref, my_ref, zi_ref, mz_ref, after_ref,
    table_ref, y_ref, y_metric_ref, z_ref, z_metric_ref, x_ref, m_ref, sem,
):
    ends = Ends(n)
    nz = table_ref.shape[2]
    small = [pltpu.make_async_copy(xi_ref, x_ref, sem.at[0]), pltpu.make_async_copy(mx_ref, m_ref, sem.at[1])]
    copies = [
        pltpu.make_async_copy(zi_ref, z_ref, sem.at[2]),
        pltpu.make_async_copy(mz_ref, z_metric_ref, sem.at[3]),
        pltpu.make_async_copy(yi_ref, y_ref, sem.at[4]),
        pltpu.make_async_copy(my_ref, y_metric_ref, sem.at[5]),
    ]
    for copy in small + copies:
        copy.start()
    for copy in small:
        copy.wait()

    table = Table(n)
    first = ends.first

    def spread(value):
        return jnp.broadcast_to(value, (8, nz))

    def entry(i, j):
        return spread(x_ref[i : i + 1, j : j + 1])

    metric = [spread(m_ref[0:1, k : k + 1]) for k in range(n)]
    above = [entry(i, i + 1) for i in range(n - 1)]
    diagonal = [entry(i, i) for i in range(n)]
    ratio = [-above[i] / diagonal[i + 1] for i in range(n - 1)]
    ratio.append(-entry(n - 1, n - 2) / diagonal[n - 2] * diagonal[n - 1])
    for k in range(n):
        if k == 0:
            source = metric[k]
        elif k == n - 1:
            source = diagonal[k] * metric[k]
        else:
            source = (1.0 + ratio[k] * ratio[k - 1]) * metric[k]
        table_ref[table.source + k] = FAR * source
        table_ref[table.forward + k] = ratio[k] * metric[k] / metric[k - 1] if k > 0 else metric[k]
        table_ref[table.backward + k] = ratio[k] * metric[k] / metric[k + 1] if k < n - 1 else metric[k]

    top = [entry(0, k) for k in range(n)]
    bottom = [entry(n - 1, k) for k in range(n)]
    outer = [jnp.where(first, top[k], bottom[k]) for k in range(n)]
    inner = [jnp.where(first, bottom[k], top[k]) for k in range(n)]
    sign_o, sign_q = ends.sign_o, ends.sign_q
    for base, row, factor in ((table.send, outer, -COUPLING), (table.last, inner, 1.0)):

        def at(k):
            return row[k] if 0 <= k < n else jnp.zeros_like(row[0])

        for k in range(n):
            value = factor * (NEAR * (at(k - 1) - at(k + 1)) + FAR * (at(k - 2) - at(k + 2)))
            if base == table.send:
                if k == 0:
                    value = value + jnp.where(first, NEAR, 0.0)
                elif k == 1:
                    value = value + jnp.where(first, FAR, 0.0)
                elif k == n - 2:
                    value = value - jnp.where(first, 0.0, FAR)
                elif k == n - 1:
                    value = value - jnp.where(first, 0.0, NEAR)
            table_ref[base + k] = value
        at_q = jnp.where(first, row[n - 1], row[0])
        at_q1 = jnp.where(first, row[n - 2], row[1])
        near = factor * sign_q * (NEAR * at_q + FAR * at_q1)
        far = factor * sign_q * FAR * at_q
        table_ref[base + n] = jnp.where(first, near, far)
        table_ref[base + n + 1] = jnp.where(first, far, near)
    for k in range(n):
        left, right = FAR * metric[k] * entry(k, 0), FAR * metric[k] * entry(k, n - 1)
        table_ref[table.outer + k] = jnp.where(first, left, right)
        table_ref[table.inner + k] = jnp.where(first, right, left)
    table_ref[table.oo] = jnp.where(first, outer[0], outer[n - 1])
    table_ref[table.oo1] = jnp.where(first, outer[1], outer[n - 2])
    table_ref[table.qo] = jnp.where(first, inner[0], inner[n - 1])
    table_ref[table.qo1] = jnp.where(first, inner[1], inner[n - 2])
    table_ref[table.qq] = jnp.where(first, inner[n - 1], inner[0])
    for copy in copies:
        copy.wait()


def tables(x_inverse, metric_x, y_inverse, metric_y, z_inverse, metric_z, after):
    n, ny, nz = x_inverse.shape[0], y_inverse.shape[0], z_inverse.shape[0]
    inputs = (x_inverse, metric_x, y_inverse, metric_y, z_inverse, metric_z)
    return pl.pallas_call(
        functools.partial(tables_kernel, n),
        in_specs=[ANY] * 7,
        out_specs=[WHOLE] * 5,
        out_shape=[
            in_vmem(Table(n).size, 8, nz),
            in_vmem(ny, ny),
            in_vmem(1, ny),
            in_vmem(nz, nz),
            in_vmem(1, nz),
        ],
        scratch_shapes=[pltpu.VMEM((n, n), F32), pltpu.VMEM((1, n), F32), pltpu.SemaphoreType.DMA((6,))],
        compiler_params=params(),
        cost_estimate=cost(LONG),
        name="tables",
    )(*(pltpu.with_memory_space_constraint(value, pltpu.HBM) for value in inputs), after)


def x_ends_kernel(n, ny, table_ref, v_ref, halo_ref, w_ref, l_ref):
    table = Table(n)

    def tile(index, carry):
        start = pl.multiple_of(index * 8, 8)
        rows = pl.ds(start, 8)
        w = [None] * 6
        l = [None] * 6
        for k in range(n + 2):
            if k < n:
                fields = six([v_ref[i, k, rows, :] for i in range(3)], 0)
            else:
                fields = six([halo_ref[i, k - n, rows, :] for i in range(3)], 0)
            a, b = table_ref[table.send + k], table_ref[table.last + k]
            for f in range(6):
                w[f] = a * fields[f] if k == 0 else w[f] + a * fields[f]
                l[f] = b * fields[f] if k == 0 else l[f] + b * fields[f]
        for f in range(6):
            w_ref[pl.ds(f * ny + start, 8), :] = w[f]
            l_ref[f, rows, :] = l[f]
        return carry

    lax.fori_loop(0, ny // 8, tile, 0)
    index = lax.broadcasted_iota(jnp.int32, (8, w_ref.shape[1]), 0)
    w_ref[6 * ny : 6 * ny + 8, :] = jnp.where(index == 0, table_ref[table.oo], table_ref[table.oo1])


def x_ends(table, velocity, halo):
    _, n, ny, nz = velocity.shape
    return pl.pallas_call(
        functools.partial(x_ends_kernel, n, ny),
        in_specs=[WHOLE] * 3,
        out_specs=[WHOLE, WHOLE],
        out_shape=[layer_shape(6 * ny + 8, nz), layer_shape(6, ny, nz)],
        compiler_params=params(),
        cost_estimate=cost(SHORT),
        name="x_ends",
    )(table, velocity, halo)


def x_face_kernel(n, ny, table_ref, wr_ref, ws_ref, l_ref, own_ref, near_ref, after_ref, w_ref, e_ref):
    ends = Ends(n)
    table = Table(n)
    shape = (8, wr_ref.shape[1])
    p_oo = jnp.broadcast_to(wr_ref[6 * ny : 6 * ny + 1, :], shape)
    p_oo1 = jnp.broadcast_to(wr_ref[6 * ny + 1 : 6 * ny + 2, :], shape)
    x_qo = table_ref[table.qo]
    inverse_den = 1.0 / (1.0 - COUPLING * COUPLING * table_ref[table.oo] * p_oo)
    sent_weight = COUPLING * p_oo
    own_weight = COUPLING * FAR * ends.sign_o * p_oo1
    near_weight = COUPLING * FAR * ends.sign_o * COUPLING * table_ref[table.oo1] * p_oo
    end_weight = ends.sign_o * FAR * table_ref[table.qo1]

    def tile(index, carry):
        start = pl.multiple_of(index * 8, 8)
        rows = pl.ds(start, 8)
        own = six([own_ref[i, rows, :] for i in range(3)], 0)
        near = six([near_ref[i, rows, :] for i in range(3)], 0)
        for f in range(6):
            field = pl.ds(f * ny + start, 8)
            w = wr_ref[field, :] - sent_weight * ws_ref[field, :]
            w = (w + own_weight * own[f] + near_weight * near[f]) * inverse_den
            w_ref[f, rows, :] = 36.0 * w
            e_ref[field, :] = l_ref[f, rows, :] + x_qo * w + end_weight * near[f]
        return carry

    lax.fori_loop(0, ny // 8, tile, 0)
    e_ref[6 * ny : 6 * ny + 8, :] = table_ref[table.qq]


def x_face(table, received, sent, partial, own, near, after, n):
    _, ny, nz = own.shape
    return pl.pallas_call(
        functools.partial(x_face_kernel, n, ny),
        in_specs=[WHOLE] * 6 + [ANY],
        out_specs=[WHOLE, WHOLE],
        out_shape=[layer_shape(6, ny, nz), layer_shape(6 * ny + 8, nz)],
        compiler_params=params(),
        cost_estimate=cost(SHORT),
        name="x_face",
    )(table, received, sent, partial, own, near, after)


def x_sweeps(n, table, table_ref, line, at_first, at_second, at_last_but_one, at_last):
    forward = []
    for k in range(n):
        if k == 0:
            source = 28.0 * line[1] + (line[2] + at_first)
        elif k == 1:
            source = 28.0 * (line[2] - line[0]) + (line[3] + at_second)
        elif k == n - 1:
            source = (at_last - line[n - 3]) - 28.0 * line[n - 2]
        elif k == n - 2:
            source = 28.0 * (line[n - 1] - line[n - 3]) + (at_last_but_one - line[n - 4])
        else:
            source = 28.0 * (line[k + 1] - line[k - 1]) + (line[k + 2] - line[k - 2])
        value = table_ref[table.source + k] * source
        if k > 0:
            value = value - table_ref[table.forward + k] * forward[k - 1]
        forward.append(value)
    solved = [None] * (n - 1) + [forward[n - 1]]
    for k in reversed(range(n - 1)):
        solved[k] = forward[k] - table_ref[table.backward + k] * solved[k + 1]
    return solved


def each_side(run):
    first = lax.axis_index("gy") == 0
    pl.when(first)(functools.partial(run, True))
    pl.when(jnp.logical_not(first))(functools.partial(run, False))


def x_gradient_kernel(n, ny, table_ref, v_ref, near_ref, halo_ref, y_ref, gradient_ref, g_ref, sem):
    table = Table(n)
    y_copy = pltpu.make_async_copy(y_ref, gradient_ref.at[:, 1], sem)
    y_copy.start()

    def run(first):
        sign = -1.0 if first else 1.0
        near_j, far_j = (0, 1) if first else (1, 0)

        def tile(index, carry):
            rows = pl.ds(pl.multiple_of(index * 8, 8), 8)
            for f in range(3):
                line = [v_ref[f, k, rows, :] for k in range(n)]
                inner_near = -sign * halo_ref[f, near_j, rows, :]
                inner = 28.0 * inner_near - sign * halo_ref[f, far_j, rows, :]
                near = sign * near_ref[f, rows, :]
                zero = jnp.zeros_like(near)
                ends = (zero, near, inner_near, inner) if first else (inner, inner_near, near, zero)
                for k, value in enumerate(x_sweeps(n, table, table_ref, line, *ends)):
                    g_ref[f, k, rows, :] = value
            return carry

        lax.fori_loop(0, ny // 8, tile, 0)

    each_side(run)
    y_copy.wait()


def x_gradient_own(table, velocity, near, halo, y_gradient):
    _, n, ny, nz = velocity.shape
    return pl.pallas_call(
        functools.partial(x_gradient_kernel, n, ny),
        in_specs=[WHOLE] * 5,
        out_specs=[ANY, WHOLE],
        out_shape=[layer_shape(3, 3, n, ny, nz), in_vmem(3, n, ny, nz)],
        scratch_shapes=[pltpu.SemaphoreType.DMA],
        compiler_params=params(),
        cost_estimate=cost(SHORT),
        name="x_gradient_own",
    )(table, velocity, near, halo, y_gradient)


def x_solve_kernel(
    n, ny, table_ref, v_ref, near_ref, halo_ref, w_ref, e_ref, r_ref, own_ref, part_ref, lines_ref, side_ref, z_ref, held_ref,
    gradient_ref, convection_ref, g_ref, c_ref, beside_ref, sem,
):
    table = Table(n)
    nz = v_ref.shape[3]
    parts = sem.shape[1]
    share = ny // parts
    z_copy = pltpu.make_async_copy(z_ref, gradient_ref.at[:, 2], sem.at[2, 0])
    z_copy.start()
    p_qq = r_ref[6 * ny : 6 * ny + 8, :]
    weight = COUPLING * p_qq
    scale = -36.0 * COUPLING / (1.0 - COUPLING * COUPLING * table_ref[table.qq] * p_qq)

    def copies(part):
        rows = pl.ds(pl.multiple_of(part * share, 8), share)
        return (
            pltpu.make_async_copy(g_ref.at[:, :, rows], gradient_ref.at[:, 0, :, rows], sem.at[0, part]),
            pltpu.make_async_copy(c_ref.at[:, :, rows], convection_ref.at[:, :, rows], sem.at[1, part]),
        )

    def run(first):
        sign = -1.0 if first else 1.0
        near_j, far_j = (0, 1) if first else (1, 0)

        def step(part, carry):
            base = pl.multiple_of(part * share, 16)
            lines = lines_ref[:, pl.ds(base, share), :].reshape(n * share, lines_ref.shape[2])
            beside_ref[...] = dot(lines, side_ref[:, 3 * nz :])
            def inner_end(f, start):
                field = pl.ds(f * ny + start, 8)
                return scale * (r_ref[field, :] - weight * e_ref[field, :])

            added = []
            for offset in range(0, share, 8):
                rows = pl.ds(base + offset, 8)
                for f in range(3):
                    added.append((f, rows, w_ref[f, rows, :], inner_end(f, base + offset)))
            for k in range(n):
                a, b = table_ref[table.outer + k], table_ref[table.inner + k]
                for f, rows, outer, inner in added:
                    g_ref[f, k, rows, :] = own_ref[f, k, rows, :] + a * outer + b * inner
            for offset in range(0, share, 8):
                start = base + offset
                rows = pl.ds(start, 8)
                near = six([near_ref[i, rows, :] for i in range(3)], 0)
                inner_near = six([halo_ref[i, near_j, rows, :] for i in range(3)], 0)
                inner_far = six([halo_ref[i, far_j, rows, :] for i in range(3)], 0)
                for f in range(3, 6):
                    outer = w_ref[f, rows, :]
                    inner = inner_end(f, start)
                    line = [v_ref[f - 3, k, rows, :] * v_ref[0, k, rows, :] for k in range(n)]
                    inner = inner - sign * (28.0 * inner_near[f] + inner_far[f])
                    ends = (outer, sign * near[f], -sign * inner_near[f], inner)
                    ends = ends if first else ends[::-1]
                    for k, value in enumerate(x_sweeps(n, table, table_ref, line, *ends)):
                        row = k * share + offset
                        beside = beside_ref[row : row + 8, (f - 3) * nz : (f - 2) * nz]
                        c_ref[f - 3, k, rows, :] = value + (part_ref[f - 3, k, rows, :] + beside)
            for copy in copies(part):
                copy.start()
            return carry

        lax.fori_loop(0, parts, step, 0)

    each_side(run)

    def drain(part, carry):
        for copy in copies(part):
            copy.wait()
        return carry

    z_copy.wait()
    lax.fori_loop(0, parts, drain, 0)


def x_solve(table, velocity, near, halo, outer, ends, received, own, partial, lines, side, z_gradient, gradient, share=16):
    _, n, ny, nz = velocity.shape
    return pl.pallas_call(
        functools.partial(x_solve_kernel, n, ny),
        in_specs=[WHOLE] * 12 + [ANY],
        out_specs=[ANY, ANY],
        out_shape=[layer_shape(*gradient.shape), layer_shape(3, n, ny, nz)],
        scratch_shapes=[
            pltpu.VMEM((3, n, ny, nz), F32),
            pltpu.VMEM((3, n, ny, nz), F32),
            pltpu.VMEM((n * share, 3 * nz), F32),
            pltpu.SemaphoreType.DMA((3, ny // share)),
        ],
        input_output_aliases={12: 0},
        compiler_params=params(),
        cost_estimate=cost(SHORT),
        name="x_solve",
    )(table, velocity, near, halo, outer, ends, received, own, partial, lines, side, z_gradient, gradient)


def y_plane(velocities, high_ref, low_ref):
    fields = six(velocities, 1)
    nz = fields[0].shape[1]
    values = []
    for a in (0, 2, 4):
        high, low = split(jnp.concatenate(fields[a : a + 2], axis=1))
        result = dot(high_ref[...], high) + dot(low_ref[...], high) + dot(high_ref[...], low)
        values = values + [result[:, :nz], result[:, nz:]]
    return values


def y_kernel(n, high_ref, low_ref, v_ref, held_ref, part_ref, after_ref, g_ref, c_ref):
    def step(group, carry):
        for u in range(EARLY, GROUP):
            p = group * GROUP + u
            values = y_plane([v_ref[i, p] for i in range(3)], high_ref, low_ref)
            for f in range(3):
                g_ref[f, p] = values[f]
                c_ref[f, p] = values[3 + f] + part_ref[f, p]
        return carry

    lax.fori_loop(0, n // GROUP, step, 0)


def y_solve(high, low, velocity, early, partial, after):
    _, n, ny, nz = velocity.shape
    return pl.pallas_call(
        functools.partial(y_kernel, n),
        in_specs=[WHOLE] * 5 + [ANY],
        out_specs=[WHOLE, WHOLE],
        out_shape=[in_vmem(3, n, ny, nz), in_vmem(3, n, ny, nz)],
        input_output_aliases={3: 0, 4: 1},
        compiler_params=params(),
        cost_estimate=cost(LONG),
        name="y_solve",
    )(high, low, velocity, early, partial, after)


LINES = 128
PACK = 4


def z_own_kernel(
    n, y_inv_ref, y_m_ref, inv_ref, m_ref, v_ref, after_ref,
    g_ref, c_ref, y_ref, high_ref, low_ref, right_ref, left_ref, far_ref, main_ref, turned_ref,
):
    nz = inv_ref.shape[0]
    ny = v_ref.shape[2]
    row = lax.broadcasted_iota(jnp.int32, (ny, ny), 0)
    column = lax.broadcasted_iota(jnp.int32, (ny, ny), 1)
    y_metric = jnp.sum(jnp.where(row == column, y_m_ref[...], 0.0), axis=1, keepdims=True)
    high_ref[...], low_ref[...] = split(times_stencil(y_inv_ref[...]) * y_metric)
    high, low = split(times_stencil(inv_ref[...]).T * m_ref[...])
    both = jnp.concatenate([high, low], axis=1)
    main_ref[...] = jnp.concatenate([both, both], axis=0)
    first_scale = 1.0 / m_ref[0:1, 0:1]
    last_scale = 1.0 / m_ref[0:1, nz - 1 : nz]
    lane = lax.broadcasted_iota(jnp.int32, (ny, nz), 1)

    m = nz - 1
    index = lax.broadcasted_iota(jnp.int32, right_ref.shape[1:], 0)
    for ref, corners in ((right_ref, ((m, m), (m, m - 1), (m, 0), (m, 1))), (left_ref, ((0, 0), (0, 1), (0, m), (0, m - 1)))):
        row = jnp.zeros(right_ref.shape[1:], F32)
        for position, (i, j) in enumerate(corners):
            row = jnp.where(index == position, inv_ref[i : i + 1, j : j + 1], row)
        ref[12] = row

    def segments(u):
        start = u * ny
        while start < (u + 1) * ny:
            stop = min((start // LINES + 1) * LINES, (u + 1) * ny)
            yield start // LINES, start - u * ny, stop - u * ny
            start = stop

    def step(group, carry):
        pieces = [[] for _ in range(GROUP * ny // LINES)]
        for u in range(GROUP):
            p = group * GROUP + u
            velocities = [v_ref[i, p] for i in range(3)]
            values = []
            y_values = [None] * 6
            if u < EARLY:
                y_values = y_plane(velocities, high_ref, low_ref)
                for f in range(3):
                    y_ref[f, p] = y_values[f]
            for f, field in enumerate(six(velocities, 2)):
                high, low = split(field)
                both = dot(jnp.concatenate([high, low], axis=1), main_ref[...])
                value = both[:, :nz] + both[:, nz:]
                if f < 3:
                    g_ref[f, p] = value
                else:
                    c_ref[f - 3, p] = value if u >= EARLY else value + y_values[f]
                values.append(value)
            for block, start, stop in segments(u):
                base = block % PACK * 32
                columns = pltpu.roll(values[0][start:stop], base + 1, axis=1)
                for f in range(1, 6):
                    moved = pltpu.roll(values[f][start:stop], (base + 1 + 2 * f) % nz, axis=1)
                    columns = jnp.where(lane[start:stop] // 2 == base // 2 + f, moved, columns)
                for i in range(3):
                    moved = pltpu.roll(velocities[i][start:stop], (base + 14 + 4 * i) % nz, axis=1)
                    columns = jnp.where(lane[start:stop] // 4 == base // 4 + 3 + i, moved, columns)
                pieces[block].append(columns)
        for j, parts in enumerate(pieces):
            if j % PACK == 0:
                packed = jnp.concatenate(parts, axis=0)
                for other in range(1, PACK):
                    columns = jnp.concatenate(pieces[j + other], axis=0)
                    packed = jnp.where(lane[0:LINES] // 32 == other, columns, packed)
                turned_ref[j // PACK, 0:LINES, :] = packed.T
                blocks = pl.ds(group * len(pieces) + j, PACK)

                def rows(position):
                    return turned_ref[j // PACK, pl.ds(position, PACK, stride=32), :]

                for f in range(6):
                    right_ref[f, blocks, :] = rows(2 * f) * last_scale
                    left_ref[f, blocks, :] = rows(2 * f + 1) * first_scale
                for column in range(4):
                    for i in range(3):
                        values = rows(12 + 4 * i + column)
                        ref = right_ref if column < 2 else left_ref
                        ref[6 + 3 * (column % 2) + i, blocks, :] = values
                        far_ref[3 * column + i, blocks, :] = values
        return carry

    lax.fori_loop(0, n // GROUP, step, 0)


def z_own(y_inverse, y_metric, z_inverse, metric, velocity, after):
    _, n, ny, nz = velocity.shape
    return pl.pallas_call(
        functools.partial(z_own_kernel, n),
        in_specs=[WHOLE] * 5 + [ANY],
        out_specs=[WHOLE] * 8,
        out_shape=[in_vmem(3, n, ny, nz)] * 3
        + [pltpu.VMEM((ny, ny), BF16)] * 2
        + [layer_shape(13, n * ny // LINES, LINES)] * 2
        + [layer_shape(12, n * ny // LINES, LINES)],
        scratch_shapes=[
            pltpu.VMEM((2 * nz, 2 * nz), BF16),
            pltpu.VMEM((GROUP * ny // LINES // PACK, LINES + 32, LINES), F32),
        ],
        compiler_params=params(),
        cost_estimate=cost(SHORT),
        name="z_own",
    )(y_inverse, y_metric, z_inverse, metric, velocity, after)


def z_side(own_right, own_left, left, right, left_2, right_2, out_ref):
    blocks = own_left.shape[1]
    shape = own_left.shape[1:]

    def pair(ref, start):
        return six([ref[start + i] for i in range(3)], 2), six([ref[start + 3 + i] for i in range(3)], 2)

    def from_left(ref, start):
        far, near = pair(ref, start)
        return [(-NEAR * near[f] - FAR * far[f], -FAR * near[f]) for f in range(6)]

    def from_right(ref, start):
        near, far = pair(ref, start)
        return [(NEAR * near[f] + FAR * far[f], FAR * near[f]) for f in range(6)]

    def entries(ref):
        return [jnp.broadcast_to(ref[12, i : i + 1], shape) for i in range(4)]

    def first_value(ref, corners, f, at_left, at_right):
        x_00, x_01, x_0m, x_0l = corners
        return ref[f] + x_00 * at_left[f][0] + x_01 * at_left[f][1] + x_0m * at_right[f][0] + x_0l * at_right[f][1]

    def last_value(ref, corners, f, at_left, at_right):
        x_mm, x_ml, x_m0, x_m1 = corners
        return ref[f] + x_m0 * at_left[f][0] + x_m1 * at_left[f][1] + x_mm * at_right[f][0] + x_ml * at_right[f][1]

    own_first_row, own_last_row, left_row, right_row = (entries(ref) for ref in (own_left, own_right, left, right))
    at_left, at_right = from_left(left, 6), from_right(right, 6)
    left_at_left, left_at_right = from_left(left_2, 0), from_right(own_left, 6)
    right_at_left, right_at_right = from_left(own_right, 6), from_right(right_2, 6)
    left_den = 1.0 / (1.0 - COUPLING * COUPLING * left_row[0] * own_first_row[0])
    right_den = 1.0 / (1.0 - COUPLING * COUPLING * right_row[0] * own_last_row[0])
    for f in range(8):
        if f < 6:
            own_first = first_value(own_left, own_first_row, f, at_left, at_right)
            own_last = last_value(own_right, own_last_row, f, at_left, at_right)
            left_value = last_value(left, left_row, f, left_at_left, left_at_right)
            right_value = first_value(right, right_row, f, right_at_left, right_at_right)
            left_final = (left_value - COUPLING * left_row[0] * own_first) * left_den
            right_start = (right_value - COUPLING * right_row[0] * own_last) * right_den
            kinds = (
                at_left[f][0] - COUPLING * left_final,
                at_left[f][1],
                at_right[f][0] - COUPLING * right_start,
                at_right[f][1],
            )
        else:
            kinds = (jnp.zeros(shape, F32),) * 4
        for kind, values in enumerate(kinds):
            start = (8 * kind + f) * blocks
            out_ref[start : start + blocks, :] = values


def z_gradient_kernel(
    n, inv_ref, m_ref, g_ref, own_right_ref, own_left_ref, left_ref, right_ref, left_2_ref, right_2_ref,
    after_ref, out_ref, lines_ref, side_ref, beside_ref,
):
    nz = inv_ref.shape[0]
    ny = g_ref.shape[2]
    columns = inv_ref[...].T * m_ref[...]
    index = lax.broadcasted_iota(jnp.int32, (32, nz), 0)
    kind = index // 8
    picked = jnp.where(
        kind == 0,
        columns[0:1],
        jnp.where(kind == 1, columns[1:2], jnp.where(kind == 2, columns[nz - 1 : nz], columns[nz - 2 : nz - 1])),
    )
    wide = jnp.concatenate([jnp.where(index % 8 == f, picked, 0.0) for f in range(6)], axis=1)
    high, low = split(wide)
    side_ref[...] = jnp.concatenate([high, high, low], axis=0)
    planes = GROUP
    blocks = planes * ny // LINES
    all_blocks = n * ny // LINES
    z_side(own_right_ref, own_left_ref, left_ref, right_ref, left_2_ref, right_2_ref, beside_ref)

    def step(group, carry):
        sides = []
        for j in range(blocks):
            beside = beside_ref[pl.ds(group * blocks + j, 32, stride=all_blocks), :]
            high, low = split(beside.T)
            sides.append(jnp.concatenate([high, low, high], axis=1))
        for pair in range(planes // 2):
            half = blocks // (planes // 2)
            lines = jnp.concatenate(sides[pair * half : (pair + 1) * half], axis=0)
            for u in range(2):
                lines_ref[group * planes + 2 * pair + u] = lines[u * ny : (u + 1) * ny]
            for f in range(0, 3):
                added = dot(lines, side_ref[:, f * nz : (f + 1) * nz])
                for u in range(2):
                    p = group * planes + 2 * pair + u
                    out_ref[f, p] = added[u * ny : (u + 1) * ny] + g_ref[f, p]
        return carry

    lax.fori_loop(0, n // planes, step, 0)


def z_gradient_join(z_inverse, metric, own, lines, after):
    _, n, ny, nz = own.shape
    return pl.pallas_call(
        functools.partial(z_gradient_kernel, n),
        in_specs=[WHOLE] * 9 + [ANY],
        out_specs=[WHOLE, WHOLE, WHOLE],
        out_shape=[
            in_vmem(3, n, ny, nz),
            pltpu.VMEM((n, ny, 96), BF16),
            pltpu.VMEM((96, 6 * nz), BF16),
        ],
        scratch_shapes=[pltpu.VMEM((33 * (n * ny // LINES), LINES), F32)],
        input_output_aliases={2: 0},
        compiler_params=params(),
        cost_estimate=cost(LONG),
        name="z_gradient_join",
    )(z_inverse, metric, own, *lines, after)


def on_device(mesh, velocity, metric_x, metric_y, metric_z, x_inverse, y_inverse, z_inverse):
    n = velocity.shape[1]
    blocks = mesh.shape["gx"] * 2
    across = [(i, (i + 1) % blocks) for i in range(1, blocks, 2)]
    across = across + [(j, i) for i, j in across]
    beside = [(0, 1), (1, 0)]
    count = mesh.shape["gz"]

    def shift(by):
        return [(i, (i + by) % count) for i in range(count)]

    own, inner = prepare(velocity)
    near = lax.ppermute(own, ("gx", "gy"), across)
    halo = lax.ppermute(inner, "gy", beside)
    held = pltpu.with_memory_space_constraint(velocity, pltpu.VMEM)
    table, y_inverse, metric_y, z_inverse, metric_z = tables(
        x_inverse, metric_x[None], y_inverse, metric_y[None], z_inverse, metric_z[None], own
    )

    x_sent, x_partial = x_ends(table, held, halo)
    x_received = lax.ppermute(x_sent, ("gx", "gy"), across)

    z_gradient, convection, y_gradient, y_high, y_low, to_right, to_left, to_far = z_own(
        y_inverse, metric_y, z_inverse, metric_z, held, x_sent
    )
    left_far = lax.ppermute(to_far, "gz", shift(2))
    right_far = left_far if shift(2) == shift(-2) else lax.ppermute(to_far, "gz", shift(-2))
    z_lines = (
        to_right,
        to_left,
        lax.ppermute(to_right, "gz", shift(1)),
        lax.ppermute(to_left, "gz", shift(-1)),
        left_far,
        right_far,
    )

    y_gradient, convection = y_solve(y_high, y_low, held, y_gradient, convection, near)
    gradient, x_gradient = x_gradient_own(table, held, near, halo, y_gradient)
    outer, x_end = x_face(table, x_received, x_sent, x_partial, own, near, x_gradient, n)
    x_other = lax.ppermute(x_end, "gy", beside)
    z_gradient, lines, side = z_gradient_join(z_inverse, metric_z, z_gradient, z_lines, x_end)
    return tuple(
        x_solve(
            table, held, near, halo, outer, x_end, x_other, x_gradient, convection, lines, side, z_gradient, gradient
        )
    )


def solution(mesh):
    return jax.shard_map(
        functools.partial(on_device, mesh),
        mesh=mesh,
        in_specs=(
            P(None, ("gx", "gy"), None, "gz"),
            P(("gx", "gy")),
            P(),
            P("gz"),
            P(("gx", "gy"), None),
            P(),
            P("gz", None),
        ),
        out_specs=(P(None, None, ("gx", "gy"), None, "gz"), P(None, ("gx", "gy"), None, "gz")),
        check_vma=False,
    )
```

```python
import functools

import jax
import jax.numpy as jnp
from jax import lax
from jax.experimental import pallas as pl
from jax.experimental.pallas import tpu as pltpu
from jax.sharding import PartitionSpec as P

COUPLING = 1.0 / 3.0
NEAR = 7.0 / 9.0
FAR = 1.0 / 36.0
F32 = jnp.float32
BF16 = jnp.bfloat16
SMEM = pltpu.SMEM
VMEM_LIMIT = 20 * 1024 * 1024
GROUP = 8
EARLY = 4
SHORT, LONG = 4, 20_000_000_000


def split(values):
    high = values.astype(BF16)
    low = (values - high.astype(F32)).astype(BF16)
    return high, low


def dot(a, b):
    return lax.dot_general(a, b, (((1,), (0,)), ((), ())), preferred_element_type=F32)


def params():
    return pltpu.CompilerParams(vmem_limit_bytes=VMEM_LIMIT)


def six(velocity, direction):
    return list(velocity) + [velocity[i] * velocity[direction] for i in range(3)]


def times_stencil(inverse):
    rows, length = inverse.shape
    zeros = jnp.zeros((rows, 2), F32)
    wide = jnp.concatenate([zeros, inverse, zeros], axis=1)

    def column(offset):
        return wide[:, 2 + offset : 2 + offset + length]

    return NEAR * (column(-1) - column(1)) + FAR * (column(-2) - column(2))


def in_vmem(*shape):
    return pltpu.VMEM(shape, F32)


ANY = pl.BlockSpec(memory_space=pl.ANY)
WHOLE = pl.BlockSpec(memory_space=pltpu.VMEM)
SCALARS = pl.BlockSpec(memory_space=SMEM)


def cost(flops):
    return pl.CostEstimate(flops=flops, bytes_accessed=1, transcendentals=0)


def layer_shape(*shape):
    return jax.ShapeDtypeStruct(shape, F32)


class Ends:
    def __init__(self, n):
        self.first = lax.axis_index("gy") == 0
        self.n = n
        self.o = jnp.where(self.first, 0, n - 1)
        self.o1 = jnp.where(self.first, 1, n - 2)
        self.q = jnp.where(self.first, n - 1, 0)
        self.q1 = jnp.where(self.first, n - 2, 1)
        self.sign_o = jnp.where(self.first, -1.0, 1.0).astype(F32)
        self.sign_q = -self.sign_o


class Table:
    def __init__(self, n):
        self.source, self.forward, self.backward = 0, n, 2 * n
        self.send, self.last = 3 * n, 4 * n + 2
        self.outer, self.inner = 5 * n + 4, 6 * n + 4
        self.oo, self.oo1, self.qo, self.qo1, self.qq = range(7 * n + 4, 7 * n + 9)
        self.size = 7 * n + 9


def prepare_kernel(n, v_ref, own_ref, halo_ref, sem):
    ends = Ends(n)
    copies = []
    for i in range(3):
        copies.append(pltpu.make_async_copy(v_ref.at[i, ends.o], own_ref.at[i], sem.at[3 * i]))
        for j in range(2):
            plane = jnp.where(ends.first, n - 2 + j, j)
            copies.append(pltpu.make_async_copy(v_ref.at[i, plane], halo_ref.at[i, j], sem.at[3 * i + 1 + j]))
    for copy in copies:
        copy.start()
    for copy in copies:
        copy.wait()


def prepare(velocity):
    _, n, ny, nz = velocity.shape
    return pl.pallas_call(
        functools.partial(prepare_kernel, n),
        in_specs=[ANY],
        out_specs=[WHOLE] * 2,
        out_shape=[layer_shape(3, ny, nz), layer_shape(3, 2, ny, nz)],
        scratch_shapes=[pltpu.SemaphoreType.DMA((9,))],
        compiler_params=params(),
        name="prepare",
    )(pltpu.with_memory_space_constraint(velocity, pltpu.HBM))


def tables_kernel(
    n, xi_ref, mx_ref, yi_ref, my_ref, zi_ref, mz_ref, after_ref,
    table_ref, y_ref, y_metric_ref, z_ref, z_metric_ref, x_ref, m_ref, sem,
):
    ends = Ends(n)
    nz = table_ref.shape[2]
    small = [pltpu.make_async_copy(xi_ref, x_ref, sem.at[0]), pltpu.make_async_copy(mx_ref, m_ref, sem.at[1])]
    copies = [
        pltpu.make_async_copy(zi_ref, z_ref, sem.at[2]),
        pltpu.make_async_copy(mz_ref, z_metric_ref, sem.at[3]),
        pltpu.make_async_copy(yi_ref, y_ref, sem.at[4]),
        pltpu.make_async_copy(my_ref, y_metric_ref, sem.at[5]),
    ]
    for copy in small + copies:
        copy.start()
    for copy in small:
        copy.wait()

    table = Table(n)
    first = ends.first

    def spread(value):
        return jnp.broadcast_to(value, (8, nz))

    def entry(i, j):
        return spread(x_ref[i : i + 1, j : j + 1])

    metric = [spread(m_ref[0:1, k : k + 1]) for k in range(n)]
    above = [entry(i, i + 1) for i in range(n - 1)]
    diagonal = [entry(i, i) for i in range(n)]
    ratio = [-above[i] / diagonal[i + 1] for i in range(n - 1)]
    ratio.append(-entry(n - 1, n - 2) / diagonal[n - 2] * diagonal[n - 1])
    for k in range(n):
        if k == 0:
            source = metric[k]
        elif k == n - 1:
            source = diagonal[k] * metric[k]
        else:
            source = (1.0 + ratio[k] * ratio[k - 1]) * metric[k]
        table_ref[table.source + k] = FAR * source
        table_ref[table.forward + k] = ratio[k] * metric[k] / metric[k - 1] if k > 0 else metric[k]
        table_ref[table.backward + k] = ratio[k] * metric[k] / metric[k + 1] if k < n - 1 else metric[k]

    top = [entry(0, k) for k in range(n)]
    bottom = [entry(n - 1, k) for k in range(n)]
    outer = [jnp.where(first, top[k], bottom[k]) for k in range(n)]
    inner = [jnp.where(first, bottom[k], top[k]) for k in range(n)]
    sign_o, sign_q = ends.sign_o, ends.sign_q
    for base, row, factor in ((table.send, outer, -COUPLING), (table.last, inner, 1.0)):

        def at(k):
            return row[k] if 0 <= k < n else jnp.zeros_like(row[0])

        for k in range(n):
            value = factor * (NEAR * (at(k - 1) - at(k + 1)) + FAR * (at(k - 2) - at(k + 2)))
            if base == table.send:
                if k == 0:
                    value = value + jnp.where(first, NEAR, 0.0)
                elif k == 1:
                    value = value + jnp.where(first, FAR, 0.0)
                elif k == n - 2:
                    value = value - jnp.where(first, 0.0, FAR)
                elif k == n - 1:
                    value = value - jnp.where(first, 0.0, NEAR)
            table_ref[base + k] = value
        at_q = jnp.where(first, row[n - 1], row[0])
        at_q1 = jnp.where(first, row[n - 2], row[1])
        near = factor * sign_q * (NEAR * at_q + FAR * at_q1)
        far = factor * sign_q * FAR * at_q
        table_ref[base + n] = jnp.where(first, near, far)
        table_ref[base + n + 1] = jnp.where(first, far, near)
    for k in range(n):
        left, right = FAR * metric[k] * entry(k, 0), FAR * metric[k] * entry(k, n - 1)
        table_ref[table.outer + k] = jnp.where(first, left, right)
        table_ref[table.inner + k] = jnp.where(first, right, left)
    table_ref[table.oo] = jnp.where(first, outer[0], outer[n - 1])
    table_ref[table.oo1] = jnp.where(first, outer[1], outer[n - 2])
    table_ref[table.qo] = jnp.where(first, inner[0], inner[n - 1])
    table_ref[table.qo1] = jnp.where(first, inner[1], inner[n - 2])
    table_ref[table.qq] = jnp.where(first, inner[n - 1], inner[0])
    for copy in copies:
        copy.wait()


def tables(x_inverse, metric_x, y_inverse, metric_y, z_inverse, metric_z, after):
    n, ny, nz = x_inverse.shape[0], y_inverse.shape[0], z_inverse.shape[0]
    inputs = (x_inverse, metric_x, y_inverse, metric_y, z_inverse, metric_z)
    return pl.pallas_call(
        functools.partial(tables_kernel, n),
        in_specs=[ANY] * 7,
        out_specs=[WHOLE] * 5,
        out_shape=[
            in_vmem(Table(n).size, 8, nz),
            in_vmem(ny, ny),
            in_vmem(1, ny),
            in_vmem(nz, nz),
            in_vmem(1, nz),
        ],
        scratch_shapes=[pltpu.VMEM((n, n), F32), pltpu.VMEM((1, n), F32), pltpu.SemaphoreType.DMA((6,))],
        compiler_params=params(),
        cost_estimate=cost(LONG),
        name="tables",
    )(*(pltpu.with_memory_space_constraint(value, pltpu.HBM) for value in inputs), after)


def x_ends_kernel(n, ny, table_ref, v_ref, halo_ref, w_ref):
    table = Table(n)

    def tile(index, carry):
        start = pl.multiple_of(index * 8, 8)
        rows = pl.ds(start, 8)
        w = [None] * 6
        for k in range(n + 2):
            if k < n:
                fields = six([v_ref[i, k, rows, :] for i in range(3)], 0)
            else:
                fields = six([halo_ref[i, k - n, rows, :] for i in range(3)], 0)
            a = table_ref[table.send + k]
            for f in range(6):
                w[f] = a * fields[f] if k == 0 else w[f] + a * fields[f]
        for f in range(6):
            w_ref[pl.ds(f * ny + start, 8), :] = w[f]
        return carry

    lax.fori_loop(0, ny // 8, tile, 0)
    index = lax.broadcasted_iota(jnp.int32, (8, w_ref.shape[1]), 0)
    w_ref[6 * ny : 6 * ny + 8, :] = jnp.where(index == 0, table_ref[table.oo], table_ref[table.oo1])


def x_ends(table, velocity, halo):
    _, n, ny, nz = velocity.shape
    return pl.pallas_call(
        functools.partial(x_ends_kernel, n, ny),
        in_specs=[WHOLE] * 3,
        out_specs=WHOLE,
        out_shape=layer_shape(6 * ny + 8, nz),
        compiler_params=params(),
        cost_estimate=cost(SHORT),
        name="x_ends",
    )(table, velocity, halo)


def x_face_kernel(n, ny, table_ref, wr_ref, ws_ref, l_ref, own_ref, near_ref, after_ref, w_ref, e_ref):
    ends = Ends(n)
    table = Table(n)
    shape = (8, wr_ref.shape[1])
    p_oo = jnp.broadcast_to(wr_ref[6 * ny : 6 * ny + 1, :], shape)
    p_oo1 = jnp.broadcast_to(wr_ref[6 * ny + 1 : 6 * ny + 2, :], shape)
    x_qo = table_ref[table.qo]
    inverse_den = 1.0 / (1.0 - COUPLING * COUPLING * table_ref[table.oo] * p_oo)
    sent_weight = COUPLING * p_oo
    own_weight = COUPLING * FAR * ends.sign_o * p_oo1
    near_weight = COUPLING * FAR * ends.sign_o * COUPLING * table_ref[table.oo1] * p_oo
    end_weight = ends.sign_o * FAR * table_ref[table.qo1]

    def tile(index, carry):
        start = pl.multiple_of(index * 8, 8)
        rows = pl.ds(start, 8)
        own = six([own_ref[i, rows, :] for i in range(3)], 0)
        near = six([near_ref[i, rows, :] for i in range(3)], 0)
        for f in range(6):
            field = pl.ds(f * ny + start, 8)
            w = wr_ref[field, :] - sent_weight * ws_ref[field, :]
            w = (w + own_weight * own[f] + near_weight * near[f]) * inverse_den
            w_ref[f, rows, :] = 36.0 * w
            e_ref[field, :] = l_ref[f, rows, :] + x_qo * w + end_weight * near[f]
        return carry

    lax.fori_loop(0, ny // 8, tile, 0)
    e_ref[6 * ny : 6 * ny + 8, :] = table_ref[table.qq]


def x_face(table, received, sent, partial, own, near, after, n):
    _, ny, nz = own.shape
    return pl.pallas_call(
        functools.partial(x_face_kernel, n, ny),
        in_specs=[WHOLE] * 6 + [ANY],
        out_specs=[WHOLE, WHOLE],
        out_shape=[layer_shape(6, ny, nz), layer_shape(6 * ny + 8, nz)],
        compiler_params=params(),
        cost_estimate=cost(SHORT),
        name="x_face",
    )(table, received, sent, partial, own, near, after)


def x_sweeps(n, table, table_ref, line, at_first, at_second, at_last_but_one, at_last):
    forward = []
    for k in range(n):
        if k == 0:
            source = 28.0 * line[1] + (line[2] + at_first)
        elif k == 1:
            source = 28.0 * (line[2] - line[0]) + (line[3] + at_second)
        elif k == n - 1:
            source = (at_last - line[n - 3]) - 28.0 * line[n - 2]
        elif k == n - 2:
            source = 28.0 * (line[n - 1] - line[n - 3]) + (at_last_but_one - line[n - 4])
        else:
            source = 28.0 * (line[k + 1] - line[k - 1]) + (line[k + 2] - line[k - 2])
        value = table_ref[table.source + k] * source
        if k > 0:
            value = value - table_ref[table.forward + k] * forward[k - 1]
        forward.append(value)
    solved = [None] * (n - 1) + [forward[n - 1]]
    for k in reversed(range(n - 1)):
        solved[k] = forward[k] - table_ref[table.backward + k] * solved[k + 1]
    return solved


def each_side(run):
    first = lax.axis_index("gy") == 0
    pl.when(first)(functools.partial(run, True))
    pl.when(jnp.logical_not(first))(functools.partial(run, False))


def x_gradient_kernel(n, ny, table_ref, v_ref, near_ref, halo_ref, y_ref, gradient_ref, g_ref, sem):
    table = Table(n)
    y_copy = pltpu.make_async_copy(y_ref, gradient_ref.at[:, 1], sem)
    y_copy.start()

    def run(first):
        sign = -1.0 if first else 1.0
        near_j, far_j = (0, 1) if first else (1, 0)

        def tile(index, carry):
            rows = pl.ds(pl.multiple_of(index * 8, 8), 8)
            for f in range(3):
                line = [v_ref[f, k, rows, :] for k in range(n)]
                inner_near = -sign * halo_ref[f, near_j, rows, :]
                inner = 28.0 * inner_near - sign * halo_ref[f, far_j, rows, :]
                near = sign * near_ref[f, rows, :]
                zero = jnp.zeros_like(near)
                ends = (zero, near, inner_near, inner) if first else (inner, inner_near, near, zero)
                for k, value in enumerate(x_sweeps(n, table, table_ref, line, *ends)):
                    g_ref[f, k, rows, :] = value
            return carry

        lax.fori_loop(0, ny // 8, tile, 0)

    each_side(run)
    y_copy.wait()


def x_gradient_own(table, velocity, near, halo, y_gradient):
    _, n, ny, nz = velocity.shape
    return pl.pallas_call(
        functools.partial(x_gradient_kernel, n, ny),
        in_specs=[WHOLE] * 5,
        out_specs=[ANY, WHOLE],
        out_shape=[layer_shape(3, 3, n, ny, nz), in_vmem(3, n, ny, nz)],
        scratch_shapes=[pltpu.SemaphoreType.DMA],
        compiler_params=params(),
        cost_estimate=cost(SHORT),
        name="x_gradient_own",
    )(table, velocity, near, halo, y_gradient)


def x_solve_kernel(
    n, ny, table_ref, v_ref, near_ref, halo_ref, w_ref, e_ref, r_ref, own_ref, part_ref, lines_ref, side_ref, z_ref, held_ref,
    gradient_ref, convection_ref, g_ref, c_ref, beside_ref, sem,
):
    table = Table(n)
    nz = v_ref.shape[3]
    parts = sem.shape[1]
    share = ny // parts
    z_copy = pltpu.make_async_copy(z_ref, gradient_ref.at[:, 2], sem.at[2, 0])
    z_copy.start()
    p_qq = r_ref[6 * ny : 6 * ny + 8, :]
    weight = COUPLING * p_qq
    scale = -36.0 * COUPLING / (1.0 - COUPLING * COUPLING * table_ref[table.qq] * p_qq)

    def copies(part):
        rows = pl.ds(pl.multiple_of(part * share, 8), share)
        return (
            pltpu.make_async_copy(g_ref.at[:, :, rows], gradient_ref.at[:, 0, :, rows], sem.at[0, part]),
            pltpu.make_async_copy(c_ref.at[:, :, rows], convection_ref.at[:, :, rows], sem.at[1, part]),
        )

    def run(first):
        sign = -1.0 if first else 1.0
        near_j, far_j = (0, 1) if first else (1, 0)

        def step(part, carry):
            base = pl.multiple_of(part * share, 16)
            lines = lines_ref[:, pl.ds(base, share), :].reshape(n * share, lines_ref.shape[2])
            beside_ref[...] = dot(lines, side_ref[:, 3 * nz :])
            def inner_end(f, start):
                field = pl.ds(f * ny + start, 8)
                return scale * (r_ref[field, :] - weight * e_ref[field, :])

            added = []
            for offset in range(0, share, 8):
                rows = pl.ds(base + offset, 8)
                for f in range(3):
                    added.append((f, rows, w_ref[f, rows, :], inner_end(f, base + offset)))
            for k in range(n):
                a, b = table_ref[table.outer + k], table_ref[table.inner + k]
                for f, rows, outer, inner in added:
                    g_ref[f, k, rows, :] = own_ref[f, k, rows, :] + a * outer + b * inner
            for offset in range(0, share, 8):
                start = base + offset
                rows = pl.ds(start, 8)
                near = six([near_ref[i, rows, :] for i in range(3)], 0)
                inner_near = six([halo_ref[i, near_j, rows, :] for i in range(3)], 0)
                inner_far = six([halo_ref[i, far_j, rows, :] for i in range(3)], 0)
                for f in range(3, 6):
                    outer = w_ref[f, rows, :]
                    inner = inner_end(f, start)
                    line = [v_ref[f - 3, k, rows, :] * v_ref[0, k, rows, :] for k in range(n)]
                    inner = inner - sign * (28.0 * inner_near[f] + inner_far[f])
                    ends = (outer, sign * near[f], -sign * inner_near[f], inner)
                    ends = ends if first else ends[::-1]
                    for k, value in enumerate(x_sweeps(n, table, table_ref, line, *ends)):
                        row = k * share + offset
                        beside = beside_ref[row : row + 8, (f - 3) * nz : (f - 2) * nz]
                        c_ref[f - 3, k, rows, :] = value + (part_ref[f - 3, k, rows, :] + beside)
            for copy in copies(part):
                copy.start()
            return carry

        lax.fori_loop(0, parts, step, 0)

    each_side(run)

    def drain(part, carry):
        for copy in copies(part):
            copy.wait()
        return carry

    z_copy.wait()
    lax.fori_loop(0, parts, drain, 0)


def x_solve(table, velocity, near, halo, outer, ends, received, own, partial, lines, side, z_gradient, gradient, share=16):
    _, n, ny, nz = velocity.shape
    return pl.pallas_call(
        functools.partial(x_solve_kernel, n, ny),
        in_specs=[WHOLE] * 12 + [ANY],
        out_specs=[ANY, ANY],
        out_shape=[layer_shape(*gradient.shape), layer_shape(3, n, ny, nz)],
        scratch_shapes=[
            pltpu.VMEM((3, n, ny, nz), F32),
            pltpu.VMEM((3, n, ny, nz), F32),
            pltpu.VMEM((n * share, 3 * nz), F32),
            pltpu.SemaphoreType.DMA((3, ny // share)),
        ],
        input_output_aliases={12: 0},
        compiler_params=params(),
        cost_estimate=cost(SHORT),
        name="x_solve",
    )(table, velocity, near, halo, outer, ends, received, own, partial, lines, side, z_gradient, gradient)


def y_plane(velocities, high_ref, low_ref):
    fields = six(velocities, 1)
    nz = fields[0].shape[1]
    values = []
    for a in (0, 2, 4):
        high, low = split(jnp.concatenate(fields[a : a + 2], axis=1))
        result = dot(high_ref[...], high) + dot(low_ref[...], high) + dot(high_ref[...], low)
        values = values + [result[:, :nz], result[:, nz:]]
    return values


def y_kernel(n, high_ref, low_ref, v_ref, held_ref, part_ref, table_ref, halo_ref, after_ref, g_ref, c_ref, l_ref):
    table = Table(n)
    tiles = v_ref.shape[2] // 8 // (n // GROUP)
    share = tiles // (GROUP - EARLY)

    def inner_end(index):
        rows = pl.ds(pl.multiple_of(index * 8, 8), 8)
        l = [None] * 6
        for k in range(n + 2):
            fields = six([v_ref[i, k, rows, :] if k < n else halo_ref[i, k - n, rows, :] for i in range(3)], 0)
            b = table_ref[table.last + k]
            for f in range(6):
                l[f] = b * fields[f] if k == 0 else l[f] + b * fields[f]
        for f in range(6):
            l_ref[f, rows, :] = l[f]

    def step(group, carry):
        for u in range(EARLY, GROUP):
            p = group * GROUP + u
            values = y_plane([v_ref[i, p] for i in range(3)], high_ref, low_ref)
            for f in range(3):
                g_ref[f, p] = values[f]
                c_ref[f, p] = values[3 + f] + part_ref[f, p]
            for j in range(share):
                inner_end(group * tiles + (u - EARLY) * share + j)
        return carry

    lax.fori_loop(0, n // GROUP, step, 0)


def y_solve(high, low, velocity, early, partial, table, halo, after):
    _, n, ny, nz = velocity.shape
    return pl.pallas_call(
        functools.partial(y_kernel, n),
        in_specs=[WHOLE] * 7 + [ANY],
        out_specs=[WHOLE] * 3,
        out_shape=[in_vmem(3, n, ny, nz), in_vmem(3, n, ny, nz), layer_shape(6, ny, nz)],
        input_output_aliases={3: 0, 4: 1},
        compiler_params=params(),
        cost_estimate=cost(LONG),
        name="y_solve",
    )(high, low, velocity, early, partial, table, halo, after)


LINES = 128
PACK = 4


def z_own_kernel(
    n, y_inv_ref, y_m_ref, inv_ref, m_ref, v_ref, after_ref,
    g_ref, c_ref, y_ref, high_ref, low_ref, right_ref, left_ref, far_ref, main_ref, turned_ref,
):
    nz = inv_ref.shape[0]
    ny = v_ref.shape[2]
    row = lax.broadcasted_iota(jnp.int32, (ny, ny), 0)
    column = lax.broadcasted_iota(jnp.int32, (ny, ny), 1)
    y_metric = jnp.sum(jnp.where(row == column, y_m_ref[...], 0.0), axis=1, keepdims=True)
    high_ref[...], low_ref[...] = split(times_stencil(y_inv_ref[...]) * y_metric)
    high, low = split(times_stencil(inv_ref[...]).T * m_ref[...])
    both = jnp.concatenate([high, low], axis=1)
    main_ref[...] = jnp.concatenate([both, both], axis=0)
    first_scale = 1.0 / m_ref[0:1, 0:1]
    last_scale = 1.0 / m_ref[0:1, nz - 1 : nz]
    lane = lax.broadcasted_iota(jnp.int32, (ny, nz), 1)

    m = nz - 1
    index = lax.broadcasted_iota(jnp.int32, right_ref.shape[1:], 0)
    for ref, corners in ((right_ref, ((m, m), (m, m - 1), (m, 0), (m, 1))), (left_ref, ((0, 0), (0, 1), (0, m), (0, m - 1)))):
        row = jnp.zeros(right_ref.shape[1:], F32)
        for position, (i, j) in enumerate(corners):
            row = jnp.where(index == position, inv_ref[i : i + 1, j : j + 1], row)
        ref[12] = row

    def segments(u):
        start = u * ny
        while start < (u + 1) * ny:
            stop = min((start // LINES + 1) * LINES, (u + 1) * ny)
            yield start // LINES, start - u * ny, stop - u * ny
            start = stop

    def step(group, carry):
        pieces = [[] for _ in range(GROUP * ny // LINES)]
        for u in range(GROUP):
            p = group * GROUP + u
            velocities = [v_ref[i, p] for i in range(3)]
            values = []
            y_values = [None] * 6
            if u < EARLY:
                y_values = y_plane(velocities, high_ref, low_ref)
                for f in range(3):
                    y_ref[f, p] = y_values[f]
            for f, field in enumerate(six(velocities, 2)):
                high, low = split(field)
                both = dot(jnp.concatenate([high, low], axis=1), main_ref[...])
                value = both[:, :nz] + both[:, nz:]
                if f < 3:
                    g_ref[f, p] = value
                else:
                    c_ref[f - 3, p] = value if u >= EARLY else value + y_values[f]
                values.append(value)
            for block, start, stop in segments(u):
                base = block % PACK * 32
                columns = pltpu.roll(values[0][start:stop], base + 1, axis=1)
                for f in range(1, 6):
                    moved = pltpu.roll(values[f][start:stop], (base + 1 + 2 * f) % nz, axis=1)
                    columns = jnp.where(lane[start:stop] // 2 == base // 2 + f, moved, columns)
                for i in range(3):
                    moved = pltpu.roll(velocities[i][start:stop], (base + 14 + 4 * i) % nz, axis=1)
                    columns = jnp.where(lane[start:stop] // 4 == base // 4 + 3 + i, moved, columns)
                pieces[block].append(columns)
        for j, parts in enumerate(pieces):
            if j % PACK == 0:
                packed = jnp.concatenate(parts, axis=0)
                for other in range(1, PACK):
                    columns = jnp.concatenate(pieces[j + other], axis=0)
                    packed = jnp.where(lane[0:LINES] // 32 == other, columns, packed)
                turned_ref[j // PACK, 0:LINES, :] = packed.T
                blocks = pl.ds(group * len(pieces) + j, PACK)

                def rows(position):
                    return turned_ref[j // PACK, pl.ds(position, PACK, stride=32), :]

                for f in range(6):
                    right_ref[f, blocks, :] = rows(2 * f) * last_scale
                    left_ref[f, blocks, :] = rows(2 * f + 1) * first_scale
                for column in range(4):
                    for i in range(3):
                        values = rows(12 + 4 * i + column)
                        ref = right_ref if column < 2 else left_ref
                        ref[6 + 3 * (column % 2) + i, blocks, :] = values
                        far_ref[3 * column + i, blocks, :] = values
        return carry

    lax.fori_loop(0, n // GROUP, step, 0)


def z_own(y_inverse, y_metric, z_inverse, metric, velocity, after):
    _, n, ny, nz = velocity.shape
    return pl.pallas_call(
        functools.partial(z_own_kernel, n),
        in_specs=[WHOLE] * 5 + [ANY],
        out_specs=[WHOLE] * 8,
        out_shape=[in_vmem(3, n, ny, nz)] * 3
        + [pltpu.VMEM((ny, ny), BF16)] * 2
        + [layer_shape(13, n * ny // LINES, LINES)] * 2
        + [layer_shape(12, n * ny // LINES, LINES)],
        scratch_shapes=[
            pltpu.VMEM((2 * nz, 2 * nz), BF16),
            pltpu.VMEM((GROUP * ny // LINES // PACK, LINES + 32, LINES), F32),
        ],
        compiler_params=params(),
        cost_estimate=cost(SHORT),
        name="z_own",
    )(y_inverse, y_metric, z_inverse, metric, velocity, after)


def z_side(own_right, own_left, left, right, left_2, right_2, out_ref):
    blocks = own_left.shape[1]
    shape = own_left.shape[1:]

    def pair(ref, start):
        return six([ref[start + i] for i in range(3)], 2), six([ref[start + 3 + i] for i in range(3)], 2)

    def from_left(ref, start):
        far, near = pair(ref, start)
        return [(-NEAR * near[f] - FAR * far[f], -FAR * near[f]) for f in range(6)]

    def from_right(ref, start):
        near, far = pair(ref, start)
        return [(NEAR * near[f] + FAR * far[f], FAR * near[f]) for f in range(6)]

    def entries(ref):
        return [jnp.broadcast_to(ref[12, i : i + 1], shape) for i in range(4)]

    def first_value(ref, corners, f, at_left, at_right):
        x_00, x_01, x_0m, x_0l = corners
        return ref[f] + x_00 * at_left[f][0] + x_01 * at_left[f][1] + x_0m * at_right[f][0] + x_0l * at_right[f][1]

    def last_value(ref, corners, f, at_left, at_right):
        x_mm, x_ml, x_m0, x_m1 = corners
        return ref[f] + x_m0 * at_left[f][0] + x_m1 * at_left[f][1] + x_mm * at_right[f][0] + x_ml * at_right[f][1]

    own_first_row, own_last_row, left_row, right_row = (entries(ref) for ref in (own_left, own_right, left, right))
    at_left, at_right = from_left(left, 6), from_right(right, 6)
    left_at_left, left_at_right = from_left(left_2, 0), from_right(own_left, 6)
    right_at_left, right_at_right = from_left(own_right, 6), from_right(right_2, 6)
    left_den = 1.0 / (1.0 - COUPLING * COUPLING * left_row[0] * own_first_row[0])
    right_den = 1.0 / (1.0 - COUPLING * COUPLING * right_row[0] * own_last_row[0])
    for f in range(8):
        if f < 6:
            own_first = first_value(own_left, own_first_row, f, at_left, at_right)
            own_last = last_value(own_right, own_last_row, f, at_left, at_right)
            left_value = last_value(left, left_row, f, left_at_left, left_at_right)
            right_value = first_value(right, right_row, f, right_at_left, right_at_right)
            left_final = (left_value - COUPLING * left_row[0] * own_first) * left_den
            right_start = (right_value - COUPLING * right_row[0] * own_last) * right_den
            kinds = (
                at_left[f][0] - COUPLING * left_final,
                at_left[f][1],
                at_right[f][0] - COUPLING * right_start,
                at_right[f][1],
            )
        else:
            kinds = (jnp.zeros(shape, F32),) * 4
        for kind, values in enumerate(kinds):
            start = (8 * kind + f) * blocks
            out_ref[start : start + blocks, :] = values


def z_gradient_kernel(
    n, inv_ref, m_ref, g_ref, own_right_ref, own_left_ref, left_ref, right_ref, left_2_ref, right_2_ref,
    after_ref, out_ref, lines_ref, side_ref, beside_ref,
):
    nz = inv_ref.shape[0]
    ny = g_ref.shape[2]
    columns = inv_ref[...].T * m_ref[...]
    index = lax.broadcasted_iota(jnp.int32, (32, nz), 0)
    kind = index // 8
    picked = jnp.where(
        kind == 0,
        columns[0:1],
        jnp.where(kind == 1, columns[1:2], jnp.where(kind == 2, columns[nz - 1 : nz], columns[nz - 2 : nz - 1])),
    )
    wide = jnp.concatenate([jnp.where(index % 8 == f, picked, 0.0) for f in range(6)], axis=1)
    high, low = split(wide)
    side_ref[...] = jnp.concatenate([high, high, low], axis=0)
    planes = GROUP
    blocks = planes * ny // LINES
    all_blocks = n * ny // LINES
    z_side(own_right_ref, own_left_ref, left_ref, right_ref, left_2_ref, right_2_ref, beside_ref)

    def step(group, carry):
        sides = []
        for j in range(blocks):
            beside = beside_ref[pl.ds(group * blocks + j, 32, stride=all_blocks), :]
            high, low = split(beside.T)
            sides.append(jnp.concatenate([high, low, high], axis=1))
        for pair in range(planes // 2):
            half = blocks // (planes // 2)
            lines = jnp.concatenate(sides[pair * half : (pair + 1) * half], axis=0)
            for u in range(2):
                lines_ref[group * planes + 2 * pair + u] = lines[u * ny : (u + 1) * ny]
            for f in range(0, 3):
                added = dot(lines, side_ref[:, f * nz : (f + 1) * nz])
                for u in range(2):
                    p = group * planes + 2 * pair + u
                    out_ref[f, p] = added[u * ny : (u + 1) * ny] + g_ref[f, p]
        return carry

    lax.fori_loop(0, n // planes, step, 0)


def z_gradient_join(z_inverse, metric, own, lines, after):
    _, n, ny, nz = own.shape
    return pl.pallas_call(
        functools.partial(z_gradient_kernel, n),
        in_specs=[WHOLE] * 9 + [ANY],
        out_specs=[WHOLE, WHOLE, WHOLE],
        out_shape=[
            in_vmem(3, n, ny, nz),
            pltpu.VMEM((n, ny, 96), BF16),
            pltpu.VMEM((96, 6 * nz), BF16),
        ],
        scratch_shapes=[pltpu.VMEM((33 * (n * ny // LINES), LINES), F32)],
        input_output_aliases={2: 0},
        compiler_params=params(),
        cost_estimate=cost(LONG),
        name="z_gradient_join",
    )(z_inverse, metric, own, *lines, after)


def on_device(mesh, velocity, metric_x, metric_y, metric_z, x_inverse, y_inverse, z_inverse):
    n = velocity.shape[1]
    blocks = mesh.shape["gx"] * 2
    across = [(i, (i + 1) % blocks) for i in range(1, blocks, 2)]
    across = across + [(j, i) for i, j in across]
    beside = [(0, 1), (1, 0)]
    count = mesh.shape["gz"]

    def shift(by):
        return [(i, (i + by) % count) for i in range(count)]

    own, inner = prepare(velocity)
    near = lax.ppermute(own, ("gx", "gy"), across)
    halo = lax.ppermute(inner, "gy", beside)
    held = pltpu.with_memory_space_constraint(velocity, pltpu.VMEM)
    table, y_inverse, metric_y, z_inverse, metric_z = tables(
        x_inverse, metric_x[None], y_inverse, metric_y[None], z_inverse, metric_z[None], own
    )

    x_sent = x_ends(table, held, halo)
    x_received = lax.ppermute(x_sent, ("gx", "gy"), across)

    z_gradient, convection, y_gradient, y_high, y_low, to_right, to_left, to_far = z_own(
        y_inverse, metric_y, z_inverse, metric_z, held, x_sent
    )
    left_far = lax.ppermute(to_far, "gz", shift(2))
    right_far = left_far if shift(2) == shift(-2) else lax.ppermute(to_far, "gz", shift(-2))
    z_lines = (
        to_right,
        to_left,
        lax.ppermute(to_right, "gz", shift(1)),
        lax.ppermute(to_left, "gz", shift(-1)),
        left_far,
        right_far,
    )

    y_gradient, convection, x_partial = y_solve(
        y_high, y_low, held, y_gradient, convection, table, halo, near
    )
    gradient, x_gradient = x_gradient_own(table, held, near, halo, y_gradient)
    outer, x_end = x_face(table, x_received, x_sent, x_partial, own, near, x_gradient, n)
    x_other = lax.ppermute(x_end, "gy", beside)
    z_gradient, lines, side = z_gradient_join(z_inverse, metric_z, z_gradient, z_lines, x_end)
    return tuple(
        x_solve(
            table, held, near, halo, outer, x_end, x_other, x_gradient, convection, lines, side, z_gradient, gradient
        )
    )


def solution(mesh):
    return jax.shard_map(
        functools.partial(on_device, mesh),
        mesh=mesh,
        in_specs=(
            P(None, ("gx", "gy"), None, "gz"),
            P(("gx", "gy")),
            P(),
            P("gz"),
            P(("gx", "gy"), None),
            P(),
            P("gz", None),
        ),
        out_specs=(P(None, None, ("gx", "gy"), None, "gz"), P(None, ("gx", "gy"), None, "gz")),
        check_vma=False,
    )
```
